256 devices in a mesh: dof: 32 (over z, x), dir: 8 (over y, core).
Axes of the slice: x: 4, y: 4, z: 8, core: 2. Of those that a mesh axis runs over, the one named last changes fastest.
Arguments:
- start_disp: float32 [4, 256, 32768], P(None, 'dir', 'dof')
- start_vel: float32 [4, 256, 32768], P(None, 'dir', 'dof')
- elem_stiff: float32 [8, 8, 32768], P(None, None, 'dof'), may hold values from -1.5 to 1.5
- link_stiff: float32 [4, 4, 32768], P(None, None, 'dof'), may hold values from -1.5 to 1.5
- block_inv: float32 [4, 4, 32768], P(None, None, 'dof'), may hold values from -0.3 to 1.4
- link_offset: int32 [32768], P('dof'), may hold values from -8 to 8
- damper_nodes: int32 [64], P('dof'), may hold values from 0 to 32767, as said below
- damper_stiff: float32 [2, 2, 64], P(None, None, 'dof'), may hold values from -4 to 4
- damper_damp: float32 [2, 2, 64], P(None, None, 'dof'), may hold values from -4 to 4
Outputs:
- end_velocity: float32 [4, 256, 32768], P(None, 'dir', 'dof')
- q_block: float32 [4, 256, 32768], P(None, None, ('dof', 'dir'))
- r_factor: float32 [256, 256], replicated
The draws below stay inside these ranges and needn't reach their ends.
Inputs may be any that keep to these rules, and one draw needn't show every extreme that they name: `damper_nodes`: the ids rise; the k-th aligned block of 2 ids names nodes of k * 1024 to (k + 1) * 1024 - 1, its j-th id lying in j * 512 to (j + 1) * 512 - 1 of that range; nodes 0 and 32767 carry dampers.
All inputs are finite; a program needn't handle non-finite values.
Results may differ from the reference program's by a relative error of at most 0.0002.
Values sent between devices are 32-bit elements; how exact they have to be, the bound alone decides.
A program may use at most 128 MiB of HBM per device.

```python
import jax
import jax.numpy as jnp
from jax import lax

NODE_DEV = 1024
DIR_DEV = 32
HALO = 8
DAMP_DEV = 2
NODES = 32768
DIRS = 256
NDAMP = 64


def scale_state(key, noise):
    key_rows = jax.random.fold_in(key, 1)
    key_cols = jax.random.fold_in(key, 2)
    ramp = 1.0 + 2.0 * jnp.arange(NODES, dtype=jnp.float32) / NODES
    row_scale = ramp * jnp.exp(jax.random.uniform(key_rows, (NODES,), jnp.float32, 0.0, 1.25))
    col_scale = jnp.exp(jax.random.uniform(key_cols, (DIRS,), jnp.float32, 0.0, 2.3))
    return 0.1 * noise * row_scale[None, None, :] * col_scale[None, :, None]


def draw_start_disp(key, part):
    key = jax.random.fold_in(key, 11)
    key_noise = jax.random.fold_in(key, 3)
    noise = jax.random.normal(key_noise, (4, DIRS, NODES), jnp.float32)
    return scale_state(key, noise)


def draw_start_vel(key, part):
    key = jax.random.fold_in(key, 13)
    key_noise = jax.random.fold_in(key, 3)
    noise = jax.random.normal(key_noise, (4, DIRS, NODES), jnp.float32)
    return scale_state(key, noise)


def draw_block_inv(key, part):
    key = jax.random.fold_in(key, 23)
    key_diag = jax.random.fold_in(key, 1)
    key_off = jax.random.fold_in(key, 2)
    diagonal = jax.random.uniform(key_diag, (4, NODES), jnp.float32, 0.6, 1.4)
    offdiag = jax.random.uniform(key_off, (4, 4, NODES), jnp.float32, -0.3, 0.3)
    identity = jnp.eye(4, dtype=jnp.float32)[:, :, None]
    return identity * diagonal[:, None, :] + (1.0 - identity) * offdiag


def draw_link_offset(key, part):
    key = jax.random.fold_in(key, 37)
    key_main = jax.random.fold_in(key, 1)
    key_upper = jax.random.fold_in(key, 2)
    key_lower = jax.random.fold_in(key, 3)
    offsets = jax.random.randint(key_main, (NODES,), -HALO, HALO + 1, dtype=jnp.int32)
    far_upper = jax.random.randint(key_upper, (), 0, NODES, dtype=jnp.int32)
    far_lower = (far_upper + 1 + jax.random.randint(key_lower, (), 0, NODES - 1, dtype=jnp.int32)) % NODES
    positions = jnp.arange(NODES, dtype=jnp.int32)
    offsets = jnp.where(positions == far_upper, HALO, offsets)
    offsets = jnp.where(positions == far_lower, -HALO, offsets)
    return offsets.astype(jnp.int32)


def draw_damper_nodes(key, part):
    key = jax.random.fold_in(key, 41)
    stride = NODE_DEV // DAMP_DEV
    within = jax.random.randint(key, (NDAMP,), 0, stride, dtype=jnp.int32)
    positions = jnp.arange(NDAMP, dtype=jnp.int32)
    within = jnp.where(positions == 0, 0, within)
    within = jnp.where(positions == NDAMP - 1, stride - 1, within)
    return (positions * stride + within).astype(jnp.int32)


def levels(stream_key, shape, shards, smallest, high):
    factor_of, own = 1.0, jax.random.fold_in(stream_key, 6)
    for axis_at, shards_of in shards:
        heights = jnp.exp(jax.random.uniform(jax.random.fold_in(own, axis_at), (shards_of,), jnp.float32, smallest / len(shards), high / len(shards)))
        factor_of = factor_of * jnp.repeat(heights, shape[axis_at] // shards_of).reshape([-1 if axis == axis_at else 1 for axis in range(len(shape))])
    return factor_of


def bell_draw(key, extent, width, limit, cuts=(), kind=jnp.bfloat16):
    entries = jax.random.normal(key, extent, jnp.float32) * width
    if len(cuts) > 0:
        entries = levels(key, extent, cuts, -0.22, 0.18) * entries
    return jnp.clip(entries, min=-limit, max=limit).astype(kind)


def setup_inputs(seed: int = 0) -> dict:
    key_of = jax.random.split(jax.random.key(seed), 10)
    return {
        "start_disp": draw_start_disp(jax.random.fold_in(key_of[9], 71), 0),
        "start_vel": draw_start_vel(jax.random.fold_in(key_of[9], 71), 0),
        "elem_stiff": bell_draw(key_of[2], (8, 8, NODES), 0.3, 1.5, ((2, 32),), jnp.float32),
        "link_stiff": bell_draw(key_of[3], (4, 4, NODES), 0.3, 1.5, ((2, 32),), jnp.float32),
        "block_inv": draw_block_inv(jax.random.fold_in(key_of[9], 71), 0),
        "link_offset": draw_link_offset(jax.random.fold_in(key_of[9], 71), 0),
        "damper_nodes": draw_damper_nodes(jax.random.fold_in(key_of[9], 71), 0),
        "damper_stiff": bell_draw(key_of[7], (2, 2, NDAMP), 1.0, 4.0, ((2, 32),), jnp.float32),
        "damper_damp": bell_draw(key_of[8], (2, 2, NDAMP), 1.0, 4.0, ((2, 32),), jnp.float32),
    }


time_step = 0.5

def apply_block(block, field):
    summed = block[:, 0, None, :] * field[0][None]
    for column in range(1, block.shape[1]):
        summed = summed + block[:, column, None, :] * field[column][None]
    return summed

def forces(disp, veloc, elem_stiff, link_stiff, block_inv, link_offset, damper_nodes, damper_stiff, damper_damp):
    node_count = disp.shape[2]
    padded = jnp.pad(disp, ((0, 0), (0, 0), (HALO, HALO)))
    ahead_disp = padded[:, :, HALO + 1:HALO + 1 + node_count]
    stacked = jnp.concatenate([disp, ahead_disp], axis=0)
    own_part = apply_block(elem_stiff[0:4], stacked)
    next_part = apply_block(elem_stiff[4:8], stacked)
    behind = jnp.pad(next_part[:, :, :node_count - 1], ((0, 0), (0, 0), (1, 0)))
    partner = (HALO + jnp.arange(node_count, dtype=jnp.int32) + link_offset).astype(jnp.int32)
    linked = jnp.take(padded, partner, axis=2)
    summed = own_part + behind + apply_block(link_stiff, linked)
    lateral_disp = disp[0:2][:, :, damper_nodes]
    lateral_vel = veloc[0:2][:, :, damper_nodes]
    film_force = apply_block(damper_stiff, lateral_disp) + apply_block(damper_damp, lateral_vel)
    summed = summed.at[0:2, :, damper_nodes].add(film_force)
    return apply_block(block_inv, -summed)

def reference(start_disp, start_vel, elem_stiff, link_stiff, block_inv, link_offset, damper_nodes, damper_stiff, damper_damp):
    group_count = DIRS // DIR_DEV

    def propagate(states):
        disp, veloc = states
        accel = forces(disp, veloc, elem_stiff, link_stiff, block_inv, link_offset, damper_nodes, damper_stiff, damper_damp)
        for repeat in range(2):
            disp = disp + time_step * veloc + 0.5 * time_step * time_step * accel
            middle = veloc + 0.5 * time_step * accel
            accel = forces(disp, middle, elem_stiff, link_stiff, block_inv, link_offset, damper_nodes, damper_stiff, damper_damp)
            veloc = middle + 0.5 * time_step * accel
        return (disp, veloc)
    disp_groups = jnp.moveaxis(start_disp.reshape(4, group_count, DIR_DEV, NODES), 1, 0)
    vel_groups = jnp.moveaxis(start_vel.reshape(4, group_count, DIR_DEV, NODES), 1, 0)
    end_groups, vel_out = lax.map(propagate, (disp_groups, vel_groups))
    end_disp = jnp.moveaxis(end_groups, 0, 1).reshape(4, DIRS, NODES)
    end_velocity = jnp.moveaxis(vel_out, 0, 1).reshape(4, DIRS, NODES)
    gram_matrix = jnp.einsum('cdn,cen->de', end_disp, end_disp, precision=lax.Precision.HIGHEST)
    gram_matrix = gram_matrix / (4.0 * NODES)
    lower_factor = jnp.linalg.cholesky(gram_matrix)
    q_parts = []
    for component in range(4):
        q_parts.append(lax.linalg.triangular_solve(lower_factor, end_disp[component], left_side=True, lower=True))
    q_block = jnp.stack(q_parts, axis=0)
    return (end_velocity, q_block, jnp.transpose(lower_factor))
```

```python
import functools

import jax
import jax.numpy as jnp
from jax import lax
from jax.experimental import pallas as pl
from jax.experimental.pallas import tpu as pltpu
from jax.sharding import PartitionSpec as P

STEP = 0.5
LANES = 128
SUB = 8
REACH = 32
MESH = pl.DeviceIdType.MESH
HIGHEST = lax.Precision.HIGHEST


def iota(shape, axis):
    return lax.broadcasted_iota(jnp.int32, shape, axis)


def rolled(x, by, axis):
    by = by % x.shape[axis]
    return pltpu.roll(x, by, axis) if by else x


def lane_gather(x, index):
    return jnp.take_along_axis(x, index, axis=1, mode="promise_in_bounds")


def newmark_kernel(
    ndof,
    ndir,
    disp_in,
    vel_in,
    elem_in,
    link_in,
    inv_in,
    offset_in,
    damper_at,
    damper_k,
    damper_c,
    vel_out,
    x_out,
    gram_out,
    disp_a,
    disp_b,
    vel,
    coef,
    link_raw,
    inv_raw,
    offset_raw,
    pm,
    qm,
    vm,
    to_send,
    arrived,
    x_all,
    gram_part,
    dir_slots,
    dir_sum,
    dof_slots,
    gram,
    load_sem,
    halo_send,
    halo_recv,
    a2a_send,
    a2a_recv,
    rs_send,
    rs_recv,
    ds_send,
    ds_recv,
    dg_send,
    dg_recv,
    ag_send,
    ag_recv,
    store_sem,
):
    me_p = lax.axis_index("dof")
    me_t = lax.axis_index("dir")
    dirs = disp_in.shape[1]
    nodes = disp_in.shape[2]
    tiles = nodes // LANES
    around = tiles + 1
    per_dof = dirs // ndof

    loads = [
        (disp_in, disp_a.at[:, :, 0:nodes]),
        (vel_in, vel.at[:, :, 0:nodes]),
        (elem_in, coef.at[0:8, :, 0:nodes]),
        (link_in, link_raw),
        (inv_in, inv_raw),
        (offset_in, offset_raw),
    ]
    loads = [pltpu.make_async_copy(s, d, load_sem.at[i]) for i, (s, d) in enumerate(loads)]
    for copy in loads:
        copy.start()

    barrier = pltpu.get_barrier_semaphore()

    def greet_dof(k, carry):
        peer = lax.rem(me_p + k, ndof)
        pl.semaphore_signal(barrier, inc=1, device_id=(peer, me_t), device_id_type=MESH)
        return carry

    def greet_dir(k, carry):
        peer = lax.rem(me_t + k, ndir)
        pl.semaphore_signal(barrier, inc=1, device_id=(me_p, peer), device_id_type=MESH)
        return carry

    lax.fori_loop(1, ndof, greet_dof, 0)
    lax.fori_loop(1, ndir, greet_dir, 0)

    lane = iota((SUB, LANES), 1)
    sub = iota((SUB, LANES), 0)

    def at_tile(t):
        return pl.ds(pl.multiple_of(t * LANES, LANES), LANES)

    columns = []
    for q in range(2):
        column = jnp.zeros((SUB, LANES), jnp.float32)
        for kind, table in enumerate((damper_k, damper_c)):
            for i in range(2):
                for j in range(2):
                    column = jnp.where(sub == 4 * kind + 2 * i + j, table[i, j, q], column)
        columns.append(column)
    for copy in loads[2:]:
        copy.wait()
    for t in range(tiles):
        where = slice(t * LANES, (t + 1) * LANES)
        dense = jnp.zeros((SUB, LANES), jnp.float32)
        for q in range(2):
            place = damper_at[q] - me_p * nodes - t * LANES
            dense = dense + jnp.where(lane == place, columns[q], 0.0)
        coef[12, :, where] = dense
        row = offset_raw[t : t + 1, :].astype(jnp.float32)
        coef[13, :, where] = jnp.broadcast_to(row, (SUB, LANES))
    for half in range(2):
        coef[8 + half, 0:4, 0:nodes] = link_raw[2 * half]
        coef[8 + half, 4:8, 0:nodes] = link_raw[2 * half + 1]
        coef[10 + half, 0:4, 0:nodes] = inv_raw[2 * half]
        coef[10 + half, 4:8, 0:nodes] = inv_raw[2 * half + 1]
    for copy in loads[:2]:
        copy.wait()

    groups = dirs // SUB
    packs = []
    for ref in (disp_a, vel):
        for g in range(groups):
            packs.append([(ref, c, slice(g * SUB, (g + 1) * SUB)) for c in range(4)])
    for g in range(0, 14, 4):
        packs.append([(coef, k, slice(0, SUB)) for k in range(g, min(g + 4, 14))])
    for side, start, first in ((0, nodes - LANES, LANES - REACH), (1, 0, 0)):
        for n, pack in enumerate(packs):
            held = None
            for s, (ref, c, rows) in enumerate(pack):
                piece = rolled(ref[c, rows, start : start + LANES], REACH * s - first, 1)
                held = piece if held is None else jnp.where(lane >= REACH * s, piece, held)
            to_send[side, n] = held

    pl.semaphore_wait(barrier, ndof - 1 + ndir - 1)
    halo = []
    for side, by in ((0, 1), (1, ndof - 1)):
        halo.append(
            pltpu.make_async_remote_copy(
                src_ref=to_send.at[side],
                dst_ref=arrived.at[side],
                send_sem=halo_send.at[side],
                recv_sem=halo_recv.at[side],
                device_id=(lax.rem(me_p + by, ndof), me_t),
                device_id_type=MESH,
            )
        )
        halo[-1].start()

    def prepare(t):
        now = at_tile(t)
        before = at_tile(lax.rem(t + around - 1, around))
        p_rows, q_rows = [], []
        for i in range(4):
            shifted = jnp.where(
                lane == 0,
                rolled(coef[4 + i, :, before], 1, 1),
                rolled(coef[4 + i, :, now], 1, 1),
            )
            link = coef[8 + i // 2, :, now]
            if i % 2 == 0:
                link = rolled(link, 4, 0)
            q_rows.append(jnp.where(sub < 4, shifted, link))
            p_rows.append(coef[i, :, now] + jnp.where(sub < 4, rolled(shifted, 4, 0), 0.0))
        film = coef[12, :, now]
        for k in range(2):
            p_rows[k] = p_rows[k] + jnp.where(sub < 2, rolled(film, -2 * k, 0), 0.0)
        v_rows = [rolled(film, -4 - 2 * k, 0) for k in range(2)]
        for i in range(4):
            inv = [
                -coef[10 + i // 2, 4 * (i % 2) + k : 4 * (i % 2) + k + 1, now] for k in range(4)
            ]
            for out, rows in ((pm, p_rows), (qm, q_rows), (vm, v_rows)):
                total = inv[0] * rows[0]
                for k in range(1, len(rows)):
                    total = total + inv[k] * rows[k]
                out[i, :, now] = total

    chunk = min(16, dirs)

    def evaluate(disp, t, finish):
        now = at_tile(t)
        before = at_tile(lax.rem(t + around - 1, around))
        after = at_tile(lax.rem(t + 1, around))
        wide_lane = iota((chunk, LANES), 1)
        target = coef[13, 0:1, now].astype(jnp.int32) + lane[0:1, :]
        inside = jnp.broadcast_to((target >= 0) & (target < LANES), (chunk, LANES))
        index = jnp.broadcast_to(target & (LANES - 1), (chunk, LANES))
        for r in range(0, dirs, chunk):
            rows = slice(r, r + chunk)
            speed = [vel[j, rows, now] for j in range(2)]
            acc = [None] * 4
            for j in range(4):
                here = disp[j, rows, now]
                left = disp[j, rows, before]
                right = disp[j, rows, after]
                previous = jnp.where(wide_lane == 0, rolled(left, 1, 1), rolled(here, 1, 1))
                following = jnp.where(
                    wide_lane == LANES - 1, rolled(right, -1, 1), rolled(here, -1, 1)
                )
                other = jnp.where(wide_lane < LANES // 2, right, left)
                linked = jnp.where(inside, lane_gather(here, index), lane_gather(other, index))
                for i in range(4):
                    total = pm[i, j : j + 1, now] * here
                    total = total + pm[i, 4 + j : 5 + j, now] * following
                    total = total + qm[i, j : j + 1, now] * previous
                    total = total + qm[i, 4 + j : 5 + j, now] * linked
                    if j < 2:
                        total = total + vm[i, j : j + 1, now] * speed[j]
                    acc[i] = total if acc[i] is None else acc[i] + total
            finish(rows, now, acc)

    def finish_first(rows, now, acc):
        for i in range(4):
            v = vel[i, rows, now]
            disp_b[i, rows, now] = (
                disp_a[i, rows, now] + STEP * v + (0.5 * STEP * STEP) * acc[i]
            )
            vel[i, rows, now] = v + (0.5 * STEP) * acc[i]

    def finish_second(rows, now, acc):
        for i in range(4):
            v = vel[i, rows, now] + (0.5 * STEP) * acc[i]
            disp_a[i, rows, now] = (
                disp_b[i, rows, now] + STEP * v + (0.5 * STEP * STEP) * acc[i]
            )
            vel[i, rows, now] = v + (0.5 * STEP) * acc[i]

    def finish_last(rows, now, acc):
        for i in range(4):
            vel[i, rows, now] = vel[i, rows, now] + (0.5 * STEP) * acc[i]

    def prepare_tile(t, carry):
        prepare(t)
        return carry

    def first_tile(t, carry):
        evaluate(disp_a, t, finish_first)
        return carry

    lax.fori_loop(1, tiles, prepare_tile, 0)
    lax.fori_loop(1, tiles - 1, first_tile, 0)

    for copy in halo:
        copy.wait_recv()
    right_end = jnp.where(me_p < ndof - 1, REACH, 0)
    left_start = jnp.where(me_p > 0, LANES - REACH, LANES)
    for n, pack in enumerate(packs):
        from_left, from_right = arrived[0, n], arrived[1, n]
        for s, (ref, c, rows) in enumerate(pack):
            piece = jnp.where(lane < right_end, rolled(from_right, -REACH * s, 1), 0.0)
            ref[c, rows, nodes : nodes + LANES] = jnp.where(
                lane >= left_start, rolled(from_left, LANES - REACH - REACH * s, 1), piece
            )

    def wrapped(k):
        return lax.rem(k, around)

    lax.fori_loop(tiles, tiles + 2, lambda k, c: prepare_tile(wrapped(k), c), 0)
    lax.fori_loop(tiles - 1, tiles + 2, lambda k, c: first_tile(wrapped(k), c), 0)

    def tile_copy(peer):
        return pltpu.make_async_remote_copy(
            src_ref=disp_a.at[:, :, at_tile(peer)],
            dst_ref=x_all.at[:, pl.ds(pl.multiple_of(me_t * dirs, dirs), dirs), :],
            send_sem=a2a_send.at[peer],
            recv_sem=a2a_recv.at[me_t],
            device_id=(me_p, peer),
            device_id_type=MESH,
        )

    def second_tile(by, carry):
        t = lax.rem(me_t + by, ndir)
        evaluate(disp_b, t, finish_second)
        tile_copy(t).start()
        return carry

    half = ndir // 2
    lax.fori_loop(half, ndir, second_tile, 0)
    lax.fori_loop(1, half, lambda k, c: second_tile(half - k, c), 0)
    evaluate(disp_b, me_t, finish_second)
    x_all[:, pl.ds(pl.multiple_of(me_t * dirs, dirs), dirs), :] = disp_a[:, :, at_tile(me_t)]
    evaluate(disp_b, tiles, finish_second)

    def last_tile(t, carry):
        evaluate(disp_a, t, finish_last)
        return carry

    lax.fori_loop(0, tiles, last_tile, 0)
    vel_store = pltpu.make_async_copy(vel.at[:, :, 0:nodes], vel_out, store_sem.at[0])
    vel_store.start()

    def tile_arrival(by):
        source = lax.rem(me_t + by, ndir)
        return pltpu.make_async_remote_copy(
            src_ref=disp_a.at[:, :, at_tile(source)],
            dst_ref=x_all.at[:, pl.ds(pl.multiple_of(source * dirs, dirs), dirs), :],
            send_sem=a2a_send.at[source],
            recv_sem=a2a_recv.at[source],
            device_id=(me_p, source),
            device_id_type=MESH,
        )

    for by in range(1, ndir):
        tile_arrival(by).wait_recv()
    x_store = pltpu.make_async_copy(x_all, x_out, store_sem.at[1])
    x_store.start()

    total = None
    for c in range(4):
        product = lax.dot_general(
            x_all[c],
            x_all[c],
            (((1,), (1,)), ((), ())),
            precision=HIGHEST,
            preferred_element_type=jnp.float32,
        )
        total = product if total is None else total + product
    gram_part[...] = total

    def part_copy(by, source):
        peer = lax.rem(me_t + by, ndir)
        return pltpu.make_async_remote_copy(
            src_ref=gram_part.at[pl.ds(pl.multiple_of(peer * dirs, dirs), dirs), :],
            dst_ref=dir_slots.at[source],
            send_sem=rs_send.at[by],
            recv_sem=rs_recv.at[source],
            device_id=(me_p, peer),
            device_id_type=MESH,
        )

    for by in range(1, ndir):
        part_copy(by, me_t).start()
    dir_slots[me_t] = gram_part[pl.ds(pl.multiple_of(me_t * dirs, dirs), dirs), :]
    for by in range(1, ndir):
        part_copy(by, lax.rem(me_t + by, ndir)).wait_recv()
    total = dir_slots[0]
    for k in range(1, ndir):
        total = total + dir_slots[k]
    dir_sum[...] = total

    def row_copy(by, source):
        peer = lax.rem(me_p + by, ndof)
        return pltpu.make_async_remote_copy(
            src_ref=dir_sum.at[pl.ds(peer * per_dof, per_dof), :],
            dst_ref=dof_slots.at[pl.ds(source * per_dof, per_dof), :],
            send_sem=ds_send.at[by],
            recv_sem=ds_recv.at[source],
            device_id=(peer, me_t),
            device_id_type=MESH,
        )

    def start_row(by, carry):
        row_copy(by, me_p).start()
        return carry

    def await_row(by, carry):
        row_copy(by, lax.rem(me_p + by, ndof)).wait_recv()
        return carry

    lax.fori_loop(1, ndof, start_row, 0)
    dof_slots[pl.ds(me_p * per_dof, per_dof), :] = dir_sum[pl.ds(me_p * per_dof, per_dof), :]
    lax.fori_loop(1, ndof, await_row, 0)
    if per_dof == 1:
        total = jnp.sum(dof_slots[...], axis=0, keepdims=True)
    else:
        total = dof_slots[0:per_dof, :]
        for k in range(1, ndof):
            total = total + dof_slots[k * per_dof : (k + 1) * per_dof, :]
    gram[pl.ds(me_t * dirs + me_p * per_dof, per_dof), :] = total

    def sum_copy(by, source):
        peer = lax.rem(me_p + by, ndof)
        own = pl.ds(me_t * dirs + source * per_dof, per_dof)
        return pltpu.make_async_remote_copy(
            src_ref=gram.at[own, :],
            dst_ref=gram.at[own, :],
            send_sem=dg_send.at[by],
            recv_sem=dg_recv.at[source],
            device_id=(peer, me_t),
            device_id_type=MESH,
        )

    def start_sum(by, carry):
        sum_copy(by, me_p).start()
        return carry

    def await_sum(by, carry):
        sum_copy(by, lax.rem(me_p + by, ndof)).wait_recv()
        return carry

    lax.fori_loop(1, ndof, start_sum, 0)
    lax.fori_loop(1, ndof, await_sum, 0)

    def block_copy(by, source):
        peer = lax.rem(me_t + by, ndir)
        own = pl.ds(pl.multiple_of(source * dirs, dirs), dirs)
        return pltpu.make_async_remote_copy(
            src_ref=gram.at[own, :],
            dst_ref=gram.at[own, :],
            send_sem=ag_send.at[by],
            recv_sem=ag_recv.at[source],
            device_id=(me_p, peer),
            device_id_type=MESH,
        )

    for by in range(1, ndir):
        block_copy(by, me_t).start()
    for by in range(1, ndir):
        block_copy(by, lax.rem(me_t + by, ndir)).wait_recv()
    gram_store = pltpu.make_async_copy(gram, gram_out, store_sem.at[2])
    gram_store.start()

    for copy in halo:
        copy.wait_send()
    for by in range(1, ndir):
        tile_copy(lax.rem(me_t + by, ndir)).wait_send()
        part_copy(by, me_t).wait_send()
        block_copy(by, me_t).wait_send()

    def sent_rows(by, carry):
        row_copy(by, me_p).wait_send()
        sum_copy(by, me_p).wait_send()
        return carry

    lax.fori_loop(1, ndof, sent_rows, 0)
    vel_store.wait()
    x_store.wait()
    gram_store.wait()


def newmark(ndof, ndir, *args):
    dirs, nodes = args[0].shape[1:]
    around = nodes + LANES
    n = dirs * ndir
    packs = 2 * (dirs // SUB) + 4
    f32 = jnp.float32
    hbm = pl.BlockSpec(memory_space=pl.ANY)
    smem = pl.BlockSpec(memory_space=pltpu.SMEM)
    dma = pltpu.SemaphoreType.DMA
    return pl.pallas_call(
        functools.partial(newmark_kernel, ndof, ndir),
        out_shape=(
            jax.ShapeDtypeStruct((4, dirs, nodes), f32),
            jax.ShapeDtypeStruct((4, n, LANES), f32),
            jax.ShapeDtypeStruct((n, n), f32),
        ),
        in_specs=[hbm] * 6 + [smem] * 3,
        out_specs=[hbm] * 3,
        scratch_shapes=[
            pltpu.VMEM((4, dirs, around), f32),
            pltpu.VMEM((4, dirs, around), f32),
            pltpu.VMEM((4, dirs, around), f32),
            pltpu.VMEM((14, SUB, around), f32),
            pltpu.VMEM((4, 4, nodes), f32),
            pltpu.VMEM((4, 4, nodes), f32),
            pltpu.VMEM((nodes // LANES, LANES), jnp.int32),
            pltpu.VMEM((4, SUB, around), f32),
            pltpu.VMEM((4, SUB, around), f32),
            pltpu.VMEM((4, SUB, around), f32),
            pltpu.VMEM((2, packs, SUB, LANES), f32),
            pltpu.VMEM((2, packs, SUB, LANES), f32),
            pltpu.VMEM((4, n, LANES), f32),
            pltpu.VMEM((n, n), f32),
            pltpu.VMEM((ndir, dirs, n), f32),
            pltpu.VMEM((dirs, n), f32),
            pltpu.VMEM((dirs, n), f32),
            pltpu.VMEM((n, n), f32),
            dma((6,)),
            dma((2,)),
            dma((2,)),
            dma((ndir,)),
            dma((ndir,)),
            dma((ndir,)),
            dma((ndir,)),
            dma((ndof,)),
            dma((ndof,)),
            dma((ndof,)),
            dma((ndof,)),
            dma((ndir,)),
            dma((ndir,)),
            dma((3,)),
        ],
        compiler_params=pltpu.CompilerParams(
            collective_id=0, has_side_effects=True, vmem_limit_bytes=48 * 2**20
        ),
        name="newmark_and_gram",
    )(*args)


def spread(x, lane):
    return jnp.broadcast_to(x[:, lane : lane + 1], (x.shape[0], LANES))


def tiled(x, width):
    return x if width == LANES else jnp.concatenate([x] * (width // LANES), axis=1)


def eliminate(block, micro):
    size, width = block.shape
    row = iota((micro, LANES), 0)
    done = []
    for s in range(0, size, micro):
        top = block[0:micro]
        rest = [block[i : i + SUB] for i in range(micro, size - s, SUB)]
        column = [spread(top, s + j) for j in range(micro)]
        inverse = []
        pivots = jnp.broadcast_to(column[0][0:1], (micro, LANES))
        for j in range(micro):
            pivot = column[j][j : j + 1]
            inverse.append(1.0 / pivot)
            pivots = jnp.where(row == j, pivot, pivots)
            if j == micro - 1:
                break
            factor = jnp.where(row > j, column[j] * inverse[j], 0.0)
            for m in range(j + 1, micro):
                column[m] = column[m] - factor * column[m][j : j + 1]
            top = top - tiled(factor, width) * top[j : j + 1]
        below = []
        for part in rest:
            own = [spread(part, s + j) for j in range(micro)]
            for j in range(micro):
                factor = own[j] * inverse[j]
                for m in range(j + 1, micro):
                    own[m] = own[m] - factor * column[m][j : j + 1]
                part = part - tiled(factor, width) * top[j : j + 1]
            below.append(part)
        done.append(top * tiled(lax.rsqrt(pivots), width))
        if below:
            block = jnp.concatenate(below, axis=0) if len(below) > 1 else below[0]
    return jnp.concatenate(done, axis=0)


def factor_kernel(scale, size, micro, gram, x, q_out, r_out, work):
    n = gram.shape[0]
    row, col = iota((size, size), 0), iota((size, size), 1)
    identity = (row == col).astype(jnp.float32)
    work[:, 0:n] = gram[...] * scale
    for c in range(4):
        work[:, n + LANES * c : n + LANES * (c + 1)] = x[c]
    for low in range(0, n, size):
        high = low + size
        block = jnp.concatenate([work[low:high, low:high], identity], axis=1)
        block = eliminate(block, micro)
        later = jnp.dot(
            block[:, size:],
            work[low:high, high:],
            precision=HIGHEST,
            preferred_element_type=jnp.float32,
        )
        if low > 0:
            r_out[low:high, 0:low] = jnp.zeros((size, low), jnp.float32)
        r_out[low:high, low:high] = jnp.where(row <= col, block[:, 0:size], 0.0)
        if high < n:
            r_out[low:high, high:n] = later[:, 0 : n - high]
            work[high:, high:] = work[high:, high:] - lax.dot_general(
                later[:, 0 : n - high],
                later,
                (((0,), (0,)), ((), ())),
                precision=HIGHEST,
                preferred_element_type=jnp.float32,
            )
        for c in range(4):
            start = n - high + LANES * c
            q_out[c, low:high, :] = later[:, start : start + LANES]


def factor(gram, x, scale):
    n = gram.shape[0]
    vmem = pl.BlockSpec(memory_space=pltpu.VMEM)
    return pl.pallas_call(
        functools.partial(factor_kernel, scale, n // 2, SUB),
        out_shape=(
            jax.ShapeDtypeStruct(x.shape, jnp.float32),
            jax.ShapeDtypeStruct((n, n), jnp.float32),
        ),
        in_specs=[vmem, vmem],
        out_specs=[vmem, vmem],
        scratch_shapes=[pltpu.VMEM((n, n + 4 * LANES), jnp.float32)],
        compiler_params=pltpu.CompilerParams(vmem_limit_bytes=32 * 2**20),
        name="factor_and_solve",
    )(gram, x)


def on_device(ndof, ndir, disp, veloc, elem, link, inv, offset, damper_at, damper_k, damper_c):
    nodes = disp.shape[2]
    offset = offset.reshape(nodes // LANES, LANES)
    veloc, x, gram = newmark(
        ndof, ndir, disp, veloc, elem, link, inv, offset, damper_at, damper_k, damper_c
    )
    q_block, r_factor = factor(gram, x, 1.0 / (4.0 * nodes * ndof))
    return veloc, q_block, r_factor


def solution(mesh):
    in_specs = (
        P(None, "dir", "dof"),
        P(None, "dir", "dof"),
        P(None, None, "dof"),
        P(None, None, "dof"),
        P(None, None, "dof"),
        P("dof"),
        P("dof"),
        P(None, None, "dof"),
        P(None, None, "dof"),
    )
    out_specs = (P(None, "dir", "dof"), P(None, None, ("dof", "dir")), P())
    return jax.shard_map(
        functools.partial(on_device, mesh.shape["dof"], mesh.shape["dir"]),
        mesh=mesh,
        in_specs=in_specs,
        out_specs=out_specs,
        check_vma=False,
    )
```

```python
import functools

import jax
import jax.numpy as jnp
from jax import lax
from jax.experimental import pallas as pl
from jax.experimental.pallas import tpu as pltpu
from jax.sharding import PartitionSpec as P

STEP = 0.5
LANES = 128
SUB = 8
REACH = 32
CHIPS_X = 4
MESH = pl.DeviceIdType.MESH
HIGHEST = lax.Precision.HIGHEST


def iota(shape, axis):
    return lax.broadcasted_iota(jnp.int32, shape, axis)


def rolled(x, by, axis):
    by = by % x.shape[axis]
    return pltpu.roll(x, by, axis) if by else x


def lane_gather(x, index):
    return jnp.take_along_axis(x, index, axis=1, mode="promise_in_bounds")


def far_first(offsets, sizes):
    def distance(offset):
        return sum(min(o, n - o) for o, n in zip(offset, sizes))

    return [o for o in sorted(offsets, key=distance, reverse=True) if distance(o)]


def newmark_kernel(
    ndof,
    nx,
    ndir,
    disp_in,
    vel_in,
    elem_in,
    link_in,
    inv_in,
    offset_in,
    damper_at,
    damper_k,
    damper_c,
    vel_out,
    x_out,
    gram_out,
    disp_a,
    disp_b,
    vel,
    coef,
    link_raw,
    inv_raw,
    offset_raw,
    pm,
    qm,
    vm,
    to_send,
    arrived,
    x_all,
    gram_part,
    slots,
    z_part,
    z_slots,
    z_sum,
    gram,
    load_sem,
    halo_send,
    halo_recv,
    a2a_send,
    a2a_recv,
    rs_send,
    rs_recv,
    z_send,
    z_recv,
    ag_send,
    ag_recv,
    store_sem,
):
    me_p = lax.axis_index("dof")
    me_t = lax.axis_index("dir")
    dirs = disp_in.shape[1]
    nodes = disp_in.shape[2]
    tiles = nodes // LANES
    around = tiles + 1
    nz = ndof // nx
    me_z, me_x = me_p // nx, lax.rem(me_p, nx)
    me = me_t * nx + me_x
    share = gram.shape[1] // (nx * ndir)
    plane = far_first([(x, t) for x in range(nx) for t in range(ndir)], (nx, ndir))
    line = [by for by, in far_first([(z,) for z in range(nz)], (nz,))]

    loads = [
        (disp_in, disp_a.at[:, :, 0:nodes]),
        (vel_in, vel.at[:, :, 0:nodes]),
        (elem_in, coef.at[0:8, :, 0:nodes]),
        (link_in, link_raw),
        (inv_in, inv_raw),
        (offset_in, offset_raw),
    ]
    loads = [pltpu.make_async_copy(s, d, load_sem.at[i]) for i, (s, d) in enumerate(loads)]
    for copy in loads:
        copy.start()

    barrier = pltpu.get_barrier_semaphore()

    def greet(p, t):
        pl.semaphore_signal(barrier, inc=1, device_id=(p, t), device_id_type=MESH)

    for by in line:
        greet(lax.rem(me_z + by, nz) * nx + me_x, me_t)
    for by in (1, ndof - 1):
        greet(lax.rem(me_p + by, ndof), me_t)
    for by_x, by_t in plane:
        greet(me_z * nx + lax.rem(me_x + by_x, nx), lax.rem(me_t + by_t, ndir))

    lane = iota((SUB, LANES), 1)
    sub = iota((SUB, LANES), 0)

    def at_tile(t):
        return pl.ds(pl.multiple_of(t * LANES, LANES), LANES)

    columns = []
    for q in range(2):
        column = jnp.zeros((SUB, LANES), jnp.float32)
        for kind, table in enumerate((damper_k, damper_c)):
            for i in range(2):
                for j in range(2):
                    column = jnp.where(sub == 4 * kind + 2 * i + j, table[i, j, q], column)
        columns.append(column)
    for copy in loads[2:]:
        copy.wait()
    for t in range(tiles):
        where = slice(t * LANES, (t + 1) * LANES)
        dense = jnp.zeros((SUB, LANES), jnp.float32)
        for q in range(2):
            place = damper_at[q] - me_p * nodes - t * LANES
            dense = dense + jnp.where(lane == place, columns[q], 0.0)
        coef[12, :, where] = dense
        row = offset_raw[t : t + 1, :].astype(jnp.float32)
        coef[13, :, where] = jnp.broadcast_to(row, (SUB, LANES))
    for half in range(2):
        coef[8 + half, 0:4, 0:nodes] = link_raw[2 * half]
        coef[8 + half, 4:8, 0:nodes] = link_raw[2 * half + 1]
        coef[10 + half, 0:4, 0:nodes] = inv_raw[2 * half]
        coef[10 + half, 4:8, 0:nodes] = inv_raw[2 * half + 1]
    for copy in loads[:2]:
        copy.wait()

    groups = dirs // SUB
    packs = []
    for ref in (disp_a, vel):
        for g in range(groups):
            packs.append([(ref, c, slice(g * SUB, (g + 1) * SUB)) for c in range(4)])
    for g in range(0, 14, 4):
        packs.append([(coef, k, slice(0, SUB)) for k in range(g, min(g + 4, 14))])
    for side, start, first in ((0, nodes - LANES, LANES - REACH), (1, 0, 0)):
        for n, pack in enumerate(packs):
            held = None
            for s, (ref, c, rows) in enumerate(pack):
                piece = rolled(ref[c, rows, start : start + LANES], REACH * s - first, 1)
                held = piece if held is None else jnp.where(lane >= REACH * s, piece, held)
            to_send[side, n] = held

    pl.semaphore_wait(barrier, len(line) + 2 + len(plane))
    halo = []
    for side, by in ((0, 1), (1, ndof - 1)):
        halo.append(
            pltpu.make_async_remote_copy(
                src_ref=to_send.at[side],
                dst_ref=arrived.at[side],
                send_sem=halo_send.at[side],
                recv_sem=halo_recv.at[side],
                device_id=(lax.rem(me_p + by, ndof), me_t),
                device_id_type=MESH,
            )
        )
        halo[-1].start()

    def prepare(t):
        now = at_tile(t)
        before = at_tile(lax.rem(t + around - 1, around))
        p_rows, q_rows = [], []
        for i in range(4):
            shifted = jnp.where(
                lane == 0,
                rolled(coef[4 + i, :, before], 1, 1),
                rolled(coef[4 + i, :, now], 1, 1),
            )
            link = coef[8 + i // 2, :, now]
            if i % 2 == 0:
                link = rolled(link, 4, 0)
            q_rows.append(jnp.where(sub < 4, shifted, link))
            p_rows.append(coef[i, :, now] + jnp.where(sub < 4, rolled(shifted, 4, 0), 0.0))
        film = coef[12, :, now]
        for k in range(2):
            p_rows[k] = p_rows[k] + jnp.where(sub < 2, rolled(film, -2 * k, 0), 0.0)
        v_rows = [rolled(film, -4 - 2 * k, 0) for k in range(2)]
        for i in range(4):
            inv = [
                -coef[10 + i // 2, 4 * (i % 2) + k : 4 * (i % 2) + k + 1, now] for k in range(4)
            ]
            for out, rows in ((pm, p_rows), (qm, q_rows), (vm, v_rows)):
                total = inv[0] * rows[0]
                for k in range(1, len(rows)):
                    total = total + inv[k] * rows[k]
                out[i, :, now] = total

    chunk = min(16, dirs)

    def evaluate(disp, t, finish):
        now = at_tile(t)
        before = at_tile(lax.rem(t + around - 1, around))
        after = at_tile(lax.rem(t + 1, around))
        wide_lane = iota((chunk, LANES), 1)
        target = coef[13, 0:1, now].astype(jnp.int32) + lane[0:1, :]
        inside = jnp.broadcast_to((target >= 0) & (target < LANES), (chunk, LANES))
        index = jnp.broadcast_to(target & (LANES - 1), (chunk, LANES))
        for r in range(0, dirs, chunk):
            rows = slice(r, r + chunk)
            speed = [vel[j, rows, now] for j in range(2)]
            acc = [None] * 4
            for j in range(4):
                here = disp[j, rows, now]
                left = disp[j, rows, before]
                right = disp[j, rows, after]
                previous = jnp.where(wide_lane == 0, rolled(left, 1, 1), rolled(here, 1, 1))
                following = jnp.where(
                    wide_lane == LANES - 1, rolled(right, -1, 1), rolled(here, -1, 1)
                )
                other = jnp.where(wide_lane < LANES // 2, right, left)
                linked = jnp.where(inside, lane_gather(here, index), lane_gather(other, index))
                for i in range(4):
                    total = pm[i, j : j + 1, now] * here
                    total = total + pm[i, 4 + j : 5 + j, now] * following
                    total = total + qm[i, j : j + 1, now] * previous
                    total = total + qm[i, 4 + j : 5 + j, now] * linked
                    if j < 2:
                        total = total + vm[i, j : j + 1, now] * speed[j]
                    acc[i] = total if acc[i] is None else acc[i] + total
            finish(rows, now, acc)

    def finish_first(rows, now, acc):
        for i in range(4):
            v = vel[i, rows, now]
            disp_b[i, rows, now] = (
                disp_a[i, rows, now] + STEP * v + (0.5 * STEP * STEP) * acc[i]
            )
            vel[i, rows, now] = v + (0.5 * STEP) * acc[i]

    def finish_second(rows, now, acc):
        for i in range(4):
            v = vel[i, rows, now] + (0.5 * STEP) * acc[i]
            disp_a[i, rows, now] = (
                disp_b[i, rows, now] + STEP * v + (0.5 * STEP * STEP) * acc[i]
            )
            vel[i, rows, now] = v + (0.5 * STEP) * acc[i]

    def finish_last(rows, now, acc):
        for i in range(4):
            vel[i, rows, now] = vel[i, rows, now] + (0.5 * STEP) * acc[i]

    def prepare_tile(t, carry):
        prepare(t)
        return carry

    def first_tile(t, carry):
        evaluate(disp_a, t, finish_first)
        return carry

    lax.fori_loop(1, tiles, prepare_tile, 0)
    lax.fori_loop(1, tiles - 1, first_tile, 0)

    for copy in halo:
        copy.wait_recv()
    right_end = jnp.where(me_p < ndof - 1, REACH, 0)
    left_start = jnp.where(me_p > 0, LANES - REACH, LANES)
    for n, pack in enumerate(packs):
        from_left, from_right = arrived[0, n], arrived[1, n]
        for s, (ref, c, rows) in enumerate(pack):
            piece = jnp.where(lane < right_end, rolled(from_right, -REACH * s, 1), 0.0)
            ref[c, rows, nodes : nodes + LANES] = jnp.where(
                lane >= left_start, rolled(from_left, LANES - REACH - REACH * s, 1), piece
            )

    def wrapped(k):
        return lax.rem(k, around)

    lax.fori_loop(tiles, tiles + 2, lambda k, c: prepare_tile(wrapped(k), c), 0)
    lax.fori_loop(tiles - 1, tiles + 2, lambda k, c: first_tile(wrapped(k), c), 0)

    def tile_copy(peer):
        return pltpu.make_async_remote_copy(
            src_ref=disp_a.at[:, :, at_tile(peer)],
            dst_ref=x_all.at[:, pl.ds(pl.multiple_of(me_t * dirs, dirs), dirs), :],
            send_sem=a2a_send.at[peer],
            recv_sem=a2a_recv.at[me_t],
            device_id=(me_p, peer),
            device_id_type=MESH,
        )

    def second_tile(by, carry):
        t = lax.rem(me_t + by, ndir)
        evaluate(disp_b, t, finish_second)
        tile_copy(t).start()
        return carry

    half = ndir // 2
    lax.fori_loop(half, ndir, second_tile, 0)
    lax.fori_loop(1, half, lambda k, c: second_tile(half - k, c), 0)
    evaluate(disp_b, me_t, finish_second)
    x_all[:, pl.ds(pl.multiple_of(me_t * dirs, dirs), dirs), :] = disp_a[:, :, at_tile(me_t)]
    evaluate(disp_b, tiles, finish_second)

    def last_tile(t, carry):
        evaluate(disp_a, t, finish_last)
        return carry

    lax.fori_loop(0, tiles, last_tile, 0)
    vel_store = pltpu.make_async_copy(vel.at[:, :, 0:nodes], vel_out, store_sem.at[0])
    vel_store.start()

    def tile_arrival(by):
        source = lax.rem(me_t + by, ndir)
        return pltpu.make_async_remote_copy(
            src_ref=disp_a.at[:, :, at_tile(source)],
            dst_ref=x_all.at[:, pl.ds(pl.multiple_of(source * dirs, dirs), dirs), :],
            send_sem=a2a_send.at[source],
            recv_sem=a2a_recv.at[source],
            device_id=(me_p, source),
            device_id_type=MESH,
        )

    for by in range(1, ndir):
        tile_arrival(by).wait_recv()
    x_store = pltpu.make_async_copy(x_all, x_out, store_sem.at[1])
    x_store.start()

    half_n = gram.shape[1]
    halves = [slice(0, half_n), slice(half_n, 2 * half_n)]
    for b, (i, j) in enumerate(((0, 0), (0, 1), (1, 1))):
        total = None
        for c in range(4):
            product = lax.dot_general(
                x_all[c, halves[i], :],
                x_all[c, halves[j], :],
                (((1,), (1,)), ((), ())),
                precision=HIGHEST,
                preferred_element_type=jnp.float32,
            )
            total = product if total is None else total + product
        gram_part[b] = total

    def part_copy(by):
        peer_x, peer_t = by
        to = lax.rem(me_x + peer_x, nx), lax.rem(me_t + peer_t, ndir)
        member = to[1] * nx + to[0]
        return pltpu.make_async_remote_copy(
            src_ref=gram_part.at[:, pl.ds(member * share, share), :],
            dst_ref=slots.at[:, pl.ds(me * share, share), :],
            send_sem=rs_send,
            recv_sem=rs_recv,
            device_id=(me_z * nx + to[0], to[1]),
            device_id_type=MESH,
        )

    for by in plane:
        part_copy(by).start()
    mine = pl.ds(me * share, share)
    own = pltpu.make_async_copy(gram_part.at[:, mine, :], slots.at[:, mine, :], rs_recv)
    own.start()
    pltpu.make_async_copy(slots, slots, rs_recv).wait()
    total = slots[:, 0:SUB, :]
    for k in range(SUB, slots.shape[1], SUB):
        total = total + slots[:, k : k + SUB, :]
    for b in range(3):
        piece = total[b]
        for k in range(share, SUB, share):
            piece = piece + rolled(total[b], -k, 0)
        z_part[b] = piece

    def z_copy(by):
        return pltpu.make_async_remote_copy(
            src_ref=z_part.at[:, 0:share, :],
            dst_ref=z_slots.at[me_z, :, 0:share, :],
            send_sem=z_send,
            recv_sem=z_recv,
            device_id=(lax.rem(me_z + by, nz) * nx + me_x, me_t),
            device_id_type=MESH,
        )

    for by in line:
        z_copy(by).start()
    own = pltpu.make_async_copy(
        z_part.at[:, 0:share, :], z_slots.at[me_z, :, 0:share, :], z_recv
    )
    own.start()
    arrivals = z_slots.at[:, :, 0:share, :]
    pltpu.make_async_copy(arrivals, arrivals, z_recv).wait()
    total = z_slots[0, :, 0:share, :]
    for k in range(1, nz):
        total = total + z_slots[k, :, 0:share, :]
    z_sum[:, 0:share, :] = total

    def sum_copy(by):
        peer_x, peer_t = by
        to = lax.rem(me_x + peer_x, nx), lax.rem(me_t + peer_t, ndir)
        return pltpu.make_async_remote_copy(
            src_ref=z_sum.at[:, 0:share, :],
            dst_ref=gram.at[:, mine, :],
            send_sem=ag_send,
            recv_sem=ag_recv,
            device_id=(me_z * nx + to[0], to[1]),
            device_id_type=MESH,
        )

    for by in plane:
        sum_copy(by).start()
    own = pltpu.make_async_copy(z_sum.at[:, 0:share, :], gram.at[:, mine, :], ag_recv)
    own.start()
    pltpu.make_async_copy(gram, gram, ag_recv).wait()
    gram_store = pltpu.make_async_copy(gram, gram_out, store_sem.at[2])
    gram_store.start()

    for copy in halo:
        copy.wait_send()
    for by in range(1, ndir):
        tile_copy(lax.rem(me_t + by, ndir)).wait_send()
    for by in plane:
        part_copy(by).wait_send()
        sum_copy(by).wait_send()
    for by in line:
        z_copy(by).wait_send()
    vel_store.wait()
    x_store.wait()
    gram_store.wait()


def newmark(ndof, nx, ndir, *args):
    dirs, nodes = args[0].shape[1:]
    around = nodes + LANES
    n = dirs * ndir
    packs = 2 * (dirs // SUB) + 4
    f32 = jnp.float32
    hbm = pl.BlockSpec(memory_space=pltpu.HBM)
    smem = pl.BlockSpec(memory_space=pltpu.SMEM)
    dma = pltpu.SemaphoreType.DMA
    return pl.pallas_call(
        functools.partial(newmark_kernel, ndof, nx, ndir),
        out_shape=(
            jax.ShapeDtypeStruct((4, dirs, nodes), f32),
            jax.ShapeDtypeStruct((4, n, LANES), f32),
            jax.ShapeDtypeStruct((3, n // 2, n // 2), f32),
        ),
        in_specs=[hbm] * 6 + [smem] * 3,
        out_specs=[hbm] * 3,
        scratch_shapes=[
            pltpu.VMEM((4, dirs, around), f32),
            pltpu.VMEM((4, dirs, around), f32),
            pltpu.VMEM((4, dirs, around), f32),
            pltpu.VMEM((14, SUB, around), f32),
            pltpu.VMEM((4, 4, nodes), f32),
            pltpu.VMEM((4, 4, nodes), f32),
            pltpu.VMEM((nodes // LANES, LANES), jnp.int32),
            pltpu.VMEM((4, SUB, around), f32),
            pltpu.VMEM((4, SUB, around), f32),
            pltpu.VMEM((4, SUB, around), f32),
            pltpu.VMEM((2, packs, SUB, LANES), f32),
            pltpu.VMEM((2, packs, SUB, LANES), f32),
            pltpu.VMEM((4, n, LANES), f32),
            pltpu.VMEM((3, n // 2, n // 2), f32),
            pltpu.VMEM((3, n // 2, n // 2), f32),
            pltpu.VMEM((3, SUB, n // 2), f32),
            pltpu.VMEM((ndof // nx, 3, SUB, n // 2), f32),
            pltpu.VMEM((3, SUB, n // 2), f32),
            pltpu.VMEM((3, n // 2, n // 2), f32),
            dma((6,)),
            dma((2,)),
            dma((2,)),
            dma((ndir,)),
            dma((ndir,)),
            dma(()),
            dma(()),
            dma(()),
            dma(()),
            dma(()),
            dma(()),
            dma((3,)),
        ],
        compiler_params=pltpu.CompilerParams(
            collective_id=0, has_side_effects=True, vmem_limit_bytes=62 * 2**20
        ),
        name="newmark_and_gram",
    )(*args)


def spread(x, lane):
    return jnp.broadcast_to(x[:, lane : lane + 1], (x.shape[0], LANES))


def tiled(x, width):
    return x if width == LANES else jnp.concatenate([x] * (width // LANES), axis=1)


def eliminate(block, micro):
    size, width = block.shape
    row = iota((micro, LANES), 0)
    done = []
    for s in range(0, size, micro):
        top = block[0:micro]
        rest = [block[i : i + SUB] for i in range(micro, size - s, SUB)]
        column = [spread(top, s + j) for j in range(micro)]
        inverse = []
        pivots = jnp.broadcast_to(column[0][0:1], (micro, LANES))
        for j in range(micro):
            pivot = column[j][j : j + 1]
            inverse.append(1.0 / pivot)
            pivots = jnp.where(row == j, pivot, pivots)
            if j == micro - 1:
                break
            factor = jnp.where(row > j, column[j] * inverse[j], 0.0)
            for m in range(j + 1, micro):
                column[m] = column[m] - factor * column[m][j : j + 1]
            top = top - tiled(factor, width) * top[j : j + 1]
        below = []
        for part in rest:
            own = [spread(part, s + j) for j in range(micro)]
            for j in range(micro):
                factor = own[j] * inverse[j]
                for m in range(j + 1, micro):
                    own[m] = own[m] - factor * column[m][j : j + 1]
                part = part - tiled(factor, width) * top[j : j + 1]
            below.append(part)
        done.append(top * tiled(lax.rsqrt(pivots), width))
        if below:
            block = jnp.concatenate(below, axis=0) if len(below) > 1 else below[0]
    return jnp.concatenate(done, axis=0)


def factor_kernel(scale, micro, gram_in, x_in, vel_in, q_out, r_out, vel_out, gram, work, sems):
    size = gram.shape[1]
    n = 2 * size
    gram_load = pltpu.make_async_copy(gram_in, gram, sems.at[0])
    gram_load.start()
    x_loads = [
        pltpu.make_async_copy(
            x_in.at[c], work.at[:, n + LANES * c : n + LANES * (c + 1)], sems.at[1 + c]
        )
        for c in range(4)
    ]
    for copy in x_loads:
        copy.start()
    vel_move = pltpu.make_async_copy(vel_in, vel_out, sems.at[5])
    vel_move.start()
    row, col = iota((size, size), 0), iota((size, size), 1)
    identity = (row == col).astype(jnp.float32)
    r_out[size:, 0:size] = jnp.zeros((size, size), jnp.float32)
    gram_load.wait()
    work[0:size, size:n] = gram[1] * scale
    for low in range(0, n, size):
        high = low + size
        block = gram[0] * scale if low == 0 else work[low:high, low:high]
        block = eliminate(jnp.concatenate([block, identity], axis=1), micro)
        if low == 0:
            for copy in x_loads:
                copy.wait()
        later = jnp.dot(
            block[:, size:],
            work[low:high, high:],
            precision=HIGHEST,
            preferred_element_type=jnp.float32,
        )
        r_out[low:high, low:high] = jnp.where(row <= col, block[:, 0:size], 0.0)
        if low == 0:
            r_out[low:high, high:n] = later[:, 0:size]
            work[high:, high:n] = gram[2] * scale
            work[high:, high:] = work[high:, high:] - lax.dot_general(
                later[:, 0:size],
                later,
                (((0,), (0,)), ((), ())),
                precision=HIGHEST,
                preferred_element_type=jnp.float32,
            )
        for c in range(4):
            start = n - high + LANES * c
            q_out[c, low:high, :] = later[:, start : start + LANES]
    vel_move.wait()


def factor(gram, x, vel, scale):
    n = x.shape[1]
    vmem = pl.BlockSpec(memory_space=pltpu.VMEM)
    hbm = pl.BlockSpec(memory_space=pltpu.HBM)
    return pl.pallas_call(
        functools.partial(factor_kernel, scale, SUB),
        out_shape=(
            jax.ShapeDtypeStruct(x.shape, jnp.float32),
            jax.ShapeDtypeStruct((n, n), jnp.float32),
            jax.ShapeDtypeStruct(vel.shape, jnp.float32),
        ),
        in_specs=[hbm, hbm, hbm],
        out_specs=[vmem, vmem, hbm],
        scratch_shapes=[
            pltpu.VMEM(gram.shape, jnp.float32),
            pltpu.VMEM((n, n + 4 * LANES), jnp.float32),
            pltpu.SemaphoreType.DMA((6,)),
        ],
        compiler_params=pltpu.CompilerParams(vmem_limit_bytes=62 * 2**20),
        name="factor_and_solve",
    )(gram, x, vel)


def on_device(ndof, ndir, disp, veloc, elem, link, inv, offset, damper_at, damper_k, damper_c):
    nodes = disp.shape[2]
    offset = offset.reshape(nodes // LANES, LANES)
    nx = CHIPS_X if ndof % CHIPS_X == 0 else 1
    veloc, x, gram = newmark(
        ndof, nx, ndir, disp, veloc, elem, link, inv, offset, damper_at, damper_k, damper_c
    )
    q_block, r_factor, veloc = factor(gram, x, veloc, 1.0 / (4.0 * nodes * ndof))
    return veloc, q_block, r_factor


def solution(mesh):
    in_specs = (
        P(None, "dir", "dof"),
        P(None, "dir", "dof"),
        P(None, None, "dof"),
        P(None, None, "dof"),
        P(None, None, "dof"),
        P("dof"),
        P("dof"),
        P(None, None, "dof"),
        P(None, None, "dof"),
    )
    out_specs = (P(None, "dir", "dof"), P(None, None, ("dof", "dir")), P())
    return jax.shard_map(
        functools.partial(on_device, mesh.shape["dof"], mesh.shape["dir"]),
        mesh=mesh,
        in_specs=in_specs,
        out_specs=out_specs,
        check_vma=False,
    )
```

```python
import functools

import jax
import jax.numpy as jnp
from jax import lax
from jax.experimental import pallas as pl
from jax.experimental.pallas import tpu as pltpu
from jax.sharding import PartitionSpec as P

STEP = 0.5
LANES = 128
SUB = 8
REACH = 32
CHIPS_X = 4
MESH = pl.DeviceIdType.MESH
HIGHEST = lax.Precision.HIGHEST


def iota(shape, axis):
    return lax.broadcasted_iota(jnp.int32, shape, axis)


def rolled(x, by, axis):
    by = by % x.shape[axis]
    return pltpu.roll(x, by, axis) if by else x


def lane_gather(x, index):
    return jnp.take_along_axis(x, index, axis=1, mode="promise_in_bounds")


def far_first(offsets, sizes):
    def distance(offset):
        return sum(min(o, n - o) for o, n in zip(offset, sizes))

    return [o for o in sorted(offsets, key=distance, reverse=True) if distance(o)]


def newmark_kernel(
    ndof,
    nx,
    ndir,
    disp_in,
    vel_in,
    elem_in,
    link_in,
    inv_in,
    offset_in,
    damper_at,
    damper_k,
    damper_c,
    vel_out,
    x_out,
    gram_out,
    disp_a,
    disp_b,
    vel,
    coef,
    link_raw,
    inv_raw,
    offset_raw,
    pm,
    qm,
    vm,
    to_send,
    arrived,
    x_all,
    gram_part,
    slots,
    z_part,
    z_slots,
    z_sum,
    gram,
    load_sem,
    halo_send,
    halo_recv,
    a2a_send,
    a2a_recv,
    rs_send,
    rs_recv,
    z_send,
    z_recv,
    ag_send,
    ag_recv,
    store_sem,
):
    me_p = lax.axis_index("dof")
    me_t = lax.axis_index("dir")
    dirs = disp_in.shape[1]
    nodes = disp_in.shape[2]
    tiles = nodes // LANES
    around = tiles + 1
    nz = ndof // nx
    me_z, me_x = me_p // nx, lax.rem(me_p, nx)
    me = me_t * nx + me_x
    share = gram.shape[1] // (nx * ndir)
    plane = far_first([(x, t) for x in range(nx) for t in range(ndir)], (nx, ndir))
    line = [by for by, in far_first([(z,) for z in range(nz)], (nz,))]

    loads = [
        (disp_in, disp_a.at[:, :, 0:nodes]),
        (vel_in, vel.at[:, :, 0:nodes]),
        (elem_in, coef.at[0:8, :, 0:nodes]),
        (link_in, link_raw),
        (inv_in, inv_raw),
        (offset_in, offset_raw),
    ]
    loads = [pltpu.make_async_copy(s, d, load_sem.at[i]) for i, (s, d) in enumerate(loads)]
    for copy in loads:
        copy.start()

    barrier = pltpu.get_barrier_semaphore()

    def greet(p, t):
        pl.semaphore_signal(barrier, inc=1, device_id=(p, t), device_id_type=MESH)

    for by in line:
        greet(lax.rem(me_z + by, nz) * nx + me_x, me_t)
    for by in (1, ndof - 1):
        greet(lax.rem(me_p + by, ndof), me_t)
    for by_x, by_t in plane:
        greet(me_z * nx + lax.rem(me_x + by_x, nx), lax.rem(me_t + by_t, ndir))

    lane = iota((SUB, LANES), 1)
    sub = iota((SUB, LANES), 0)

    def at_tile(t):
        return pl.ds(pl.multiple_of(t * LANES, LANES), LANES)

    columns = []
    for q in range(2):
        column = jnp.zeros((SUB, LANES), jnp.float32)
        for kind, table in enumerate((damper_k, damper_c)):
            for i in range(2):
                for j in range(2):
                    column = jnp.where(sub == 4 * kind + 2 * i + j, table[i, j, q], column)
        columns.append(column)
    for copy in loads[2:]:
        copy.wait()
    for t in range(tiles):
        where = slice(t * LANES, (t + 1) * LANES)
        dense = jnp.zeros((SUB, LANES), jnp.float32)
        for q in range(2):
            place = damper_at[q] - me_p * nodes - t * LANES
            dense = dense + jnp.where(lane == place, columns[q], 0.0)
        coef[12, :, where] = dense
        row = offset_raw[t : t + 1, :].astype(jnp.float32)
        coef[13, :, where] = jnp.broadcast_to(row, (SUB, LANES))
    for half in range(2):
        coef[8 + half, 0:4, 0:nodes] = link_raw[2 * half]
        coef[8 + half, 4:8, 0:nodes] = link_raw[2 * half + 1]
        coef[10 + half, 0:4, 0:nodes] = inv_raw[2 * half]
        coef[10 + half, 4:8, 0:nodes] = inv_raw[2 * half + 1]
    for copy in loads[:2]:
        copy.wait()

    groups = dirs // SUB
    packs = []
    for ref in (disp_a, vel):
        for g in range(groups):
            packs.append([(ref, c, slice(g * SUB, (g + 1) * SUB)) for c in range(4)])
    for g in range(0, 14, 4):
        packs.append([(coef, k, slice(0, SUB)) for k in range(g, min(g + 4, 14))])
    for side, start, first in ((0, nodes - LANES, LANES - REACH), (1, 0, 0)):
        for n, pack in enumerate(packs):
            held = None
            for s, (ref, c, rows) in enumerate(pack):
                piece = rolled(ref[c, rows, start : start + LANES], REACH * s - first, 1)
                held = piece if held is None else jnp.where(lane >= REACH * s, piece, held)
            to_send[side, n] = held

    pl.semaphore_wait(barrier, len(line) + 2 + len(plane))
    halo = []
    for side, by in ((0, 1), (1, ndof - 1)):
        halo.append(
            pltpu.make_async_remote_copy(
                src_ref=to_send.at[side],
                dst_ref=arrived.at[side],
                send_sem=halo_send.at[side],
                recv_sem=halo_recv.at[side],
                device_id=(lax.rem(me_p + by, ndof), me_t),
                device_id_type=MESH,
            )
        )
        halo[-1].start()

    def prepare(t):
        now = at_tile(t)
        before = at_tile(lax.rem(t + around - 1, around))
        p_rows, q_rows = [], []
        for i in range(4):
            shifted = jnp.where(
                lane == 0,
                rolled(coef[4 + i, :, before], 1, 1),
                rolled(coef[4 + i, :, now], 1, 1),
            )
            link = coef[8 + i // 2, :, now]
            if i % 2 == 0:
                link = rolled(link, 4, 0)
            q_rows.append(jnp.where(sub < 4, shifted, link))
            p_rows.append(coef[i, :, now] + jnp.where(sub < 4, rolled(shifted, 4, 0), 0.0))
        film = coef[12, :, now]
        for k in range(2):
            p_rows[k] = p_rows[k] + jnp.where(sub < 2, rolled(film, -2 * k, 0), 0.0)
        v_rows = [rolled(film, -4 - 2 * k, 0) for k in range(2)]
        for i in range(4):
            inv = [
                -coef[10 + i // 2, 4 * (i % 2) + k : 4 * (i % 2) + k + 1, now] for k in range(4)
            ]
            for out, rows in ((pm, p_rows), (qm, q_rows), (vm, v_rows)):
                total = inv[0] * rows[0]
                for k in range(1, len(rows)):
                    total = total + inv[k] * rows[k]
                out[i, :, now] = total

    chunk = min(16, dirs)

    def evaluate(disp, t, finish):
        now = at_tile(t)
        before = at_tile(lax.rem(t + around - 1, around))
        after = at_tile(lax.rem(t + 1, around))
        wide_lane = iota((chunk, LANES), 1)
        target = coef[13, 0:1, now].astype(jnp.int32) + lane[0:1, :]
        inside = jnp.broadcast_to((target >= 0) & (target < LANES), (chunk, LANES))
        index = jnp.broadcast_to(target & (LANES - 1), (chunk, LANES))
        for r in range(0, dirs, chunk):
            rows = slice(r, r + chunk)
            speed = [vel[j, rows, now] for j in range(2)]
            acc = [None] * 4
            for j in range(4):
                here = disp[j, rows, now]
                left = disp[j, rows, before]
                right = disp[j, rows, after]
                previous = jnp.where(wide_lane == 0, rolled(left, 1, 1), rolled(here, 1, 1))
                following = jnp.where(
                    wide_lane == LANES - 1, rolled(right, -1, 1), rolled(here, -1, 1)
                )
                other = jnp.where(wide_lane < LANES // 2, right, left)
                linked = jnp.where(inside, lane_gather(here, index), lane_gather(other, index))
                for i in range(4):
                    total = pm[i, j : j + 1, now] * here
                    total = total + pm[i, 4 + j : 5 + j, now] * following
                    total = total + qm[i, j : j + 1, now] * previous
                    total = total + qm[i, 4 + j : 5 + j, now] * linked
                    if j < 2:
                        total = total + vm[i, j : j + 1, now] * speed[j]
                    acc[i] = total if acc[i] is None else acc[i] + total
            finish(rows, now, acc)

    def finish_first(rows, now, acc):
        for i in range(4):
            v = vel[i, rows, now]
            disp_b[i, rows, now] = (
                disp_a[i, rows, now] + STEP * v + (0.5 * STEP * STEP) * acc[i]
            )
            vel[i, rows, now] = v + (0.5 * STEP) * acc[i]

    def finish_second(rows, now, acc):
        for i in range(4):
            v = vel[i, rows, now] + (0.5 * STEP) * acc[i]
            disp_a[i, rows, now] = (
                disp_b[i, rows, now] + STEP * v + (0.5 * STEP * STEP) * acc[i]
            )
            vel[i, rows, now] = v + (0.5 * STEP) * acc[i]

    def finish_last(rows, now, acc):
        for i in range(4):
            vel[i, rows, now] = vel[i, rows, now] + (0.5 * STEP) * acc[i]

    def prepare_tile(t, carry):
        prepare(t)
        return carry

    def first_tile(t, carry):
        evaluate(disp_a, t, finish_first)
        return carry

    lax.fori_loop(1, tiles, prepare_tile, 0)
    lax.fori_loop(1, tiles - 1, first_tile, 0)

    for copy in halo:
        copy.wait_recv()
    right_end = jnp.where(me_p < ndof - 1, REACH, 0)
    left_start = jnp.where(me_p > 0, LANES - REACH, LANES)
    for n, pack in enumerate(packs):
        from_left, from_right = arrived[0, n], arrived[1, n]
        for s, (ref, c, rows) in enumerate(pack):
            piece = jnp.where(lane < right_end, rolled(from_right, -REACH * s, 1), 0.0)
            ref[c, rows, nodes : nodes + LANES] = jnp.where(
                lane >= left_start, rolled(from_left, LANES - REACH - REACH * s, 1), piece
            )

    def wrapped(k):
        return lax.rem(k, around)

    lax.fori_loop(tiles, tiles + 2, lambda k, c: prepare_tile(wrapped(k), c), 0)
    lax.fori_loop(tiles - 1, tiles + 2, lambda k, c: first_tile(wrapped(k), c), 0)

    def tile_copy(peer):
        return pltpu.make_async_remote_copy(
            src_ref=disp_a.at[:, :, at_tile(peer)],
            dst_ref=x_all.at[:, pl.ds(pl.multiple_of(me_t * dirs, dirs), dirs), :],
            send_sem=a2a_send.at[peer],
            recv_sem=a2a_recv.at[me_t],
            device_id=(me_p, peer),
            device_id_type=MESH,
        )

    def second_tile(by, carry):
        t = lax.rem(me_t + by, ndir)
        evaluate(disp_b, t, finish_second)
        tile_copy(t).start()
        return carry

    half = ndir // 2
    lax.fori_loop(half, ndir, second_tile, 0)
    lax.fori_loop(1, half, lambda k, c: second_tile(half - k, c), 0)
    evaluate(disp_b, me_t, finish_second)
    x_all[:, pl.ds(pl.multiple_of(me_t * dirs, dirs), dirs), :] = disp_a[:, :, at_tile(me_t)]
    evaluate(disp_b, tiles, finish_second)

    def last_tile(t, carry):
        evaluate(disp_a, t, finish_last)
        return carry

    lax.fori_loop(0, tiles, last_tile, 0)
    vel_store = pltpu.make_async_copy(vel.at[:, :, 0:nodes], vel_out, store_sem.at[0])
    vel_store.start()

    def tile_arrival(by):
        source = lax.rem(me_t + by, ndir)
        return pltpu.make_async_remote_copy(
            src_ref=disp_a.at[:, :, at_tile(source)],
            dst_ref=x_all.at[:, pl.ds(pl.multiple_of(source * dirs, dirs), dirs), :],
            send_sem=a2a_send.at[source],
            recv_sem=a2a_recv.at[source],
            device_id=(me_p, source),
            device_id_type=MESH,
        )

    for by in range(1, ndir):
        tile_arrival(by).wait_recv()
    x_store = pltpu.make_async_copy(x_all, x_out, store_sem.at[1])
    x_store.start()

    half_n = gram.shape[1]
    halves = [slice(0, half_n), slice(half_n, 2 * half_n)]
    for b, (i, j) in enumerate(((0, 0), (0, 1), (1, 1))):
        total = None
        for c in range(4):
            product = lax.dot_general(
                x_all[c, halves[i], :],
                x_all[c, halves[j], :],
                (((1,), (1,)), ((), ())),
                precision=HIGHEST,
                preferred_element_type=jnp.float32,
            )
            total = product if total is None else total + product
        gram_part[b] = total

    def part_copy(by):
        peer_x, peer_t = by
        to = lax.rem(me_x + peer_x, nx), lax.rem(me_t + peer_t, ndir)
        member = to[1] * nx + to[0]
        return pltpu.make_async_remote_copy(
            src_ref=gram_part.at[:, pl.ds(member * share, share), :],
            dst_ref=slots.at[:, pl.ds(me * share, share), :],
            send_sem=rs_send,
            recv_sem=rs_recv,
            device_id=(me_z * nx + to[0], to[1]),
            device_id_type=MESH,
        )

    for by in plane:
        part_copy(by).start()
    mine = pl.ds(me * share, share)
    own = pltpu.make_async_copy(gram_part.at[:, mine, :], slots.at[:, mine, :], rs_recv)
    own.start()
    pltpu.make_async_copy(slots, slots, rs_recv).wait()
    total = slots[:, 0:SUB, :]
    for k in range(SUB, slots.shape[1], SUB):
        total = total + slots[:, k : k + SUB, :]
    for b in range(3):
        piece = total[b]
        for k in range(share, SUB, share):
            piece = piece + rolled(total[b], -k, 0)
        z_part[b] = piece

    def z_copy(by):
        return pltpu.make_async_remote_copy(
            src_ref=z_part.at[:, 0:share, :],
            dst_ref=z_slots.at[me_z, :, 0:share, :],
            send_sem=z_send,
            recv_sem=z_recv,
            device_id=(lax.rem(me_z + by, nz) * nx + me_x, me_t),
            device_id_type=MESH,
        )

    for by in line:
        z_copy(by).start()
    own = pltpu.make_async_copy(
        z_part.at[:, 0:share, :], z_slots.at[me_z, :, 0:share, :], z_recv
    )
    own.start()
    arrivals = z_slots.at[:, :, 0:share, :]
    pltpu.make_async_copy(arrivals, arrivals, z_recv).wait()
    total = z_slots[0, :, 0:share, :]
    for k in range(1, nz):
        total = total + z_slots[k, :, 0:share, :]
    z_sum[:, 0:share, :] = total

    def sum_copy(by):
        peer_x, peer_t = by
        to = lax.rem(me_x + peer_x, nx), lax.rem(me_t + peer_t, ndir)
        return pltpu.make_async_remote_copy(
            src_ref=z_sum.at[:, 0:share, :],
            dst_ref=gram.at[:, mine, :],
            send_sem=ag_send,
            recv_sem=ag_recv,
            device_id=(me_z * nx + to[0], to[1]),
            device_id_type=MESH,
        )

    for by in plane:
        sum_copy(by).start()
    own = pltpu.make_async_copy(z_sum.at[:, 0:share, :], gram.at[:, mine, :], ag_recv)
    own.start()
    pltpu.make_async_copy(gram, gram, ag_recv).wait()
    gram_store = pltpu.make_async_copy(gram, gram_out, store_sem.at[2])
    gram_store.start()

    for copy in halo:
        copy.wait_send()
    for by in range(1, ndir):
        tile_copy(lax.rem(me_t + by, ndir)).wait_send()
    for by in plane:
        part_copy(by).wait_send()
        sum_copy(by).wait_send()
    for by in line:
        z_copy(by).wait_send()
    vel_store.wait()
    x_store.wait()
    gram_store.wait()


def newmark(ndof, nx, ndir, *args):
    dirs, nodes = args[0].shape[1:]
    around = nodes + LANES
    n = dirs * ndir
    packs = 2 * (dirs // SUB) + 4
    f32 = jnp.float32
    hbm = pl.BlockSpec(memory_space=pltpu.HBM)
    smem = pl.BlockSpec(memory_space=pltpu.SMEM)
    dma = pltpu.SemaphoreType.DMA
    return pl.pallas_call(
        functools.partial(newmark_kernel, ndof, nx, ndir),
        out_shape=(
            jax.ShapeDtypeStruct((4, dirs, nodes), f32),
            jax.ShapeDtypeStruct((4, n, LANES), f32),
            jax.ShapeDtypeStruct((3, n // 2, n // 2), f32),
        ),
        in_specs=[hbm] * 6 + [smem] * 3,
        out_specs=[hbm] * 3,
        scratch_shapes=[
            pltpu.VMEM((4, dirs, around), f32),
            pltpu.VMEM((4, dirs, around), f32),
            pltpu.VMEM((4, dirs, around), f32),
            pltpu.VMEM((14, SUB, around), f32),
            pltpu.VMEM((4, 4, nodes), f32),
            pltpu.VMEM((4, 4, nodes), f32),
            pltpu.VMEM((nodes // LANES, LANES), jnp.int32),
            pltpu.VMEM((4, SUB, around), f32),
            pltpu.VMEM((4, SUB, around), f32),
            pltpu.VMEM((4, SUB, around), f32),
            pltpu.VMEM((2, packs, SUB, LANES), f32),
            pltpu.VMEM((2, packs, SUB, LANES), f32),
            pltpu.VMEM((4, n, LANES), f32),
            pltpu.VMEM((3, n // 2, n // 2), f32),
            pltpu.VMEM((3, n // 2, n // 2), f32),
            pltpu.VMEM((3, SUB, n // 2), f32),
            pltpu.VMEM((ndof // nx, 3, SUB, n // 2), f32),
            pltpu.VMEM((3, SUB, n // 2), f32),
            pltpu.VMEM((3, n // 2, n // 2), f32),
            dma((6,)),
            dma((2,)),
            dma((2,)),
            dma((ndir,)),
            dma((ndir,)),
            dma(()),
            dma(()),
            dma(()),
            dma(()),
            dma(()),
            dma(()),
            dma((3,)),
        ],
        compiler_params=pltpu.CompilerParams(
            collective_id=0, has_side_effects=True, vmem_limit_bytes=62 * 2**20
        ),
        name="newmark_and_gram",
    )(*args)


def spread(x, lane):
    return jnp.broadcast_to(x[:, lane : lane + 1], (x.shape[0], LANES))


def tiled(x, width):
    return x if width == LANES else jnp.concatenate([x] * (width // LANES), axis=1)


def eliminate(block, micro, near):
    size, width = block.shape
    row = iota((micro, LANES), 0)
    rows = [block[i : i + SUB] for i in range(0, size, SUB)]
    done = []
    for s in range(0, size, micro):
        top = jnp.concatenate(rows[: micro // SUB], axis=0)
        rest = rows[micro // SUB :]
        column = [spread(top, s + j) for j in range(micro)]
        inverse = []
        pivots = jnp.broadcast_to(column[0][0:1], (micro, LANES))
        for j in range(micro):
            pivot = column[j][j : j + 1]
            inverse.append(1.0 / pivot)
            pivots = jnp.where(row == j, pivot, pivots)
            if j == micro - 1:
                break
            factor = jnp.where(row > j, column[j] * inverse[j], 0.0)
            for m in range(j + 1, micro):
                column[m] = column[m] - factor * column[m][j : j + 1]
            top = top - tiled(factor, width) * top[j : j + 1]
        rows = []
        for part in rest[:near]:
            own = [spread(part, s + j) for j in range(micro)]
            for j in range(micro):
                factor = own[j] * inverse[j]
                for m in range(j + 1, micro):
                    own[m] = own[m] - factor * column[m][j : j + 1]
                part = part - tiled(factor, width) * top[j : j + 1]
            rows.append(part)
        top = top * tiled(lax.rsqrt(pivots), width)
        if len(rest) > near:
            update = lax.dot_general(
                top[:, 0:size],
                top,
                (((0,), (0,)), ((), ())),
                precision=HIGHEST,
                preferred_element_type=jnp.float32,
            )
            for i in range(near, len(rest)):
                start = s + micro + SUB * i
                rows.append(rest[i] - update[start : start + SUB])
        done.append(top)
    return jnp.concatenate(done, axis=0)


def factor_kernel(
    scale, micro, near, gram_in, x_in, vel_in, q_out, r_out, vel_out, gram, vel, q, r, work, sems
):
    size = gram.shape[1]
    n = 2 * size
    gram_load = pltpu.make_async_copy(gram_in, gram, sems.at[0])
    gram_load.start()
    x_loads = [
        pltpu.make_async_copy(
            x_in.at[c], work.at[:, n + LANES * c : n + LANES * (c + 1)], sems.at[1 + c]
        )
        for c in range(4)
    ]
    for copy in x_loads:
        copy.start()
    vel_load = pltpu.make_async_copy(vel_in, vel, sems.at[5])
    vel_load.start()
    vel_store = pltpu.make_async_copy(vel, vel_out, sems.at[6])
    stores = []
    row, col = iota((size, size), 0), iota((size, size), 1)
    identity = (row == col).astype(jnp.float32)
    r[size:, 0:size] = jnp.zeros((size, size), jnp.float32)
    gram_load.wait()
    work[0:size, size:n] = gram[1] * scale
    for low in range(0, n, size):
        high = low + size
        block = gram[0] * scale if low == 0 else work[low:high, low:high]
        block = eliminate(jnp.concatenate([block, identity], axis=1), micro, near)
        if low == 0:
            for copy in x_loads:
                copy.wait()
            vel_load.wait()
            vel_store.start()
        later = jnp.dot(
            block[:, size:],
            work[low:high, high:],
            precision=HIGHEST,
            preferred_element_type=jnp.float32,
        )
        r[low:high, low:high] = jnp.where(row <= col, block[:, 0:size], 0.0)
        if low == 0:
            r[low:high, high:n] = later[:, 0:size]
            work[high:, high:n] = gram[2] * scale
            work[high:, high:] = work[high:, high:] - lax.dot_general(
                later[:, 0:size],
                later,
                (((0,), (0,)), ((), ())),
                precision=HIGHEST,
                preferred_element_type=jnp.float32,
            )
        for c in range(4):
            start = n - high + LANES * c
            q[c, low:high, :] = later[:, start : start + LANES]
        part = pl.ds(low, size)
        stores += [
            pltpu.make_async_copy(q.at[:, part, :], q_out.at[:, part, :], sems.at[7 + low // size]),
            pltpu.make_async_copy(r.at[part, :], r_out.at[part, :], sems.at[9 + low // size]),
        ]
        for copy in stores[-2:]:
            copy.start()
    for copy in stores:
        copy.wait()
    vel_store.wait()


def factor(gram, x, vel, scale):
    n = x.shape[1]
    hbm = pl.BlockSpec(memory_space=pltpu.HBM)
    return pl.pallas_call(
        functools.partial(factor_kernel, scale, 2 * SUB, 2),
        out_shape=(
            jax.ShapeDtypeStruct(x.shape, jnp.float32),
            jax.ShapeDtypeStruct((n, n), jnp.float32),
            jax.ShapeDtypeStruct(vel.shape, jnp.float32),
        ),
        in_specs=[hbm, hbm, hbm],
        out_specs=[hbm, hbm, hbm],
        scratch_shapes=[
            pltpu.VMEM(gram.shape, jnp.float32),
            pltpu.VMEM(vel.shape, jnp.float32),
            pltpu.VMEM(x.shape, jnp.float32),
            pltpu.VMEM((n, n), jnp.float32),
            pltpu.VMEM((n, n + 4 * LANES), jnp.float32),
            pltpu.SemaphoreType.DMA((11,)),
        ],
        compiler_params=pltpu.CompilerParams(vmem_limit_bytes=62 * 2**20),
        name="factor_and_solve",
    )(gram, x, vel)


def on_device(ndof, ndir, disp, veloc, elem, link, inv, offset, damper_at, damper_k, damper_c):
    nodes = disp.shape[2]
    offset = offset.reshape(nodes // LANES, LANES)
    nx = CHIPS_X if ndof % CHIPS_X == 0 else 1
    veloc, x, gram = newmark(
        ndof, nx, ndir, disp, veloc, elem, link, inv, offset, damper_at, damper_k, damper_c
    )
    q_block, r_factor, veloc = factor(gram, x, veloc, 1.0 / (4.0 * nodes * ndof))
    return veloc, q_block, r_factor


def solution(mesh):
    in_specs = (
        P(None, "dir", "dof"),
        P(None, "dir", "dof"),
        P(None, None, "dof"),
        P(None, None, "dof"),
        P(None, None, "dof"),
        P("dof"),
        P("dof"),
        P(None, None, "dof"),
        P(None, None, "dof"),
    )
    out_specs = (P(None, "dir", "dof"), P(None, None, ("dof", "dir")), P())
    return jax.shard_map(
        functools.partial(on_device, mesh.shape["dof"], mesh.shape["dir"]),
        mesh=mesh,
        in_specs=in_specs,
        out_specs=out_specs,
        check_vma=False,
    )
```

```python
import functools

import jax
import jax.numpy as jnp
from jax import lax
from jax.experimental import pallas as pl
from jax.experimental.pallas import tpu as pltpu
from jax.sharding import PartitionSpec as P

STEP = 0.5
LANES = 128
SUB = 8
REACH = 32
CHIPS_X = 4
MESH = pl.DeviceIdType.MESH
HIGHEST = lax.Precision.HIGHEST


def iota(shape, axis):
    return lax.broadcasted_iota(jnp.int32, shape, axis)


def rolled(x, by, axis):
    by = by % x.shape[axis]
    return pltpu.roll(x, by, axis) if by else x


def lane_gather(x, index):
    return jnp.take_along_axis(x, index, axis=1, mode="promise_in_bounds")


def far_first(offsets, sizes):
    def distance(offset):
        return sum(min(o, n - o) for o, n in zip(offset, sizes))

    return [o for o in sorted(offsets, key=distance, reverse=True) if distance(o)]


def newmark_kernel(
    ndof,
    nx,
    ndir,
    disp_in,
    vel_in,
    elem_in,
    link_in,
    inv_in,
    offset_in,
    damper_at_in,
    damper_k_in,
    damper_c_in,
    vel_out,
    x_out,
    gram,
    disp_a,
    disp_b,
    vel,
    coef,
    link_raw,
    inv_raw,
    offset_raw,
    pm,
    qm,
    vm,
    to_send,
    arrived,
    x_all,
    gram_part,
    slots,
    z_part,
    z_slots,
    z_sum,
    damper_at,
    damper_k,
    damper_c,
    load_sem,
    halo_send,
    halo_recv,
    a2a_send,
    a2a_recv,
    rs_send,
    rs_recv,
    z_send,
    z_recv,
    ag_send,
    ag_recv,
    store_sem,
):
    me_p = lax.axis_index("dof")
    me_t = lax.axis_index("dir")
    dirs = disp_in.shape[1]
    nodes = disp_in.shape[2]
    tiles = nodes // LANES
    around = tiles + 1
    nz = ndof // nx
    me_z, me_x = me_p // nx, lax.rem(me_p, nx)
    me = me_t * nx + me_x
    share = gram.shape[1] // (nx * ndir)
    plane = far_first([(x, t) for x in range(nx) for t in range(ndir)], (nx, ndir))
    line = [by for by, in far_first([(z,) for z in range(nz)], (nz,))]

    loads = [
        (disp_in, disp_a.at[:, :, 0:nodes]),
        (vel_in, vel.at[:, :, 0:nodes]),
        (elem_in, coef.at[0:8, :, 0:nodes]),
        (link_in, link_raw),
        (inv_in, inv_raw),
        (offset_in, offset_raw),
        (damper_at_in, damper_at),
        (damper_k_in, damper_k),
        (damper_c_in, damper_c),
    ]
    loads = [pltpu.make_async_copy(s, d, load_sem.at[i]) for i, (s, d) in enumerate(loads)]
    for copy in loads:
        copy.start()

    barrier = pltpu.get_barrier_semaphore()

    def greet(p, t):
        pl.semaphore_signal(barrier, inc=1, device_id=(p, t), device_id_type=MESH)

    for by in (1, ndof - 1):
        greet(lax.rem(me_p + by, ndof), me_t)
    for by, in far_first([(t,) for t in range(ndir)], (ndir,)):
        greet(me_p, lax.rem(me_t + by, ndir))
    for by in line:
        greet(lax.rem(me_z + by, nz) * nx + me_x, me_t)
    for by in range(1, nx):
        greet(me_z * nx + lax.rem(me_x + by, nx), me_t)

    lane = iota((SUB, LANES), 1)
    sub = iota((SUB, LANES), 0)

    def at_tile(t):
        return pl.ds(pl.multiple_of(t * LANES, LANES), LANES)

    for copy in loads[2:]:
        copy.wait()
    columns = []
    for q in range(2):
        column = jnp.zeros((SUB, LANES), jnp.float32)
        for kind, table in enumerate((damper_k, damper_c)):
            for i in range(2):
                for j in range(2):
                    column = jnp.where(sub == 4 * kind + 2 * i + j, table[i, j, q], column)
        columns.append(column)
    for t in range(tiles):
        where = slice(t * LANES, (t + 1) * LANES)
        dense = jnp.zeros((SUB, LANES), jnp.float32)
        for q in range(2):
            place = damper_at[q] - me_p * nodes - t * LANES
            dense = dense + jnp.where(lane == place, columns[q], 0.0)
        coef[12, :, where] = dense
        row = offset_raw[t : t + 1, :].astype(jnp.float32)
        coef[13, :, where] = jnp.broadcast_to(row, (SUB, LANES))
    for half in range(2):
        coef[8 + half, 0:4, 0:nodes] = link_raw[2 * half]
        coef[8 + half, 4:8, 0:nodes] = link_raw[2 * half + 1]
        coef[10 + half, 0:4, 0:nodes] = inv_raw[2 * half]
        coef[10 + half, 4:8, 0:nodes] = inv_raw[2 * half + 1]
    for copy in loads[:2]:
        copy.wait()

    groups = dirs // SUB
    packs = []
    for ref in (disp_a, vel):
        for g in range(groups):
            packs.append([(ref, c, slice(g * SUB, (g + 1) * SUB)) for c in range(4)])
    for g in range(0, 14, 4):
        packs.append([(coef, k, slice(0, SUB)) for k in range(g, min(g + 4, 14))])
    for side, start, first in ((0, nodes - LANES, LANES - REACH), (1, 0, 0)):
        for n, pack in enumerate(packs):
            held = None
            for s, (ref, c, rows) in enumerate(pack):
                piece = rolled(ref[c, rows, start : start + LANES], REACH * s - first, 1)
                held = piece if held is None else jnp.where(lane >= REACH * s, piece, held)
            to_send[side, n] = held

    pl.semaphore_wait(barrier, 2 + ndir - 1 + nz - 1 + nx - 1)
    halo = []
    for side, by in ((0, 1), (1, ndof - 1)):
        halo.append(
            pltpu.make_async_remote_copy(
                src_ref=to_send.at[side],
                dst_ref=arrived.at[side],
                send_sem=halo_send.at[side],
                recv_sem=halo_recv.at[side],
                device_id=(lax.rem(me_p + by, ndof), me_t),
                device_id_type=MESH,
            )
        )
        halo[-1].start()

    def prepare(t):
        now = at_tile(t)
        before = at_tile(lax.rem(t + around - 1, around))
        p_rows, q_rows = [], []
        for i in range(4):
            shifted = jnp.where(
                lane == 0,
                rolled(coef[4 + i, :, before], 1, 1),
                rolled(coef[4 + i, :, now], 1, 1),
            )
            link = coef[8 + i // 2, :, now]
            if i % 2 == 0:
                link = rolled(link, 4, 0)
            q_rows.append(jnp.where(sub < 4, shifted, link))
            p_rows.append(coef[i, :, now] + jnp.where(sub < 4, rolled(shifted, 4, 0), 0.0))
        film = coef[12, :, now]
        for k in range(2):
            p_rows[k] = p_rows[k] + jnp.where(sub < 2, rolled(film, -2 * k, 0), 0.0)
        v_rows = [rolled(film, -4 - 2 * k, 0) for k in range(2)]
        for i in range(4):
            inv = [
                -coef[10 + i // 2, 4 * (i % 2) + k : 4 * (i % 2) + k + 1, now] for k in range(4)
            ]
            for out, rows in ((pm, p_rows), (qm, q_rows), (vm, v_rows)):
                total = inv[0] * rows[0]
                for k in range(1, len(rows)):
                    total = total + inv[k] * rows[k]
                out[i, :, now] = total

    chunk = min(16, dirs)

    def evaluate(disp, t, finish):
        now = at_tile(t)
        before = at_tile(lax.rem(t + around - 1, around))
        after = at_tile(lax.rem(t + 1, around))
        wide_lane = iota((chunk, LANES), 1)
        target = coef[13, 0:1, now].astype(jnp.int32) + lane[0:1, :]
        inside = jnp.broadcast_to((target >= 0) & (target < LANES), (chunk, LANES))
        index = jnp.broadcast_to(target & (LANES - 1), (chunk, LANES))
        for r in range(0, dirs, chunk):
            rows = slice(r, r + chunk)
            speed = [vel[j, rows, now] for j in range(2)]
            acc = [None] * 4
            for j in range(4):
                here = disp[j, rows, now]
                left = disp[j, rows, before]
                right = disp[j, rows, after]
                previous = jnp.where(wide_lane == 0, rolled(left, 1, 1), rolled(here, 1, 1))
                following = jnp.where(
                    wide_lane == LANES - 1, rolled(right, -1, 1), rolled(here, -1, 1)
                )
                other = jnp.where(wide_lane < LANES // 2, right, left)
                linked = jnp.where(inside, lane_gather(here, index), lane_gather(other, index))
                for i in range(4):
                    total = pm[i, j : j + 1, now] * here
                    total = total + pm[i, 4 + j : 5 + j, now] * following
                    total = total + qm[i, j : j + 1, now] * previous
                    total = total + qm[i, 4 + j : 5 + j, now] * linked
                    if j < 2:
                        total = total + vm[i, j : j + 1, now] * speed[j]
                    acc[i] = total if acc[i] is None else acc[i] + total
            finish(rows, now, acc)

    def finish_first(rows, now, acc):
        for i in range(4):
            v = vel[i, rows, now]
            disp_b[i, rows, now] = (
                disp_a[i, rows, now] + STEP * v + (0.5 * STEP * STEP) * acc[i]
            )
            vel[i, rows, now] = v + (0.5 * STEP) * acc[i]

    def finish_second(rows, now, acc):
        for i in range(4):
            v = vel[i, rows, now] + (0.5 * STEP) * acc[i]
            disp_a[i, rows, now] = (
                disp_b[i, rows, now] + STEP * v + (0.5 * STEP * STEP) * acc[i]
            )
            vel[i, rows, now] = v + (0.5 * STEP) * acc[i]

    def finish_last(rows, now, acc):
        for i in range(4):
            vel[i, rows, now] = vel[i, rows, now] + (0.5 * STEP) * acc[i]

    def prepare_tile(t, carry):
        prepare(t)
        return carry

    def first_tile(t, carry):
        evaluate(disp_a, t, finish_first)
        return carry

    lax.fori_loop(1, tiles, prepare_tile, 0)
    lax.fori_loop(1, tiles - 1, first_tile, 0)

    for copy in halo:
        copy.wait_recv()
    right_end = jnp.where(me_p < ndof - 1, REACH, 0)
    left_start = jnp.where(me_p > 0, LANES - REACH, LANES)
    for n, pack in enumerate(packs):
        from_left, from_right = arrived[0, n], arrived[1, n]
        for s, (ref, c, rows) in enumerate(pack):
            piece = jnp.where(lane < right_end, rolled(from_right, -REACH * s, 1), 0.0)
            ref[c, rows, nodes : nodes + LANES] = jnp.where(
                lane >= left_start, rolled(from_left, LANES - REACH - REACH * s, 1), piece
            )

    def wrapped(k):
        return lax.rem(k, around)

    lax.fori_loop(tiles, tiles + 2, lambda k, c: prepare_tile(wrapped(k), c), 0)
    lax.fori_loop(tiles - 1, tiles + 2, lambda k, c: first_tile(wrapped(k), c), 0)

    def tile_copy(peer):
        return pltpu.make_async_remote_copy(
            src_ref=disp_a.at[:, :, at_tile(peer)],
            dst_ref=x_all.at[:, pl.ds(pl.multiple_of(me_t * dirs, dirs), dirs), :],
            send_sem=a2a_send.at[peer],
            recv_sem=a2a_recv.at[me_t],
            device_id=(me_p, peer),
            device_id_type=MESH,
        )

    def second_tile(by, carry):
        t = lax.rem(me_t + by, ndir)
        evaluate(disp_b, t, finish_second)
        tile_copy(t).start()
        return carry

    half = ndir // 2
    lax.fori_loop(half, ndir, second_tile, 0)
    lax.fori_loop(1, half, lambda k, c: second_tile(half - k, c), 0)
    evaluate(disp_b, me_t, finish_second)
    x_all[:, pl.ds(pl.multiple_of(me_t * dirs, dirs), dirs), :] = disp_a[:, :, at_tile(me_t)]
    evaluate(disp_b, tiles, finish_second)

    def last_tile(t, carry):
        evaluate(disp_a, t, finish_last)
        return carry

    lax.fori_loop(0, tiles, last_tile, 0)
    vel_store = pltpu.make_async_copy(vel.at[:, :, 0:nodes], vel_out, store_sem.at[0])
    vel_store.start()

    def tile_arrival(by):
        source = lax.rem(me_t + by, ndir)
        return pltpu.make_async_remote_copy(
            src_ref=disp_a.at[:, :, at_tile(source)],
            dst_ref=x_all.at[:, pl.ds(pl.multiple_of(source * dirs, dirs), dirs), :],
            send_sem=a2a_send.at[source],
            recv_sem=a2a_recv.at[source],
            device_id=(me_p, source),
            device_id_type=MESH,
        )

    for by in range(1, ndir):
        tile_arrival(by).wait_recv()
    x_store = pltpu.make_async_copy(x_all, x_out, store_sem.at[1])
    x_store.start()

    half_n = gram.shape[1]
    halves = [slice(0, half_n), slice(half_n, 2 * half_n)]
    for b, (i, j) in enumerate(((0, 0), (0, 1), (1, 1))):
        total = None
        for c in range(4):
            product = lax.dot_general(
                x_all[c, halves[i], :],
                x_all[c, halves[j], :],
                (((1,), (1,)), ((), ())),
                precision=HIGHEST,
                preferred_element_type=jnp.float32,
            )
            total = product if total is None else total + product
        gram_part[b] = total

    def part_copy(by):
        peer_x, peer_t = by
        to = lax.rem(me_x + peer_x, nx), lax.rem(me_t + peer_t, ndir)
        member = to[1] * nx + to[0]
        return pltpu.make_async_remote_copy(
            src_ref=gram_part.at[:, pl.ds(member * share, share), :],
            dst_ref=slots.at[:, pl.ds(me * share, share), :],
            send_sem=rs_send,
            recv_sem=rs_recv,
            device_id=(me_z * nx + to[0], to[1]),
            device_id_type=MESH,
        )

    for by in plane:
        part_copy(by).start()
    mine = pl.ds(me * share, share)
    own = pltpu.make_async_copy(gram_part.at[:, mine, :], slots.at[:, mine, :], rs_recv)
    own.start()
    pltpu.make_async_copy(slots, slots, rs_recv).wait()
    total = slots[:, 0:SUB, :]
    for k in range(SUB, slots.shape[1], SUB):
        total = total + slots[:, k : k + SUB, :]
    for b in range(3):
        piece = total[b]
        for k in range(share, SUB, share):
            piece = piece + rolled(total[b], -k, 0)
        z_part[b] = piece

    def z_copy(by):
        return pltpu.make_async_remote_copy(
            src_ref=z_part.at[:, 0:share, :],
            dst_ref=z_slots.at[me_z, :, 0:share, :],
            send_sem=z_send,
            recv_sem=z_recv,
            device_id=(lax.rem(me_z + by, nz) * nx + me_x, me_t),
            device_id_type=MESH,
        )

    for by in line:
        z_copy(by).start()
    own = pltpu.make_async_copy(
        z_part.at[:, 0:share, :], z_slots.at[me_z, :, 0:share, :], z_recv
    )
    own.start()
    arrivals = z_slots.at[:, :, 0:share, :]
    pltpu.make_async_copy(arrivals, arrivals, z_recv).wait()
    total = z_slots[0, :, 0:share, :]
    for k in range(1, nz):
        total = total + z_slots[k, :, 0:share, :]
    z_sum[:, 0:share, :] = total

    def sum_copy(by):
        peer_x, peer_t = by
        to = lax.rem(me_x + peer_x, nx), lax.rem(me_t + peer_t, ndir)
        return pltpu.make_async_remote_copy(
            src_ref=z_sum.at[:, 0:share, :],
            dst_ref=gram.at[:, mine, :],
            send_sem=ag_send,
            recv_sem=ag_recv,
            device_id=(me_z * nx + to[0], to[1]),
            device_id_type=MESH,
        )

    for by in plane:
        sum_copy(by).start()
    own = pltpu.make_async_copy(z_sum.at[:, 0:share, :], gram.at[:, mine, :], ag_recv)
    own.start()
    pltpu.make_async_copy(gram, gram, ag_recv).wait()

    for copy in halo:
        copy.wait_send()
    for by in range(1, ndir):
        tile_copy(lax.rem(me_t + by, ndir)).wait_send()
    for by in plane:
        part_copy(by).wait_send()
        sum_copy(by).wait_send()
    for by in line:
        z_copy(by).wait_send()
    vel_store.wait()
    x_store.wait()


def newmark(ndof, nx, ndir, *args):
    dirs, nodes = args[0].shape[1:]
    around = nodes + LANES
    n = dirs * ndir
    packs = 2 * (dirs // SUB) + 4
    f32 = jnp.float32
    hbm = pl.BlockSpec(memory_space=pltpu.HBM)
    vmem = pl.BlockSpec(memory_space=pltpu.VMEM)
    dma = pltpu.SemaphoreType.DMA
    return pl.pallas_call(
        functools.partial(newmark_kernel, ndof, nx, ndir),
        out_shape=(
            pltpu.VMEM((4, dirs, nodes), f32),
            pltpu.VMEM((4, n, LANES), f32),
            pltpu.VMEM((3, n // 2, n // 2), f32),
        ),
        in_specs=[hbm] * 9,
        out_specs=[vmem] * 3,
        scratch_shapes=[
            pltpu.VMEM((4, dirs, around), f32),
            pltpu.VMEM((4, dirs, around), f32),
            pltpu.VMEM((4, dirs, around), f32),
            pltpu.VMEM((14, SUB, around), f32),
            pltpu.VMEM((4, 4, nodes), f32),
            pltpu.VMEM((4, 4, nodes), f32),
            pltpu.VMEM((nodes // LANES, LANES), jnp.int32),
            pltpu.VMEM((4, SUB, around), f32),
            pltpu.VMEM((4, SUB, around), f32),
            pltpu.VMEM((4, SUB, around), f32),
            pltpu.VMEM((2, packs, SUB, LANES), f32),
            pltpu.VMEM((2, packs, SUB, LANES), f32),
            pltpu.VMEM((4, n, LANES), f32),
            pltpu.VMEM((3, n // 2, n // 2), f32),
            pltpu.VMEM((3, n // 2, n // 2), f32),
            pltpu.VMEM((3, SUB, n // 2), f32),
            pltpu.VMEM((ndof // nx, 3, SUB, n // 2), f32),
            pltpu.VMEM((3, SUB, n // 2), f32),
            pltpu.SMEM(args[6].shape, jnp.int32),
            pltpu.SMEM(args[7].shape, f32),
            pltpu.SMEM(args[8].shape, f32),
            dma((9,)),
            dma((2,)),
            dma((2,)),
            dma((ndir,)),
            dma((ndir,)),
            dma(()),
            dma(()),
            dma(()),
            dma(()),
            dma(()),
            dma(()),
            dma((2,)),
        ],
        compiler_params=pltpu.CompilerParams(
            collective_id=0, has_side_effects=True, vmem_limit_bytes=32 * 2**20
        ),
        name="newmark_and_gram",
    )(*[pltpu.with_memory_space_constraint(x, pltpu.HBM) for x in args])


def spread(x, lane):
    return jnp.broadcast_to(x[:, lane : lane + 1], (x.shape[0], LANES))


def tiled(x, width):
    return x if width == LANES else jnp.concatenate([x] * (width // LANES), axis=1)


def eliminate(block, micro, near):
    size, width = block.shape
    row = iota((micro, LANES), 0)
    rows = [block[i : i + SUB] for i in range(0, size, SUB)]
    done = []
    for s in range(0, size, micro):
        top = jnp.concatenate(rows[: micro // SUB], axis=0)
        rest = rows[micro // SUB :]
        column = [spread(top, s + j) for j in range(micro)]
        inverse = []
        pivots = jnp.broadcast_to(column[0][0:1], (micro, LANES))
        for j in range(micro):
            pivot = column[j][j : j + 1]
            inverse.append(1.0 / pivot)
            pivots = jnp.where(row == j, pivot, pivots)
            if j == micro - 1:
                break
            factor = jnp.where(row > j, column[j] * inverse[j], 0.0)
            for m in range(j + 1, micro):
                column[m] = column[m] - factor * column[m][j : j + 1]
            top = top - tiled(factor, width) * top[j : j + 1]
        rows = []
        for part in rest[:near]:
            own = [spread(part, s + j) for j in range(micro)]
            for j in range(micro):
                factor = own[j] * inverse[j]
                for m in range(j + 1, micro):
                    own[m] = own[m] - factor * column[m][j : j + 1]
                part = part - tiled(factor, width) * top[j : j + 1]
            rows.append(part)
        top = top * tiled(lax.rsqrt(pivots), width)
        if len(rest) > near:
            update = lax.dot_general(
                top[:, 0:size],
                top,
                (((0,), (0,)), ((), ())),
                precision=HIGHEST,
                preferred_element_type=jnp.float32,
            )
            for i in range(near, len(rest)):
                start = s + micro + SUB * i
                rows.append(rest[i] - update[start : start + SUB])
        done.append(top)
    return jnp.concatenate(done, axis=0)


def factor_kernel(
    scale, micro, near, gram, x, vel, q_out, r_out, vel_out, q, r, work, sems
):
    size = gram.shape[1]
    n = 2 * size
    vel_store = pltpu.make_async_copy(vel, vel_out, sems.at[0])
    vel_store.start()
    x_loads = [
        pltpu.make_async_copy(
            x.at[c], work.at[:, n + LANES * c : n + LANES * (c + 1)], sems.at[1 + c]
        )
        for c in range(4)
    ]
    for copy in x_loads:
        copy.start()
    stores = []
    row, col = iota((size, size), 0), iota((size, size), 1)
    identity = (row == col).astype(jnp.float32)
    r[size:, 0:size] = jnp.zeros((size, size), jnp.float32)
    work[0:size, size:n] = gram[1] * scale
    for low in range(0, n, size):
        high = low + size
        block = gram[0] * scale if low == 0 else work[low:high, low:high]
        block = eliminate(jnp.concatenate([block, identity], axis=1), micro, near)
        if low == 0:
            for copy in x_loads:
                copy.wait()
        later = jnp.dot(
            block[:, size:],
            work[low:high, high:],
            precision=HIGHEST,
            preferred_element_type=jnp.float32,
        )
        r[low:high, low:high] = jnp.where(row <= col, block[:, 0:size], 0.0)
        if low == 0:
            r[low:high, high:n] = later[:, 0:size]
            work[high:, high:n] = gram[2] * scale
            work[high:, high:] = work[high:, high:] - lax.dot_general(
                later[:, 0:size],
                later,
                (((0,), (0,)), ((), ())),
                precision=HIGHEST,
                preferred_element_type=jnp.float32,
            )
        for c in range(4):
            start = n - high + LANES * c
            q[c, low:high, :] = later[:, start : start + LANES]
        part = pl.ds(low, size)
        stores += [
            pltpu.make_async_copy(q.at[:, part, :], q_out.at[:, part, :], sems.at[5 + low // size]),
            pltpu.make_async_copy(r.at[part, :], r_out.at[part, :], sems.at[7 + low // size]),
        ]
        for copy in stores[-2:]:
            copy.start()
    for copy in stores:
        copy.wait()
    vel_store.wait()


def factor(gram, x, vel, scale):
    n = x.shape[1]
    vmem = pl.BlockSpec(memory_space=pltpu.VMEM)
    hbm = pl.BlockSpec(memory_space=pltpu.HBM)
    return pl.pallas_call(
        functools.partial(factor_kernel, scale, 2 * SUB, 2),
        out_shape=(
            pltpu.HBM(x.shape, jnp.float32),
            pltpu.HBM((n, n), jnp.float32),
            pltpu.HBM(vel.shape, jnp.float32),
        ),
        in_specs=[vmem, vmem, vmem],
        out_specs=[hbm, hbm, hbm],
        scratch_shapes=[
            pltpu.VMEM(x.shape, jnp.float32),
            pltpu.VMEM((n, n), jnp.float32),
            pltpu.VMEM((n, n + 4 * LANES), jnp.float32),
            pltpu.SemaphoreType.DMA((9,)),
        ],
        compiler_params=pltpu.CompilerParams(vmem_limit_bytes=32 * 2**20),
        name="factor_and_solve",
    )(*[pltpu.with_memory_space_constraint(y, pltpu.VMEM) for y in (gram, x, vel)])


def on_device(ndof, ndir, disp, veloc, elem, link, inv, offset, damper_at, damper_k, damper_c):
    nodes = disp.shape[2]
    offset = offset.reshape(nodes // LANES, LANES)
    nx = CHIPS_X if ndof % CHIPS_X == 0 else 1
    veloc, x, gram = newmark(
        ndof, nx, ndir, disp, veloc, elem, link, inv, offset, damper_at, damper_k, damper_c
    )
    q_block, r_factor, veloc = factor(gram, x, veloc, 1.0 / (4.0 * nodes * ndof))
    return veloc, q_block, r_factor


def solution(mesh):
    in_specs = (
        P(None, "dir", "dof"),
        P(None, "dir", "dof"),
        P(None, None, "dof"),
        P(None, None, "dof"),
        P(None, None, "dof"),
        P("dof"),
        P("dof"),
        P(None, None, "dof"),
        P(None, None, "dof"),
    )
    out_specs = (P(None, "dir", "dof"), P(None, None, ("dof", "dir")), P())
    return jax.shard_map(
        functools.partial(on_device, mesh.shape["dof"], mesh.shape["dir"]),
        mesh=mesh,
        in_specs=in_specs,
        out_specs=out_specs,
        check_vma=False,
    )
```

```python
import functools

import jax
import jax.numpy as jnp
from jax import lax
from jax.experimental import pallas as pl
from jax.experimental.pallas import tpu as pltpu
from jax.sharding import PartitionSpec as P

STEP = 0.5
LANES = 128
SUB = 8
REACH = 32
CHIPS_X = 4
MESH = pl.DeviceIdType.MESH
HIGHEST = lax.Precision.HIGHEST


def iota(shape, axis):
    return lax.broadcasted_iota(jnp.int32, shape, axis)


def rolled(x, by, axis):
    by = by % x.shape[axis]
    return pltpu.roll(x, by, axis) if by else x


def lane_gather(x, index):
    return jnp.take_along_axis(x, index, axis=1, mode="promise_in_bounds")


def far_first(offsets, sizes):
    def distance(offset):
        return sum(min(o, n - o) for o, n in zip(offset, sizes))

    return [o for o in sorted(offsets, key=distance, reverse=True) if distance(o)]


def newmark_kernel(
    ndof,
    nx,
    ndir,
    disp_in,
    vel_in,
    elem_in,
    link_in,
    inv_in,
    offset_in,
    damper_at_in,
    damper_k_in,
    damper_c_in,
    vel_out,
    x_all,
    gram,
    disp_a,
    disp_b,
    vel,
    coef,
    link_raw,
    inv_raw,
    offset_raw,
    pm,
    qm,
    vm,
    to_send,
    arrived,
    gram_part,
    slots,
    z_part,
    z_slots,
    z_sum,
    damper_at,
    damper_k,
    damper_c,
    load_sem,
    halo_send,
    halo_recv,
    a2a_send,
    a2a_recv,
    rs_send,
    rs_recv,
    z_send,
    z_recv,
    ag_send,
    ag_recv,
):
    me_p = lax.axis_index("dof")
    me_t = lax.axis_index("dir")
    dirs = disp_in.shape[1]
    nodes = disp_in.shape[2]
    tiles = nodes // LANES
    around = tiles + 1
    nz = ndof // nx
    me_z, me_x = me_p // nx, lax.rem(me_p, nx)
    me = me_t * nx + me_x
    share = gram.shape[1] // (nx * ndir)
    plane = far_first([(x, t) for x in range(nx) for t in range(ndir)], (nx, ndir))
    line = [by for by, in far_first([(z,) for z in range(nz)], (nz,))]

    loads = [
        (disp_in, disp_a.at[:, :, 0:nodes]),
        (vel_in, vel.at[:, :, 0:nodes]),
        (elem_in, coef.at[0:8, :, 0:nodes]),
        (link_in, link_raw),
        (inv_in, inv_raw),
        (offset_in, offset_raw),
        (damper_at_in, damper_at),
        (damper_k_in, damper_k),
        (damper_c_in, damper_c),
    ]
    loads = [pltpu.make_async_copy(s, d, load_sem.at[i]) for i, (s, d) in enumerate(loads)]
    for copy in loads:
        copy.start()

    at_x = [lax.rem(me_x + by, nx) for by in range(nx)]
    at_t = [lax.rem(me_t + by, ndir) for by in range(ndir)]
    barrier = pltpu.get_barrier_semaphore()

    def greet(p, t):
        pl.semaphore_signal(barrier, inc=1, device_id=(p, t), device_id_type=MESH)

    for by in (1, ndof - 1):
        greet(lax.rem(me_p + by, ndof), me_t)
    for by, in far_first([(t,) for t in range(ndir)], (ndir,)):
        greet(me_p, lax.rem(me_t + by, ndir))
    for by in line:
        greet(lax.rem(me_z + by, nz) * nx + me_x, me_t)
    for by in range(1, nx):
        greet(me_z * nx + lax.rem(me_x + by, nx), me_t)

    lane = iota((SUB, LANES), 1)
    sub = iota((SUB, LANES), 0)

    def at_tile(t):
        return pl.ds(pl.multiple_of(t * LANES, LANES), LANES)

    for copy in loads[2:]:
        copy.wait()
    columns = []
    for q in range(2):
        column = jnp.zeros((SUB, LANES), jnp.float32)
        for kind, table in enumerate((damper_k, damper_c)):
            for i in range(2):
                for j in range(2):
                    column = jnp.where(sub == 4 * kind + 2 * i + j, table[i, j, q], column)
        columns.append(column)
    for t in range(tiles):
        where = slice(t * LANES, (t + 1) * LANES)
        dense = jnp.zeros((SUB, LANES), jnp.float32)
        for q in range(2):
            place = damper_at[q] - me_p * nodes - t * LANES
            dense = dense + jnp.where(lane == place, columns[q], 0.0)
        coef[12, :, where] = dense
        row = offset_raw[t : t + 1, :].astype(jnp.float32)
        coef[13, :, where] = jnp.broadcast_to(row, (SUB, LANES))
    for half in range(2):
        coef[8 + half, 0:4, 0:nodes] = link_raw[2 * half]
        coef[8 + half, 4:8, 0:nodes] = link_raw[2 * half + 1]
        coef[10 + half, 0:4, 0:nodes] = inv_raw[2 * half]
        coef[10 + half, 4:8, 0:nodes] = inv_raw[2 * half + 1]
    for copy in loads[:2]:
        copy.wait()

    groups = dirs // SUB
    packs = []
    for ref in (disp_a, vel):
        for g in range(groups):
            packs.append([(ref, c, slice(g * SUB, (g + 1) * SUB)) for c in range(4)])
    for g in range(0, 14, 4):
        packs.append([(coef, k, slice(0, SUB)) for k in range(g, min(g + 4, 14))])
    for side, start, first in ((0, nodes - LANES, LANES - REACH), (1, 0, 0)):
        for n, pack in enumerate(packs):
            held = None
            for s, (ref, c, rows) in enumerate(pack):
                piece = rolled(ref[c, rows, start : start + LANES], REACH * s - first, 1)
                held = piece if held is None else jnp.where(lane >= REACH * s, piece, held)
            to_send[side, n] = held

    pl.semaphore_wait(barrier, 2 + ndir - 1 + nz - 1 + nx - 1)
    halo = []
    for side, by in ((0, 1), (1, ndof - 1)):
        halo.append(
            pltpu.make_async_remote_copy(
                src_ref=to_send.at[side],
                dst_ref=arrived.at[side],
                send_sem=halo_send.at[side],
                recv_sem=halo_recv.at[side],
                device_id=(lax.rem(me_p + by, ndof), me_t),
                device_id_type=MESH,
            )
        )
        halo[-1].start()

    def prepare(t):
        now = at_tile(t)
        before = at_tile(lax.rem(t + around - 1, around))
        p_rows, q_rows = [], []
        for i in range(4):
            shifted = jnp.where(
                lane == 0,
                rolled(coef[4 + i, :, before], 1, 1),
                rolled(coef[4 + i, :, now], 1, 1),
            )
            link = coef[8 + i // 2, :, now]
            if i % 2 == 0:
                link = rolled(link, 4, 0)
            q_rows.append(jnp.where(sub < 4, shifted, link))
            p_rows.append(coef[i, :, now] + jnp.where(sub < 4, rolled(shifted, 4, 0), 0.0))
        film = coef[12, :, now]
        for k in range(2):
            p_rows[k] = p_rows[k] + jnp.where(sub < 2, rolled(film, -2 * k, 0), 0.0)
        v_rows = [rolled(film, -4 - 2 * k, 0) for k in range(2)]
        for i in range(4):
            inv = [
                -coef[10 + i // 2, 4 * (i % 2) + k : 4 * (i % 2) + k + 1, now] for k in range(4)
            ]
            for out, rows in ((pm, p_rows), (qm, q_rows), (vm, v_rows)):
                total = inv[0] * rows[0]
                for k in range(1, len(rows)):
                    total = total + inv[k] * rows[k]
                out[i, :, now] = total

    chunk = min(16, dirs)

    def evaluate(disp, t, finish):
        now = at_tile(t)
        before = at_tile(lax.rem(t + around - 1, around))
        after = at_tile(lax.rem(t + 1, around))
        wide_lane = iota((chunk, LANES), 1)
        target = coef[13, 0:1, now].astype(jnp.int32) + lane[0:1, :]
        inside = jnp.broadcast_to((target >= 0) & (target < LANES), (chunk, LANES))
        index = jnp.broadcast_to(target & (LANES - 1), (chunk, LANES))
        for r in range(0, dirs, chunk):
            rows = slice(r, r + chunk)
            speed = [vel[j, rows, now] for j in range(2)]
            acc = [None] * 4
            for j in range(4):
                here = disp[j, rows, now]
                left = disp[j, rows, before]
                right = disp[j, rows, after]
                previous = jnp.where(wide_lane == 0, rolled(left, 1, 1), rolled(here, 1, 1))
                following = jnp.where(
                    wide_lane == LANES - 1, rolled(right, -1, 1), rolled(here, -1, 1)
                )
                other = jnp.where(wide_lane < LANES // 2, right, left)
                linked = jnp.where(inside, lane_gather(here, index), lane_gather(other, index))
                for i in range(4):
                    total = pm[i, j : j + 1, now] * here
                    total = total + pm[i, 4 + j : 5 + j, now] * following
                    total = total + qm[i, j : j + 1, now] * previous
                    total = total + qm[i, 4 + j : 5 + j, now] * linked
                    if j < 2:
                        total = total + vm[i, j : j + 1, now] * speed[j]
                    acc[i] = total if acc[i] is None else acc[i] + total
            finish(rows, now, acc)

    def finish_first(rows, now, acc):
        for i in range(4):
            v = vel[i, rows, now]
            disp_b[i, rows, now] = (
                disp_a[i, rows, now] + STEP * v + (0.5 * STEP * STEP) * acc[i]
            )
            vel[i, rows, now] = v + (0.5 * STEP) * acc[i]

    def finish_second(rows, now, acc):
        for i in range(4):
            v = vel[i, rows, now] + (0.5 * STEP) * acc[i]
            disp_a[i, rows, now] = (
                disp_b[i, rows, now] + STEP * v + (0.5 * STEP * STEP) * acc[i]
            )
            vel[i, rows, now] = v + (0.5 * STEP) * acc[i]

    def finish_last(rows, now, acc):
        for i in range(4):
            vel_out[i, rows, now] = vel[i, rows, now] + (0.5 * STEP) * acc[i]

    def prepare_tile(t, carry):
        prepare(t)
        return carry

    def first_tile(t, carry):
        evaluate(disp_a, t, finish_first)
        return carry

    own_rows = pl.ds(pl.multiple_of(me_t * dirs, dirs), dirs)

    def tile_copy(peer, half):
        part = pl.ds(2 * half, 2)
        return pltpu.make_async_remote_copy(
            src_ref=disp_a.at[part, :, at_tile(peer)],
            dst_ref=x_all.at[part, own_rows, :],
            send_sem=a2a_send,
            recv_sem=a2a_recv.at[half],
            device_id=(me_p, peer),
            device_id_type=MESH,
        )

    def send_tile(t, halves):
        @pl.when(t != me_t)
        def _():
            for half in halves:
                tile_copy(t, half).start()

    def second_tile(t, carry):
        evaluate(disp_b, t, finish_second)
        return carry

    def second_and_send(t, carry):
        evaluate(disp_b, t, finish_second)
        send_tile(t, (0, 1))
        return carry

    lax.fori_loop(1, tiles, prepare_tile, 0)
    lax.fori_loop(1, tiles - 1, first_tile, 0)
    lax.fori_loop(2, tiles - 2, second_and_send, 0)

    for copy in halo:
        copy.wait_recv()
    right_end = jnp.where(me_p < ndof - 1, REACH, 0)
    left_start = jnp.where(me_p > 0, LANES - REACH, LANES)
    for n, pack in enumerate(packs):
        from_left, from_right = arrived[0, n], arrived[1, n]
        for s, (ref, c, rows) in enumerate(pack):
            piece = jnp.where(lane < right_end, rolled(from_right, -REACH * s, 1), 0.0)
            ref[c, rows, nodes : nodes + LANES] = jnp.where(
                lane >= left_start, rolled(from_left, LANES - REACH - REACH * s, 1), piece
            )

    def wrapped(k):
        return lax.rem(k, around)

    lax.fori_loop(tiles, tiles + 2, lambda k, c: prepare_tile(wrapped(k), c), 0)
    lax.fori_loop(tiles - 1, tiles + 2, lambda k, c: first_tile(wrapped(k), c), 0)

    def second_then_send(k, carry):
        t = lax.rem(tiles - 2 + k, tiles)
        evaluate(disp_b, t, finish_second)
        send_tile(t, (0,))
        return carry

    def send_rest(k, carry):
        send_tile(lax.rem(tiles - 2 + k, tiles), (1,))
        return carry

    lax.fori_loop(0, 4, second_then_send, 0)
    lax.fori_loop(0, 4, send_rest, 0)
    x_all[:, own_rows, :] = disp_a[:, :, at_tile(me_t)]
    evaluate(disp_b, tiles, finish_second)

    def last_tile(t, carry):
        evaluate(disp_a, t, finish_last)
        return carry

    lax.fori_loop(0, tiles, last_tile, 0)

    total = None
    for half in range(2):
        arrivals = x_all.at[pl.ds(2 * half, 2), pl.ds(0, (ndir - 1) * dirs), :]
        pltpu.make_async_copy(arrivals, arrivals, a2a_recv.at[half]).wait()
        pair = jnp.concatenate([x_all[2 * half], x_all[2 * half + 1]], axis=1)
        product = lax.dot_general(
            pair,
            pair,
            (((1,), (1,)), ((), ())),
            precision=HIGHEST,
            preferred_element_type=jnp.float32,
        )
        total = product if total is None else total + product
    half_n = gram.shape[1]
    gram_part[0] = total[0:half_n, 0:half_n]
    gram_part[1] = total[0:half_n, half_n:]
    gram_part[2] = total[half_n:, half_n:]

    def part_copy(by):
        to = at_x[by[0]], at_t[by[1]]
        member = to[1] * nx + to[0]
        return pltpu.make_async_remote_copy(
            src_ref=gram_part.at[:, pl.ds(member * share, share), :],
            dst_ref=slots.at[:, pl.ds(me * share, share), :],
            send_sem=rs_send,
            recv_sem=rs_recv,
            device_id=(me_z * nx + to[0], to[1]),
            device_id_type=MESH,
        )

    for by in plane:
        part_copy(by).start()
    mine = pl.ds(me * share, share)
    own = pltpu.make_async_copy(gram_part.at[:, mine, :], slots.at[:, mine, :], rs_recv)
    own.start()
    pltpu.make_async_copy(slots, slots, rs_recv).wait()
    total = slots[:, 0:SUB, :]
    for k in range(SUB, slots.shape[1], SUB):
        total = total + slots[:, k : k + SUB, :]
    for b in range(3):
        piece = total[b]
        for k in range(share, SUB, share):
            piece = piece + rolled(total[b], -k, 0)
        z_part[b] = piece

    def z_copy(by):
        return pltpu.make_async_remote_copy(
            src_ref=z_part.at[:, 0:share, :],
            dst_ref=z_slots.at[me_z, :, 0:share, :],
            send_sem=z_send,
            recv_sem=z_recv,
            device_id=(lax.rem(me_z + by, nz) * nx + me_x, me_t),
            device_id_type=MESH,
        )

    for by in line:
        z_copy(by).start()
    own = pltpu.make_async_copy(
        z_part.at[:, 0:share, :], z_slots.at[me_z, :, 0:share, :], z_recv
    )
    own.start()
    arrivals = z_slots.at[:, :, 0:share, :]
    pltpu.make_async_copy(arrivals, arrivals, z_recv).wait()
    total = z_slots[0, :, 0:share, :]
    for k in range(1, nz):
        total = total + z_slots[k, :, 0:share, :]
    z_sum[:, 0:share, :] = total

    def sum_copy(by):
        to = at_x[by[0]], at_t[by[1]]
        return pltpu.make_async_remote_copy(
            src_ref=z_sum.at[:, 0:share, :],
            dst_ref=gram.at[:, mine, :],
            send_sem=ag_send,
            recv_sem=ag_recv,
            device_id=(me_z * nx + to[0], to[1]),
            device_id_type=MESH,
        )

    for by in plane:
        sum_copy(by).start()
    own = pltpu.make_async_copy(z_sum.at[:, 0:share, :], gram.at[:, mine, :], ag_recv)
    own.start()
    pltpu.make_async_copy(gram, gram, ag_recv).wait()

    for copy in halo:
        copy.wait_send()
    for sent, sem in (
        (x_all.at[:, 0 : (ndir - 1) * dirs, :], a2a_send),
        (gram_part.at[:, 0 : len(plane) * share, :], rs_send),
        (z_slots.at[0 : len(line), :, 0:share, :], z_send),
        (gram_part.at[:, 0 : len(plane) * share, :], ag_send),
    ):
        pltpu.make_async_copy(sent, sent, sem).wait()


def newmark(ndof, nx, ndir, *args):
    dirs, nodes = args[0].shape[1:]
    around = nodes + LANES
    n = dirs * ndir
    packs = 2 * (dirs // SUB) + 4
    f32 = jnp.float32
    hbm = pl.BlockSpec(memory_space=pltpu.HBM)
    vmem = pl.BlockSpec(memory_space=pltpu.VMEM)
    dma = pltpu.SemaphoreType.DMA
    return pl.pallas_call(
        functools.partial(newmark_kernel, ndof, nx, ndir),
        out_shape=(
            pltpu.VMEM((4, dirs, nodes), f32),
            pltpu.VMEM((4, n, LANES), f32),
            pltpu.VMEM((3, n // 2, n // 2), f32),
        ),
        in_specs=[hbm] * 9,
        out_specs=[vmem] * 3,
        scratch_shapes=[
            pltpu.VMEM((4, dirs, around), f32),
            pltpu.VMEM((4, dirs, around), f32),
            pltpu.VMEM((4, dirs, around), f32),
            pltpu.VMEM((14, SUB, around), f32),
            pltpu.VMEM((4, 4, nodes), f32),
            pltpu.VMEM((4, 4, nodes), f32),
            pltpu.VMEM((nodes // LANES, LANES), jnp.int32),
            pltpu.VMEM((4, SUB, around), f32),
            pltpu.VMEM((4, SUB, around), f32),
            pltpu.VMEM((4, SUB, around), f32),
            pltpu.VMEM((2, packs, SUB, LANES), f32),
            pltpu.VMEM((2, packs, SUB, LANES), f32),
            pltpu.VMEM((3, n // 2, n // 2), f32),
            pltpu.VMEM((3, n // 2, n // 2), f32),
            pltpu.VMEM((3, SUB, n // 2), f32),
            pltpu.VMEM((ndof // nx, 3, SUB, n // 2), f32),
            pltpu.VMEM((3, SUB, n // 2), f32),
            pltpu.SMEM(args[6].shape, jnp.int32),
            pltpu.SMEM(args[7].shape, f32),
            pltpu.SMEM(args[8].shape, f32),
            dma((9,)),
            dma((2,)),
            dma((2,)),
            dma(()),
            dma((2,)),
            dma(()),
            dma(()),
            dma(()),
            dma(()),
            dma(()),
            dma(()),
        ],
        compiler_params=pltpu.CompilerParams(
            collective_id=0, has_side_effects=True, vmem_limit_bytes=32 * 2**20
        ),
        name="newmark_and_gram",
    )(*[pltpu.with_memory_space_constraint(x, pltpu.HBM) for x in args])


def spread(x, lane):
    return jnp.broadcast_to(x[:, lane : lane + 1], (x.shape[0], LANES))


def tiled(x, width):
    return x if width == LANES else jnp.concatenate([x] * (width // LANES), axis=1)


def eliminate(block, micro, near):
    size, width = block.shape
    row = iota((micro, LANES), 0)
    rows = [block[i : i + SUB] for i in range(0, size, SUB)]
    done = []
    for s in range(0, size, micro):
        top = jnp.concatenate(rows[: micro // SUB], axis=0)
        rest = rows[micro // SUB :]
        column = [spread(top, s + j) for j in range(micro)]
        inverse = []
        pivots = jnp.broadcast_to(column[0][0:1], (micro, LANES))
        for j in range(micro):
            pivot = column[j][j : j + 1]
            inverse.append(1.0 / pivot)
            pivots = jnp.where(row == j, pivot, pivots)
            if j == micro - 1:
                break
            factor = jnp.where(row > j, column[j] * inverse[j], 0.0)
            for m in range(j + 1, micro):
                column[m] = column[m] - factor * column[m][j : j + 1]
            top = top - tiled(factor, width) * top[j : j + 1]
        rows = []
        for part in rest[:near]:
            own = [spread(part, s + j) for j in range(micro)]
            for j in range(micro):
                factor = own[j] * inverse[j]
                for m in range(j + 1, micro):
                    own[m] = own[m] - factor * column[m][j : j + 1]
                part = part - tiled(factor, width) * top[j : j + 1]
            rows.append(part)
        top = top * tiled(lax.rsqrt(pivots), width)
        if len(rest) > near:
            update = lax.dot_general(
                top[:, 0:size],
                top,
                (((0,), (0,)), ((), ())),
                precision=HIGHEST,
                preferred_element_type=jnp.float32,
            )
            for i in range(near, len(rest)):
                start = s + micro + SUB * i
                rows.append(rest[i] - update[start : start + SUB])
        done.append(top)
    return jnp.concatenate(done, axis=0)


def factor_kernel(
    scale, micro, near, gram, x, vel, q_out, r_out, vel_out, q, r, work, sems
):
    size = gram.shape[1]
    n = 2 * size
    vel_store = pltpu.make_async_copy(vel, vel_out, sems.at[0])
    vel_store.start()
    x_loads = [
        pltpu.make_async_copy(
            x.at[c], work.at[:, n + LANES * c : n + LANES * (c + 1)], sems.at[1 + c]
        )
        for c in range(4)
    ]
    for copy in x_loads:
        copy.start()
    stores = []
    row, col = iota((size, size), 0), iota((size, size), 1)
    identity = (row == col).astype(jnp.float32)
    r[size:, 0:size] = jnp.zeros((size, size), jnp.float32)
    work[0:size, size:n] = gram[1] * scale
    for low in range(0, n, size):
        high = low + size
        block = gram[0] * scale if low == 0 else work[low:high, low:high]
        block = eliminate(jnp.concatenate([block, identity], axis=1), micro, near)
        if low == 0:
            for copy in x_loads:
                copy.wait()
        later = jnp.dot(
            block[:, size:],
            work[low:high, high:],
            precision=HIGHEST,
            preferred_element_type=jnp.float32,
        )
        r[low:high, low:high] = jnp.where(row <= col, block[:, 0:size], 0.0)
        if low == 0:
            r[low:high, high:n] = later[:, 0:size]
            work[high:, high:n] = gram[2] * scale
            work[high:, high:] = work[high:, high:] - lax.dot_general(
                later[:, 0:size],
                later,
                (((0,), (0,)), ((), ())),
                precision=HIGHEST,
                preferred_element_type=jnp.float32,
            )
        for c in range(4):
            start = n - high + LANES * c
            q[c, low:high, :] = later[:, start : start + LANES]
        part = pl.ds(low, size)
        stores += [
            pltpu.make_async_copy(q.at[:, part, :], q_out.at[:, part, :], sems.at[5 + low // size]),
            pltpu.make_async_copy(r.at[part, :], r_out.at[part, :], sems.at[7 + low // size]),
        ]
        for copy in stores[-2:]:
            copy.start()
    for copy in stores:
        copy.wait()
    vel_store.wait()


def factor(gram, x, vel, scale):
    n = x.shape[1]
    vmem = pl.BlockSpec(memory_space=pltpu.VMEM)
    hbm = pl.BlockSpec(memory_space=pltpu.HBM)
    return pl.pallas_call(
        functools.partial(factor_kernel, scale, 2 * SUB, 2),
        out_shape=(
            pltpu.HBM(x.shape, jnp.float32),
            pltpu.HBM((n, n), jnp.float32),
            pltpu.HBM(vel.shape, jnp.float32),
        ),
        in_specs=[vmem, vmem, vmem],
        out_specs=[hbm, hbm, hbm],
        scratch_shapes=[
            pltpu.VMEM(x.shape, jnp.float32),
            pltpu.VMEM((n, n), jnp.float32),
            pltpu.VMEM((n, n + 4 * LANES), jnp.float32),
            pltpu.SemaphoreType.DMA((9,)),
        ],
        compiler_params=pltpu.CompilerParams(vmem_limit_bytes=32 * 2**20),
        name="factor_and_solve",
    )(*[pltpu.with_memory_space_constraint(y, pltpu.VMEM) for y in (gram, x, vel)])


def on_device(ndof, ndir, disp, veloc, elem, link, inv, offset, damper_at, damper_k, damper_c):
    nodes = disp.shape[2]
    offset = offset.reshape(nodes // LANES, LANES)
    nx = CHIPS_X if ndof % CHIPS_X == 0 else 1
    veloc, x, gram = newmark(
        ndof, nx, ndir, disp, veloc, elem, link, inv, offset, damper_at, damper_k, damper_c
    )
    q_block, r_factor, veloc = factor(gram, x, veloc, 1.0 / (4.0 * nodes * ndof))
    return veloc, q_block, r_factor


def solution(mesh):
    in_specs = (
        P(None, "dir", "dof"),
        P(None, "dir", "dof"),
        P(None, None, "dof"),
        P(None, None, "dof"),
        P(None, None, "dof"),
        P("dof"),
        P("dof"),
        P(None, None, "dof"),
        P(None, None, "dof"),
    )
    out_specs = (P(None, "dir", "dof"), P(None, None, ("dof", "dir")), P())
    return jax.shard_map(
        functools.partial(on_device, mesh.shape["dof"], mesh.shape["dir"]),
        mesh=mesh,
        in_specs=in_specs,
        out_specs=out_specs,
        check_vma=False,
    )
```

```python
import functools

import jax
import jax.numpy as jnp
from jax import lax
from jax.experimental import pallas as pl
from jax.experimental.pallas import tpu as pltpu
from jax.sharding import PartitionSpec as P

STEP = 0.5
LANES = 128
SUB = 8
REACH = 32
CHIPS_X = 4
MESH = pl.DeviceIdType.MESH
HIGHEST = lax.Precision.HIGHEST


def iota(shape, axis):
    return lax.broadcasted_iota(jnp.int32, shape, axis)


def rolled(x, by, axis):
    by = by % x.shape[axis]
    return pltpu.roll(x, by, axis) if by else x


def lane_gather(x, index):
    return jnp.take_along_axis(x, index, axis=1, mode="promise_in_bounds")


def far_first(offsets, sizes):
    def distance(offset):
        return sum(min(o, n - o) for o, n in zip(offset, sizes))

    return [o for o in sorted(offsets, key=distance, reverse=True) if distance(o)]


def newmark_kernel(
    ndof,
    nx,
    ndir,
    disp_in,
    vel_in,
    elem_in,
    link_in,
    inv_in,
    offset_in,
    damper_at_in,
    damper_k_in,
    damper_c_in,
    vel_out,
    x_all,
    gram,
    disp_a,
    disp_b,
    vel,
    coef,
    link_raw,
    inv_raw,
    offset_raw,
    pm,
    qm,
    vm,
    to_send,
    arrived,
    gram_part,
    slots,
    z_part,
    z_slots,
    z_sum,
    damper_at,
    damper_k,
    damper_c,
    load_sem,
    halo_send,
    halo_recv,
    a2a_send,
    a2a_recv,
    rs_send,
    rs_recv,
    z_send,
    z_recv,
    ag_send,
    ag_recv,
):
    me_p = lax.axis_index("dof")
    me_t = lax.axis_index("dir")
    dirs = disp_in.shape[1]
    nodes = disp_in.shape[2]
    tiles = nodes // LANES
    around = tiles + 1
    nz = ndof // nx
    me_z, me_x = me_p // nx, lax.rem(me_p, nx)
    me = me_t * nx + me_x
    share = gram.shape[1] // (nx * ndir)
    plane = far_first([(x, t) for x in range(nx) for t in range(ndir)], (nx, ndir))
    line = [by for by, in far_first([(z,) for z in range(nz)], (nz,))]

    at_x = [lax.rem(me_x + by, nx) for by in range(nx)]
    at_t = [lax.rem(me_t + by, ndir) for by in range(ndir)]
    barrier = pltpu.get_barrier_semaphore()

    def greet(p, t):
        pl.semaphore_signal(barrier, inc=1, device_id=(p, t), device_id_type=MESH)

    for by in (1, ndof - 1):
        greet(lax.rem(me_p + by, ndof), me_t)
    loads = [
        (disp_in, disp_a.at[:, :, 0:nodes]),
        (vel_in, vel.at[:, :, 0:nodes]),
        (elem_in, coef.at[0:8, :, 0:nodes]),
        (link_in, link_raw),
        (inv_in, inv_raw),
        (offset_in, offset_raw),
        (damper_at_in, damper_at),
        (damper_k_in, damper_k),
        (damper_c_in, damper_c),
    ]
    loads = [pltpu.make_async_copy(s, d, load_sem.at[i]) for i, (s, d) in enumerate(loads)]
    for copy in loads:
        copy.start()

    for by, in far_first([(t,) for t in range(ndir)], (ndir,)):
        greet(me_p, lax.rem(me_t + by, ndir))
    for by in line:
        greet(lax.rem(me_z + by, nz) * nx + me_x, me_t)
    for by in range(1, nx):
        greet(me_z * nx + lax.rem(me_x + by, nx), me_t)

    lane = iota((SUB, LANES), 1)
    sub = iota((SUB, LANES), 0)

    def at_tile(t):
        return pl.ds(pl.multiple_of(t * LANES, LANES), LANES)

    for copy in loads[2:]:
        copy.wait()
    columns = []
    for q in range(2):
        column = jnp.zeros((SUB, LANES), jnp.float32)
        for kind, table in enumerate((damper_k, damper_c)):
            for i in range(2):
                for j in range(2):
                    column = jnp.where(sub == 4 * kind + 2 * i + j, table[i, j, q], column)
        columns.append(column)
    for t in range(tiles):
        where = slice(t * LANES, (t + 1) * LANES)
        dense = jnp.zeros((SUB, LANES), jnp.float32)
        for q in range(2):
            place = damper_at[q] - me_p * nodes - t * LANES
            dense = dense + jnp.where(lane == place, columns[q], 0.0)
        coef[12, :, where] = dense
        row = offset_raw[t : t + 1, :].astype(jnp.float32)
        coef[13, :, where] = jnp.broadcast_to(row, (SUB, LANES))
    for half in range(2):
        coef[8 + half, 0:4, 0:nodes] = link_raw[2 * half]
        coef[8 + half, 4:8, 0:nodes] = link_raw[2 * half + 1]
        coef[10 + half, 0:4, 0:nodes] = inv_raw[2 * half]
        coef[10 + half, 4:8, 0:nodes] = inv_raw[2 * half + 1]
    for copy in loads[:2]:
        copy.wait()

    groups = dirs // SUB
    packs = []
    for ref in (disp_a, vel):
        for g in range(groups):
            packs.append([(ref, c, slice(g * SUB, (g + 1) * SUB)) for c in range(4)])
    for g in range(0, 14, 4):
        packs.append([(coef, k, slice(0, SUB)) for k in range(g, min(g + 4, 14))])
    for side, start, first in ((0, nodes - LANES, LANES - REACH), (1, 0, 0)):
        for n, pack in enumerate(packs):
            held = None
            for s, (ref, c, rows) in enumerate(pack):
                piece = rolled(ref[c, rows, start : start + LANES], REACH * s - first, 1)
                held = piece if held is None else jnp.where(lane >= REACH * s, piece, held)
            to_send[side, n] = held

    pl.semaphore_wait(barrier, 2 + ndir - 1 + nz - 1 + nx - 1)
    halo = []
    for side, by in ((0, 1), (1, ndof - 1)):
        halo.append(
            pltpu.make_async_remote_copy(
                src_ref=to_send.at[side],
                dst_ref=arrived.at[side],
                send_sem=halo_send.at[side],
                recv_sem=halo_recv.at[side],
                device_id=(lax.rem(me_p + by, ndof), me_t),
                device_id_type=MESH,
            )
        )
        halo[-1].start()

    def prepare(t):
        now = at_tile(t)
        before = at_tile(lax.rem(t + around - 1, around))
        p_rows, q_rows = [], []
        for i in range(4):
            shifted = jnp.where(
                lane == 0,
                rolled(coef[4 + i, :, before], 1, 1),
                rolled(coef[4 + i, :, now], 1, 1),
            )
            link = coef[8 + i // 2, :, now]
            if i % 2 == 0:
                link = rolled(link, 4, 0)
            q_rows.append(jnp.where(sub < 4, shifted, link))
            p_rows.append(coef[i, :, now] + jnp.where(sub < 4, rolled(shifted, 4, 0), 0.0))
        film = coef[12, :, now]
        for k in range(2):
            p_rows[k] = p_rows[k] + jnp.where(sub < 2, rolled(film, -2 * k, 0), 0.0)
        v_rows = [rolled(film, -4 - 2 * k, 0) for k in range(2)]
        for i in range(4):
            inv = [
                -coef[10 + i // 2, 4 * (i % 2) + k : 4 * (i % 2) + k + 1, now] for k in range(4)
            ]
            for out, rows in ((pm, p_rows), (qm, q_rows), (vm, v_rows)):
                total = inv[0] * rows[0]
                for k in range(1, len(rows)):
                    total = total + inv[k] * rows[k]
                out[i, :, now] = total

    chunk = min(16, dirs)

    def evaluate(disp, t, finish):
        now = at_tile(t)
        before = at_tile(lax.rem(t + around - 1, around))
        after = at_tile(lax.rem(t + 1, around))
        wide_lane = iota((chunk, LANES), 1)
        target = coef[13, 0:1, now].astype(jnp.int32) + lane[0:1, :]
        inside = jnp.broadcast_to((target >= 0) & (target < LANES), (chunk, LANES))
        index = jnp.broadcast_to(target & (LANES - 1), (chunk, LANES))
        for r in range(0, dirs, chunk):
            rows = slice(r, r + chunk)
            speed = [vel[j, rows, now] for j in range(2)]
            acc = [None] * 4
            for j in range(4):
                here = disp[j, rows, now]
                left = disp[j, rows, before]
                right = disp[j, rows, after]
                previous = jnp.where(wide_lane == 0, rolled(left, 1, 1), rolled(here, 1, 1))
                following = jnp.where(
                    wide_lane == LANES - 1, rolled(right, -1, 1), rolled(here, -1, 1)
                )
                other = jnp.where(wide_lane < LANES // 2, right, left)
                linked = jnp.where(inside, lane_gather(here, index), lane_gather(other, index))
                for i in range(4):
                    total = pm[i, j : j + 1, now] * here
                    total = total + pm[i, 4 + j : 5 + j, now] * following
                    total = total + qm[i, j : j + 1, now] * previous
                    total = total + qm[i, 4 + j : 5 + j, now] * linked
                    if j < 2:
                        total = total + vm[i, j : j + 1, now] * speed[j]
                    acc[i] = total if acc[i] is None else acc[i] + total
            finish(rows, now, acc)

    def finish_first(rows, now, acc):
        for i in range(4):
            v = vel[i, rows, now]
            disp_b[i, rows, now] = (
                disp_a[i, rows, now] + STEP * v + (0.5 * STEP * STEP) * acc[i]
            )
            vel[i, rows, now] = v + (0.5 * STEP) * acc[i]

    def finish_second(rows, now, acc):
        for i in range(4):
            v = vel[i, rows, now] + (0.5 * STEP) * acc[i]
            disp_a[i, rows, now] = (
                disp_b[i, rows, now] + STEP * v + (0.5 * STEP * STEP) * acc[i]
            )
            vel[i, rows, now] = v + (0.5 * STEP) * acc[i]

    def finish_last(rows, now, acc):
        for i in range(4):
            vel_out[i, rows, now] = vel[i, rows, now] + (0.5 * STEP) * acc[i]

    def prepare_tile(t, carry):
        prepare(t)
        return carry

    def first_tile(t, carry):
        evaluate(disp_a, t, finish_first)
        return carry

    own_rows = pl.ds(pl.multiple_of(me_t * dirs, dirs), dirs)

    def tile_copy(peer, half):
        part = pl.ds(2 * half, 2)
        return pltpu.make_async_remote_copy(
            src_ref=disp_a.at[part, :, at_tile(peer)],
            dst_ref=x_all.at[part, own_rows, :],
            send_sem=a2a_send,
            recv_sem=a2a_recv.at[half],
            device_id=(me_p, peer),
            device_id_type=MESH,
        )

    def send_tile(t, halves):
        @pl.when(t != me_t)
        def _():
            for half in halves:
                tile_copy(t, half).start()

    def second_tile(t, carry):
        evaluate(disp_b, t, finish_second)
        return carry

    def second_and_send(t, carry):
        evaluate(disp_b, t, finish_second)
        send_tile(t, (0, 1))
        return carry

    lax.fori_loop(1, tiles, prepare_tile, 0)
    lax.fori_loop(1, tiles - 1, first_tile, 0)
    lax.fori_loop(2, tiles - 2, second_and_send, 0)

    for copy in halo:
        copy.wait_recv()
    right_end = jnp.where(me_p < ndof - 1, REACH, 0)
    left_start = jnp.where(me_p > 0, LANES - REACH, LANES)
    for n, pack in enumerate(packs):
        from_left, from_right = arrived[0, n], arrived[1, n]
        for s, (ref, c, rows) in enumerate(pack):
            piece = jnp.where(lane < right_end, rolled(from_right, -REACH * s, 1), 0.0)
            ref[c, rows, nodes : nodes + LANES] = jnp.where(
                lane >= left_start, rolled(from_left, LANES - REACH - REACH * s, 1), piece
            )

    def wrapped(k):
        return lax.rem(k, around)

    lax.fori_loop(tiles, tiles + 2, lambda k, c: prepare_tile(wrapped(k), c), 0)

    def inner_end(k, carry):
        evaluate(disp_a, lax.rem(tiles - 1 + k, tiles), finish_first)
        return second_and_send(lax.rem(tiles - 2 + 3 * k, tiles), carry)

    def outer_end(k, carry):
        t = lax.rem(tiles - 1 + k, tiles)
        evaluate(disp_b, t, finish_second)
        send_tile(t, (0,))
        return carry

    def send_rest(k, carry):
        send_tile(lax.rem(tiles - 1 + k, tiles), (1,))
        return carry

    lax.fori_loop(0, 2, inner_end, 0)
    lax.fori_loop(tiles, tiles + 1, first_tile, 0)
    lax.fori_loop(0, 2, outer_end, 0)
    lax.fori_loop(0, 2, send_rest, 0)
    x_all[:, own_rows, :] = disp_a[:, :, at_tile(me_t)]
    evaluate(disp_b, tiles, finish_second)

    def last_tile(t, carry):
        evaluate(disp_a, t, finish_last)
        return carry

    lax.fori_loop(0, tiles, last_tile, 0)

    total = None
    for half in range(2):
        arrivals = x_all.at[pl.ds(2 * half, 2), pl.ds(0, (ndir - 1) * dirs), :]
        pltpu.make_async_copy(arrivals, arrivals, a2a_recv.at[half]).wait()
        pair = jnp.concatenate([x_all[2 * half], x_all[2 * half + 1]], axis=1)
        product = lax.dot_general(
            pair,
            pair,
            (((1,), (1,)), ((), ())),
            precision=HIGHEST,
            preferred_element_type=jnp.float32,
        )
        total = product if total is None else total + product
    half_n = gram.shape[1]
    gram_part[0] = total[0:half_n, 0:half_n]
    gram_part[1] = total[0:half_n, half_n:]
    gram_part[2] = total[half_n:, half_n:]

    def part_copy(by):
        to = at_x[by[0]], at_t[by[1]]
        member = to[1] * nx + to[0]
        return pltpu.make_async_remote_copy(
            src_ref=gram_part.at[:, pl.ds(member * share, share), :],
            dst_ref=slots.at[:, pl.ds(me * share, share), :],
            send_sem=rs_send,
            recv_sem=rs_recv,
            device_id=(me_z * nx + to[0], to[1]),
            device_id_type=MESH,
        )

    for by in plane:
        part_copy(by).start()
    mine = pl.ds(me * share, share)
    own = pltpu.make_async_copy(gram_part.at[:, mine, :], slots.at[:, mine, :], rs_recv)
    own.start()
    pltpu.make_async_copy(slots, slots, rs_recv).wait()
    total = slots[:, 0:SUB, :]
    for k in range(SUB, slots.shape[1], SUB):
        total = total + slots[:, k : k + SUB, :]
    for b in range(3):
        piece = total[b]
        for k in range(share, SUB, share):
            piece = piece + rolled(total[b], -k, 0)
        z_part[b] = piece

    def z_copy(by):
        return pltpu.make_async_remote_copy(
            src_ref=z_part.at[:, 0:share, :],
            dst_ref=z_slots.at[me_z, :, 0:share, :],
            send_sem=z_send,
            recv_sem=z_recv,
            device_id=(lax.rem(me_z + by, nz) * nx + me_x, me_t),
            device_id_type=MESH,
        )

    for by in line:
        z_copy(by).start()
    own = pltpu.make_async_copy(
        z_part.at[:, 0:share, :], z_slots.at[me_z, :, 0:share, :], z_recv
    )
    own.start()
    arrivals = z_slots.at[:, :, 0:share, :]
    pltpu.make_async_copy(arrivals, arrivals, z_recv).wait()
    total = z_slots[0, :, 0:share, :]
    for k in range(1, nz):
        total = total + z_slots[k, :, 0:share, :]
    z_sum[:, 0:share, :] = total

    def sum_copy(by):
        to = at_x[by[0]], at_t[by[1]]
        return pltpu.make_async_remote_copy(
            src_ref=z_sum.at[:, 0:share, :],
            dst_ref=gram.at[:, mine, :],
            send_sem=ag_send,
            recv_sem=ag_recv,
            device_id=(me_z * nx + to[0], to[1]),
            device_id_type=MESH,
        )

    for by in plane:
        sum_copy(by).start()
    own = pltpu.make_async_copy(z_sum.at[:, 0:share, :], gram.at[:, mine, :], ag_recv)
    own.start()
    pltpu.make_async_copy(gram, gram, ag_recv).wait()

    for copy in halo:
        copy.wait_send()
    for sent, sem in (
        (x_all.at[:, 0 : (ndir - 1) * dirs, :], a2a_send),
        (gram_part.at[:, 0 : len(plane) * share, :], rs_send),
        (z_slots.at[0 : len(line), :, 0:share, :], z_send),
        (gram_part.at[:, 0 : len(plane) * share, :], ag_send),
    ):
        pltpu.make_async_copy(sent, sent, sem).wait()


def newmark(ndof, nx, ndir, *args):
    dirs, nodes = args[0].shape[1:]
    around = nodes + LANES
    n = dirs * ndir
    packs = 2 * (dirs // SUB) + 4
    f32 = jnp.float32
    hbm = pl.BlockSpec(memory_space=pltpu.HBM)
    vmem = pl.BlockSpec(memory_space=pltpu.VMEM)
    dma = pltpu.SemaphoreType.DMA
    return pl.pallas_call(
        functools.partial(newmark_kernel, ndof, nx, ndir),
        out_shape=(
            pltpu.VMEM((4, dirs, nodes), f32),
            pltpu.VMEM((4, n, LANES), f32),
            pltpu.VMEM((3, n // 2, n // 2), f32),
        ),
        in_specs=[hbm] * 9,
        out_specs=[vmem] * 3,
        scratch_shapes=[
            pltpu.VMEM((4, dirs, around), f32),
            pltpu.VMEM((4, dirs, around), f32),
            pltpu.VMEM((4, dirs, around), f32),
            pltpu.VMEM((14, SUB, around), f32),
            pltpu.VMEM((4, 4, nodes), f32),
            pltpu.VMEM((4, 4, nodes), f32),
            pltpu.VMEM((nodes // LANES, LANES), jnp.int32),
            pltpu.VMEM((4, SUB, around), f32),
            pltpu.VMEM((4, SUB, around), f32),
            pltpu.VMEM((4, SUB, around), f32),
            pltpu.VMEM((2, packs, SUB, LANES), f32),
            pltpu.VMEM((2, packs, SUB, LANES), f32),
            pltpu.VMEM((3, n // 2, n // 2), f32),
            pltpu.VMEM((3, n // 2, n // 2), f32),
            pltpu.VMEM((3, SUB, n // 2), f32),
            pltpu.VMEM((ndof // nx, 3, SUB, n // 2), f32),
            pltpu.VMEM((3, SUB, n // 2), f32),
            pltpu.SMEM(args[6].shape, jnp.int32),
            pltpu.SMEM(args[7].shape, f32),
            pltpu.SMEM(args[8].shape, f32),
            dma((9,)),
            dma((2,)),
            dma((2,)),
            dma(()),
            dma((2,)),
            dma(()),
            dma(()),
            dma(()),
            dma(()),
            dma(()),
            dma(()),
        ],
        compiler_params=pltpu.CompilerParams(
            collective_id=0, has_side_effects=True, vmem_limit_bytes=32 * 2**20
        ),
        name="newmark_and_gram",
    )(*[pltpu.with_memory_space_constraint(x, pltpu.HBM) for x in args])


def spread(x, lane):
    return jnp.broadcast_to(x[:, lane : lane + 1], (x.shape[0], LANES))


def tiled(x, width):
    return x if width == LANES else jnp.concatenate([x] * (width // LANES), axis=1)


def eliminate(block, micro, near):
    size, width = block.shape
    sub = iota((SUB, LANES), 0)
    groups = micro // SUB
    rows = [block[i : i + SUB] for i in range(0, size, SUB)]
    done = []
    for s in range(0, size, micro):
        top = rows[:groups]
        rest = rows[groups:]
        column = [
            [spread(top[g], s + j) if g >= j // SUB else None for g in range(groups)]
            for j in range(micro)
        ]

        def entry(j, m):
            return column[j][m // SUB][m % SUB : m % SUB + 1]

        inverse = []
        pivots = [None] * groups
        for j in range(micro):
            group, at = j // SUB, j % SUB
            pivot = entry(j, j)
            inverse.append(1.0 / pivot)
            held = jnp.broadcast_to(pivot, (SUB, LANES))
            pivots[group] = held if at == 0 else jnp.where(sub == at, held, pivots[group])
            source = top[group][at : at + 1]
            for g in range(group, groups):
                if g == group and at == SUB - 1:
                    continue
                factor = column[j][g] * inverse[j]
                if g == group:
                    factor = jnp.where(sub > at, factor, 0.0)
                for m in range(j + 1, min(micro, (g + 1) * SUB)):
                    column[m][g] = column[m][g] - factor * entry(j, m)
                top[g] = top[g] - tiled(factor, width) * source
        rows = []
        for part in rest[:near]:
            own = [spread(part, s + j) for j in range(micro)]
            for j in range(micro):
                factor = own[j] * inverse[j]
                for m in range(j + 1, micro):
                    own[m] = own[m] - factor * entry(j, m)
                part = part - tiled(factor, width) * top[j // SUB][j % SUB : j % SUB + 1]
            rows.append(part)
        top = jnp.concatenate(
            [t * tiled(lax.rsqrt(p), width) for t, p in zip(top, pivots)], axis=0
        )
        if len(rest) > near:
            update = lax.dot_general(
                top[:, 0:size],
                top,
                (((0,), (0,)), ((), ())),
                precision=HIGHEST,
                preferred_element_type=jnp.float32,
            )
            for i in range(near, len(rest)):
                start = s + micro + SUB * i
                rows.append(rest[i] - update[start : start + SUB])
        done.append(top)
    return jnp.concatenate(done, axis=0)


def factor_kernel(
    scale, micro, near, gram, x, vel, q_out, r_out, vel_out, q, r, work, sems
):
    size = gram.shape[1]
    n = 2 * size
    vel_store = pltpu.make_async_copy(vel, vel_out, sems.at[0])
    vel_store.start()
    x_loads = [
        pltpu.make_async_copy(
            x.at[c], work.at[:, n + LANES * c : n + LANES * (c + 1)], sems.at[1 + c]
        )
        for c in range(4)
    ]
    for copy in x_loads:
        copy.start()
    stores = []
    row, col = iota((size, size), 0), iota((size, size), 1)
    identity = (row == col).astype(jnp.float32)
    r[size:, 0:size] = jnp.zeros((size, size), jnp.float32)
    work[0:size, size:n] = gram[1] * scale
    for low in range(0, n, size):
        high = low + size
        block = gram[0] * scale if low == 0 else work[low:high, low:high]
        block = eliminate(jnp.concatenate([block, identity], axis=1), micro, near)
        if low == 0:
            for copy in x_loads:
                copy.wait()
        later = jnp.dot(
            block[:, size:],
            work[low:high, high:],
            precision=HIGHEST,
            preferred_element_type=jnp.float32,
        )
        r[low:high, low:high] = jnp.where(row <= col, block[:, 0:size], 0.0)
        if low == 0:
            r[low:high, high:n] = later[:, 0:size]
            work[high:, high:n] = gram[2] * scale
            work[high:, high:] = work[high:, high:] - lax.dot_general(
                later[:, 0:size],
                later,
                (((0,), (0,)), ((), ())),
                precision=HIGHEST,
                preferred_element_type=jnp.float32,
            )
        for c in range(4):
            start = n - high + LANES * c
            q[c, low:high, :] = later[:, start : start + LANES]
        part = pl.ds(low, size)
        stores += [
            pltpu.make_async_copy(q.at[:, part, :], q_out.at[:, part, :], sems.at[5 + low // size]),
            pltpu.make_async_copy(r.at[part, :], r_out.at[part, :], sems.at[7 + low // size]),
        ]
        for copy in stores[-2:]:
            copy.start()
    for copy in stores:
        copy.wait()
    vel_store.wait()


def factor(gram, x, vel, scale):
    n = x.shape[1]
    vmem = pl.BlockSpec(memory_space=pltpu.VMEM)
    hbm = pl.BlockSpec(memory_space=pltpu.HBM)
    return pl.pallas_call(
        functools.partial(factor_kernel, scale, 2 * SUB, 2),
        out_shape=(
            pltpu.HBM(x.shape, jnp.float32),
            pltpu.HBM((n, n), jnp.float32),
            pltpu.HBM(vel.shape, jnp.float32),
        ),
        in_specs=[vmem, vmem, vmem],
        out_specs=[hbm, hbm, hbm],
        scratch_shapes=[
            pltpu.VMEM(x.shape, jnp.float32),
            pltpu.VMEM((n, n), jnp.float32),
            pltpu.VMEM((n, n + 4 * LANES), jnp.float32),
            pltpu.SemaphoreType.DMA((9,)),
        ],
        compiler_params=pltpu.CompilerParams(vmem_limit_bytes=32 * 2**20),
        name="factor_and_solve",
    )(*[pltpu.with_memory_space_constraint(y, pltpu.VMEM) for y in (gram, x, vel)])


def on_device(ndof, ndir, disp, veloc, elem, link, inv, offset, damper_at, damper_k, damper_c):
    nodes = disp.shape[2]
    offset = offset.reshape(nodes // LANES, LANES)
    nx = CHIPS_X if ndof % CHIPS_X == 0 else 1
    veloc, x, gram = newmark(
        ndof, nx, ndir, disp, veloc, elem, link, inv, offset, damper_at, damper_k, damper_c
    )
    q_block, r_factor, veloc = factor(gram, x, veloc, 1.0 / (4.0 * nodes * ndof))
    return veloc, q_block, r_factor


def solution(mesh):
    in_specs = (
        P(None, "dir", "dof"),
        P(None, "dir", "dof"),
        P(None, None, "dof"),
        P(None, None, "dof"),
        P(None, None, "dof"),
        P("dof"),
        P("dof"),
        P(None, None, "dof"),
        P(None, None, "dof"),
    )
    out_specs = (P(None, "dir", "dof"), P(None, None, ("dof", "dir")), P())
    return jax.shard_map(
        functools.partial(on_device, mesh.shape["dof"], mesh.shape["dir"]),
        mesh=mesh,
        in_specs=in_specs,
        out_specs=out_specs,
        check_vma=False,
    )
```

```python
import functools

import jax
import jax.numpy as jnp
from jax import lax
from jax.experimental import pallas as pl
from jax.experimental.pallas import tpu as pltpu
from jax.sharding import PartitionSpec as P

STEP = 0.5
LANES = 128
SUB = 8
REACH = 32
CHIPS_X = 4
MESH = pl.DeviceIdType.MESH
HIGHEST = lax.Precision.HIGHEST


def iota(shape, axis):
    return lax.broadcasted_iota(jnp.int32, shape, axis)


def rolled(x, by, axis):
    by = by % x.shape[axis]
    return pltpu.roll(x, by, axis) if by else x


def lane_gather(x, index):
    return jnp.take_along_axis(x, index, axis=1, mode="promise_in_bounds")


def far_first(offsets, sizes):
    def distance(offset):
        return sum(min(o, n - o) for o, n in zip(offset, sizes))

    return [o for o in sorted(offsets, key=distance, reverse=True) if distance(o)]


def newmark_kernel(
    ndof,
    nx,
    ndir,
    disp_in,
    vel_in,
    elem_in,
    link_in,
    inv_in,
    offset_in,
    damper_at_in,
    damper_k_in,
    damper_c_in,
    vel_out,
    x_all,
    gram,
    disp_a,
    disp_b,
    vel,
    coef,
    link_raw,
    inv_raw,
    offset_raw,
    pm,
    qm,
    vm,
    to_send,
    arrived,
    gram_part,
    slots,
    z_part,
    z_slots,
    z_sum,
    damper_at,
    damper_k,
    damper_c,
    load_sem,
    halo_send,
    halo_recv,
    a2a_send,
    a2a_recv,
    rs_send,
    rs_recv,
    z_send,
    z_recv,
    ag_send,
    ag_recv,
):
    me_p = lax.axis_index("dof")
    me_t = lax.axis_index("dir")
    dirs = disp_in.shape[1]
    nodes = disp_in.shape[2]
    tiles = nodes // LANES
    around = tiles + 1
    nz = ndof // nx
    me_z, me_x = me_p // nx, lax.rem(me_p, nx)
    me = me_t * nx + me_x
    share = gram.shape[1] // (nx * ndir)
    plane = far_first([(x, t) for x in range(nx) for t in range(ndir)], (nx, ndir))
    line = [by for by, in far_first([(z,) for z in range(nz)], (nz,))]

    at_x = [lax.rem(me_x + by, nx) for by in range(nx)]
    at_t = [lax.rem(me_t + by, ndir) for by in range(ndir)]
    barrier = pltpu.get_barrier_semaphore()

    def greet(p, t):
        pl.semaphore_signal(barrier, inc=1, device_id=(p, t), device_id_type=MESH)

    for by in (1, ndof - 1):
        greet(lax.rem(me_p + by, ndof), me_t)
    loads = [
        (disp_in, disp_a.at[:, :, 0:nodes]),
        (vel_in, vel.at[:, :, 0:nodes]),
        (elem_in, coef.at[0:8, :, 0:nodes]),
        (link_in, link_raw),
        (inv_in, inv_raw),
        (offset_in, offset_raw),
        (damper_at_in, damper_at),
        (damper_k_in, damper_k),
        (damper_c_in, damper_c),
    ]
    loads = [pltpu.make_async_copy(s, d, load_sem.at[i]) for i, (s, d) in enumerate(loads)]
    for copy in loads:
        copy.start()

    for by, in far_first([(t,) for t in range(ndir)], (ndir,)):
        greet(me_p, lax.rem(me_t + by, ndir))
    for by in line:
        greet(lax.rem(me_z + by, nz) * nx + me_x, me_t)
    for by in range(1, nx):
        greet(me_z * nx + lax.rem(me_x + by, nx), me_t)

    lane = iota((SUB, LANES), 1)
    sub = iota((SUB, LANES), 0)

    def at_tile(t):
        return pl.ds(pl.multiple_of(t * LANES, LANES), LANES)

    for copy in loads[2:]:
        copy.wait()
    columns = []
    for q in range(2):
        column = jnp.zeros((SUB, LANES), jnp.float32)
        for kind, table in enumerate((damper_k, damper_c)):
            for i in range(2):
                for j in range(2):
                    column = jnp.where(sub == 4 * kind + 2 * i + j, table[i, j, q], column)
        columns.append(column)
    for t in range(tiles):
        where = slice(t * LANES, (t + 1) * LANES)
        dense = jnp.zeros((SUB, LANES), jnp.float32)
        for q in range(2):
            place = damper_at[q] - me_p * nodes - t * LANES
            dense = dense + jnp.where(lane == place, columns[q], 0.0)
        coef[12, :, where] = dense
        row = offset_raw[t : t + 1, :].astype(jnp.float32)
        coef[13, :, where] = jnp.broadcast_to(row, (SUB, LANES))
    for half in range(2):
        coef[8 + half, 0:4, 0:nodes] = link_raw[2 * half]
        coef[8 + half, 4:8, 0:nodes] = link_raw[2 * half + 1]
        coef[10 + half, 0:4, 0:nodes] = inv_raw[2 * half]
        coef[10 + half, 4:8, 0:nodes] = inv_raw[2 * half + 1]
    for copy in loads[:2]:
        copy.wait()

    groups = dirs // SUB
    packs = []
    for ref in (disp_a, vel):
        for g in range(groups):
            packs.append([(ref, c, slice(g * SUB, (g + 1) * SUB)) for c in range(4)])
    for g in range(0, 14, 4):
        packs.append([(coef, k, slice(0, SUB)) for k in range(g, min(g + 4, 14))])
    for side, start, first in ((0, nodes - LANES, LANES - REACH), (1, 0, 0)):
        for n, pack in enumerate(packs):
            held = None
            for s, (ref, c, rows) in enumerate(pack):
                piece = rolled(ref[c, rows, start : start + LANES], REACH * s - first, 1)
                held = piece if held is None else jnp.where(lane >= REACH * s, piece, held)
            to_send[side, n] = held

    pl.semaphore_wait(barrier, 2 + ndir - 1 + nz - 1 + nx - 1)
    halo = []
    for side, by in ((0, 1), (1, ndof - 1)):
        halo.append(
            pltpu.make_async_remote_copy(
                src_ref=to_send.at[side],
                dst_ref=arrived.at[side],
                send_sem=halo_send.at[side],
                recv_sem=halo_recv.at[side],
                device_id=(lax.rem(me_p + by, ndof), me_t),
                device_id_type=MESH,
            )
        )
        halo[-1].start()

    def prepare(t):
        now = at_tile(t)
        before = at_tile(lax.rem(t + around - 1, around))
        p_rows, q_rows = [], []
        for i in range(4):
            shifted = jnp.where(
                lane == 0,
                rolled(coef[4 + i, :, before], 1, 1),
                rolled(coef[4 + i, :, now], 1, 1),
            )
            link = coef[8 + i // 2, :, now]
            if i % 2 == 0:
                link = rolled(link, 4, 0)
            q_rows.append(jnp.where(sub < 4, shifted, link))
            p_rows.append(coef[i, :, now] + jnp.where(sub < 4, rolled(shifted, 4, 0), 0.0))
        film = coef[12, :, now]
        for k in range(2):
            p_rows[k] = p_rows[k] + jnp.where(sub < 2, rolled(film, -2 * k, 0), 0.0)
        v_rows = [rolled(film, -4 - 2 * k, 0) for k in range(2)]
        for i in range(4):
            inv = [
                -coef[10 + i // 2, 4 * (i % 2) + k : 4 * (i % 2) + k + 1, now] for k in range(4)
            ]
            for out, rows in ((pm, p_rows), (qm, q_rows), (vm, v_rows)):
                total = inv[0] * rows[0]
                for k in range(1, len(rows)):
                    total = total + inv[k] * rows[k]
                out[i, :, now] = total

    chunk = min(16, dirs)

    def evaluate(disp, t, finish):
        now = at_tile(t)
        before = at_tile(lax.rem(t + around - 1, around))
        after = at_tile(lax.rem(t + 1, around))
        wide_lane = iota((chunk, LANES), 1)
        target = coef[13, 0:1, now].astype(jnp.int32) + lane[0:1, :]
        inside = jnp.broadcast_to((target >= 0) & (target < LANES), (chunk, LANES))
        index = jnp.broadcast_to(target & (LANES - 1), (chunk, LANES))
        for r in range(0, dirs, chunk):
            rows = slice(r, r + chunk)
            speed = [vel[j, rows, now] for j in range(2)]
            acc = [None] * 4
            for j in range(4):
                here = disp[j, rows, now]
                left = disp[j, rows, before]
                right = disp[j, rows, after]
                previous = jnp.where(wide_lane == 0, rolled(left, 1, 1), rolled(here, 1, 1))
                following = jnp.where(
                    wide_lane == LANES - 1, rolled(right, -1, 1), rolled(here, -1, 1)
                )
                other = jnp.where(wide_lane < LANES // 2, right, left)
                linked = jnp.where(inside, lane_gather(here, index), lane_gather(other, index))
                for i in range(4):
                    total = pm[i, j : j + 1, now] * here
                    total = total + pm[i, 4 + j : 5 + j, now] * following
                    total = total + qm[i, j : j + 1, now] * previous
                    total = total + qm[i, 4 + j : 5 + j, now] * linked
                    if j < 2:
                        total = total + vm[i, j : j + 1, now] * speed[j]
                    acc[i] = total if acc[i] is None else acc[i] + total
            finish(rows, now, acc)

    def finish_first(rows, now, acc):
        for i in range(4):
            v = vel[i, rows, now]
            disp_b[i, rows, now] = (
                disp_a[i, rows, now] + STEP * v + (0.5 * STEP * STEP) * acc[i]
            )
            vel[i, rows, now] = v + (0.5 * STEP) * acc[i]

    def finish_second(rows, now, acc):
        for i in range(4):
            v = vel[i, rows, now] + (0.5 * STEP) * acc[i]
            disp_a[i, rows, now] = (
                disp_b[i, rows, now] + STEP * v + (0.5 * STEP * STEP) * acc[i]
            )
            vel[i, rows, now] = v + (0.5 * STEP) * acc[i]

    def finish_last(rows, now, acc):
        for i in range(4):
            vel_out[i, rows, now] = vel[i, rows, now] + (0.5 * STEP) * acc[i]

    def prepare_tile(t, carry):
        prepare(t)
        return carry

    def first_tile(t, carry):
        evaluate(disp_a, t, finish_first)
        return carry

    own_rows = pl.ds(pl.multiple_of(me_t * dirs, dirs), dirs)

    def tile_copy(peer, half):
        part = pl.ds(2 * half, 2)
        return pltpu.make_async_remote_copy(
            src_ref=disp_a.at[part, :, at_tile(peer)],
            dst_ref=x_all.at[part, own_rows, :],
            send_sem=a2a_send,
            recv_sem=a2a_recv.at[half],
            device_id=(me_p, peer),
            device_id_type=MESH,
        )

    def send_tile(t, halves):
        @pl.when(t != me_t)
        def _():
            for half in halves:
                tile_copy(t, half).start()

    def second_tile(t, carry):
        evaluate(disp_b, t, finish_second)
        return carry

    def second_and_send(t, carry):
        evaluate(disp_b, t, finish_second)
        send_tile(t, (0, 1))
        return carry

    lax.fori_loop(1, tiles, prepare_tile, 0)
    lax.fori_loop(1, tiles - 1, first_tile, 0)
    lax.fori_loop(2, tiles - 2, second_and_send, 0)

    for copy in halo:
        copy.wait_recv()
    right_end = jnp.where(me_p < ndof - 1, REACH, 0)
    left_start = jnp.where(me_p > 0, LANES - REACH, LANES)
    for n, pack in enumerate(packs):
        from_left, from_right = arrived[0, n], arrived[1, n]
        for s, (ref, c, rows) in enumerate(pack):
            piece = jnp.where(lane < right_end, rolled(from_right, -REACH * s, 1), 0.0)
            ref[c, rows, nodes : nodes + LANES] = jnp.where(
                lane >= left_start, rolled(from_left, LANES - REACH - REACH * s, 1), piece
            )

    def wrapped(k):
        return lax.rem(k, around)

    lax.fori_loop(tiles, tiles + 2, lambda k, c: prepare_tile(wrapped(k), c), 0)

    def inner_end(k, carry):
        evaluate(disp_a, lax.rem(tiles - 1 + k, tiles), finish_first)
        return second_and_send(lax.rem(tiles - 2 + 3 * k, tiles), carry)

    def outer_end(k, carry):
        t = lax.rem(tiles - 1 + k, tiles)
        evaluate(disp_b, t, finish_second)
        send_tile(t, (0,))
        return carry

    def send_rest(k, carry):
        send_tile(lax.rem(tiles - 1 + k, tiles), (1,))
        return carry

    lax.fori_loop(0, 2, inner_end, 0)
    lax.fori_loop(tiles, tiles + 1, first_tile, 0)
    lax.fori_loop(0, 2, outer_end, 0)
    lax.fori_loop(0, 2, send_rest, 0)
    x_all[:, own_rows, :] = disp_a[:, :, at_tile(me_t)]
    evaluate(disp_b, tiles, finish_second)

    def last_tile(t, carry):
        evaluate(disp_a, t, finish_last)
        return carry

    lax.fori_loop(0, tiles, last_tile, 0)

    total = None
    for half in range(2):
        arrivals = x_all.at[pl.ds(2 * half, 2), pl.ds(0, (ndir - 1) * dirs), :]
        pltpu.make_async_copy(arrivals, arrivals, a2a_recv.at[half]).wait()
        pair = jnp.concatenate([x_all[2 * half], x_all[2 * half + 1]], axis=1)
        product = lax.dot_general(
            pair,
            pair,
            (((1,), (1,)), ((), ())),
            precision=HIGHEST,
            preferred_element_type=jnp.float32,
        )
        total = product if total is None else total + product
    half_n = gram.shape[1]
    gram_part[0] = total[0:half_n, 0:half_n]
    gram_part[1] = total[0:half_n, half_n:]
    gram_part[2] = total[half_n:, half_n:]

    def part_copy(by):
        to = at_x[by[0]], at_t[by[1]]
        member = to[1] * nx + to[0]
        return pltpu.make_async_remote_copy(
            src_ref=gram_part.at[:, pl.ds(member * share, share), :],
            dst_ref=slots.at[:, pl.ds(me * share, share), :],
            send_sem=rs_send,
            recv_sem=rs_recv,
            device_id=(me_z * nx + to[0], to[1]),
            device_id_type=MESH,
        )

    for by in plane:
        part_copy(by).start()
    mine = pl.ds(me * share, share)
    own = pltpu.make_async_copy(gram_part.at[:, mine, :], slots.at[:, mine, :], rs_recv)
    own.start()
    pltpu.make_async_copy(slots, slots, rs_recv).wait()
    total = slots[:, 0:SUB, :]
    for k in range(SUB, slots.shape[1], SUB):
        total = total + slots[:, k : k + SUB, :]
    for b in range(3):
        piece = total[b]
        for k in range(share, SUB, share):
            piece = piece + rolled(total[b], -k, 0)
        z_part[b] = piece

    def z_copy(by):
        return pltpu.make_async_remote_copy(
            src_ref=z_part.at[:, 0:share, :],
            dst_ref=z_slots.at[me_z, :, 0:share, :],
            send_sem=z_send,
            recv_sem=z_recv,
            device_id=(lax.rem(me_z + by, nz) * nx + me_x, me_t),
            device_id_type=MESH,
        )

    for by in line:
        z_copy(by).start()
    own = pltpu.make_async_copy(
        z_part.at[:, 0:share, :], z_slots.at[me_z, :, 0:share, :], z_recv
    )
    own.start()
    arrivals = z_slots.at[:, :, 0:share, :]
    pltpu.make_async_copy(arrivals, arrivals, z_recv).wait()
    total = z_slots[0, :, 0:share, :]
    for k in range(1, nz):
        total = total + z_slots[k, :, 0:share, :]
    z_sum[:, 0:share, :] = total

    def sum_copy(by):
        to = at_x[by[0]], at_t[by[1]]
        return pltpu.make_async_remote_copy(
            src_ref=z_sum.at[:, 0:share, :],
            dst_ref=gram.at[:, mine, :],
            send_sem=ag_send,
            recv_sem=ag_recv,
            device_id=(me_z * nx + to[0], to[1]),
            device_id_type=MESH,
        )

    for by in plane:
        sum_copy(by).start()
    own = pltpu.make_async_copy(z_sum.at[:, 0:share, :], gram.at[:, mine, :], ag_recv)
    own.start()
    pltpu.make_async_copy(gram, gram, ag_recv).wait()

    for copy in halo:
        copy.wait_send()
    for sent, sem in (
        (x_all.at[:, 0 : (ndir - 1) * dirs, :], a2a_send),
        (gram_part.at[:, 0 : len(plane) * share, :], rs_send),
        (z_slots.at[0 : len(line), :, 0:share, :], z_send),
        (gram_part.at[:, 0 : len(plane) * share, :], ag_send),
    ):
        pltpu.make_async_copy(sent, sent, sem).wait()


def newmark(ndof, nx, ndir, *args):
    dirs, nodes = args[0].shape[1:]
    around = nodes + LANES
    n = dirs * ndir
    packs = 2 * (dirs // SUB) + 4
    f32 = jnp.float32
    hbm = pl.BlockSpec(memory_space=pltpu.HBM)
    vmem = pl.BlockSpec(memory_space=pltpu.VMEM)
    dma = pltpu.SemaphoreType.DMA
    return pl.pallas_call(
        functools.partial(newmark_kernel, ndof, nx, ndir),
        out_shape=(
            pltpu.VMEM((4, dirs, nodes), f32),
            pltpu.VMEM((4, n, LANES), f32),
            pltpu.VMEM((3, n // 2, n // 2), f32),
        ),
        in_specs=[hbm] * 9,
        out_specs=[vmem] * 3,
        scratch_shapes=[
            pltpu.VMEM((4, dirs, around), f32),
            pltpu.VMEM((4, dirs, around), f32),
            pltpu.VMEM((4, dirs, around), f32),
            pltpu.VMEM((14, SUB, around), f32),
            pltpu.VMEM((4, 4, nodes), f32),
            pltpu.VMEM((4, 4, nodes), f32),
            pltpu.VMEM((nodes // LANES, LANES), jnp.int32),
            pltpu.VMEM((4, SUB, around), f32),
            pltpu.VMEM((4, SUB, around), f32),
            pltpu.VMEM((4, SUB, around), f32),
            pltpu.VMEM((2, packs, SUB, LANES), f32),
            pltpu.VMEM((2, packs, SUB, LANES), f32),
            pltpu.VMEM((3, n // 2, n // 2), f32),
            pltpu.VMEM((3, n // 2, n // 2), f32),
            pltpu.VMEM((3, SUB, n // 2), f32),
            pltpu.VMEM((ndof // nx, 3, SUB, n // 2), f32),
            pltpu.VMEM((3, SUB, n // 2), f32),
            pltpu.SMEM(args[6].shape, jnp.int32),
            pltpu.SMEM(args[7].shape, f32),
            pltpu.SMEM(args[8].shape, f32),
            dma((9,)),
            dma((2,)),
            dma((2,)),
            dma(()),
            dma((2,)),
            dma(()),
            dma(()),
            dma(()),
            dma(()),
            dma(()),
            dma(()),
        ],
        compiler_params=pltpu.CompilerParams(
            collective_id=0, has_side_effects=True, vmem_limit_bytes=32 * 2**20
        ),
        name="newmark_and_gram",
    )(*[pltpu.with_memory_space_constraint(x, pltpu.HBM) for x in args])


def spread(x, lane):
    return jnp.broadcast_to(x[:, lane : lane + 1], (x.shape[0], LANES))


def tiled(x, width):
    return x if width == LANES else jnp.concatenate([x] * (width // LANES), axis=1)


def eliminate(block, micro, near):
    size, width = block.shape
    sub = iota((SUB, LANES), 0)
    groups = micro // SUB
    rows = [block[i : i + SUB] for i in range(0, size, SUB)]
    done = []
    for s in range(0, size, micro):
        top = rows[:groups]
        rest = rows[groups:]
        column = [
            [spread(top[g], s + j) if g >= j // SUB else None for g in range(groups)]
            for j in range(micro)
        ]

        def entry(j, m):
            return column[j][m // SUB][m % SUB : m % SUB + 1]

        inverse = []
        pivots = [None] * groups
        for j in range(micro):
            group, at = j // SUB, j % SUB
            pivot = entry(j, j)
            inverse.append(1.0 / pivot)
            held = jnp.broadcast_to(pivot, (SUB, LANES))
            pivots[group] = held if at == 0 else jnp.where(sub == at, held, pivots[group])
            source = top[group][at : at + 1]
            for g in range(group, groups):
                if g == group and at == SUB - 1:
                    continue
                factor = column[j][g] * inverse[j]
                if g == group:
                    factor = jnp.where(sub > at, factor, 0.0)
                for m in range(j + 1, min(micro, (g + 1) * SUB)):
                    column[m][g] = column[m][g] - factor * entry(j, m)
                top[g] = top[g] - tiled(factor, width) * source
        rows = []
        for part in rest[:near]:
            own = [spread(part, s + j) for j in range(micro)]
            for j in range(micro):
                factor = own[j] * inverse[j]
                for m in range(j + 1, micro):
                    own[m] = own[m] - factor * entry(j, m)
                part = part - tiled(factor, width) * top[j // SUB][j % SUB : j % SUB + 1]
            rows.append(part)
        top = jnp.concatenate(
            [t * tiled(lax.rsqrt(p), width) for t, p in zip(top, pivots)], axis=0
        )
        if len(rest) > near:
            update = lax.dot_general(
                top[:, 0:size],
                top,
                (((0,), (0,)), ((), ())),
                precision=HIGHEST,
                preferred_element_type=jnp.float32,
            )
            for i in range(near, len(rest)):
                start = s + micro + SUB * i
                rows.append(rest[i] - update[start : start + SUB])
        done.append(top)
    return jnp.concatenate(done, axis=0)


def factor_kernel(
    scale, micro, near, gram, x, vel, q_out, r_out, vel_out, q, r, work, sems
):
    size = gram.shape[1]
    n = 2 * size
    vel_store = pltpu.make_async_copy(vel, vel_out, sems.at[0])
    vel_store.start()
    stores = []

    def store(source, target):
        copy = pltpu.make_async_copy(source, target, sems.at[1 + len(stores)])
        copy.start()
        stores.append(copy)

    def product(left, right, dims=(((1,), (0,)), ((), ()))):
        return lax.dot_general(
            left, right, dims, precision=HIGHEST, preferred_element_type=jnp.float32
        )

    transposed = (((0,), (0,)), ((), ()))
    row, col = iota((size, size), 0), iota((size, size), 1)
    identity = (row == col).astype(jnp.float32)
    upper, lower = pl.ds(0, size), pl.ds(size, size)
    r[size:, 0:size] = jnp.zeros((size, size), jnp.float32)

    block = eliminate(jnp.concatenate([gram[0] * scale, identity], axis=1), micro, near)
    inverse = block[:, size:]
    side = product(inverse, gram[1] * scale)
    corner = gram[2] * scale - product(side, side, transposed)
    r[0:size, 0:size] = jnp.where(row <= col, block[:, 0:size], 0.0)
    r[0:size, size:n] = side
    for c in range(4):
        first = product(inverse, x[c, 0:size, :])
        q[c, 0:size, :] = first
        work[c] = x[c, size:n, :] - product(side, first, transposed)

    block = eliminate(jnp.concatenate([corner, identity], axis=1), micro, near)
    inverse = block[:, size:]
    store(r.at[upper, :], r_out.at[upper, :])
    for c in range(4):
        store(q.at[c, upper, :], q_out.at[c, upper, :])
    r[size:n, size:n] = jnp.where(row <= col, block[:, 0:size], 0.0)
    store(r.at[lower, :], r_out.at[lower, :])
    for c in range(4):
        q[c, size:n, :] = product(inverse, work[c])
        store(q.at[c, lower, :], q_out.at[c, lower, :])
    for copy in stores:
        copy.wait()
    vel_store.wait()


def factor(gram, x, vel, scale):
    n = x.shape[1]
    vmem = pl.BlockSpec(memory_space=pltpu.VMEM)
    hbm = pl.BlockSpec(memory_space=pltpu.HBM)
    return pl.pallas_call(
        functools.partial(factor_kernel, scale, 2 * SUB, 2),
        out_shape=(
            pltpu.HBM(x.shape, jnp.float32),
            pltpu.HBM((n, n), jnp.float32),
            pltpu.HBM(vel.shape, jnp.float32),
        ),
        in_specs=[vmem, vmem, vmem],
        out_specs=[hbm, hbm, hbm],
        scratch_shapes=[
            pltpu.VMEM(x.shape, jnp.float32),
            pltpu.VMEM((n, n), jnp.float32),
            pltpu.VMEM((4, n // 2, LANES), jnp.float32),
            pltpu.SemaphoreType.DMA((11,)),
        ],
        compiler_params=pltpu.CompilerParams(vmem_limit_bytes=32 * 2**20),
        name="factor_and_solve",
    )(*[pltpu.with_memory_space_constraint(y, pltpu.VMEM) for y in (gram, x, vel)])


def on_device(ndof, ndir, disp, veloc, elem, link, inv, offset, damper_at, damper_k, damper_c):
    nodes = disp.shape[2]
    offset = offset.reshape(nodes // LANES, LANES)
    nx = CHIPS_X if ndof % CHIPS_X == 0 else 1
    veloc, x, gram = newmark(
        ndof, nx, ndir, disp, veloc, elem, link, inv, offset, damper_at, damper_k, damper_c
    )
    q_block, r_factor, veloc = factor(gram, x, veloc, 1.0 / (4.0 * nodes * ndof))
    return veloc, q_block, r_factor


def solution(mesh):
    in_specs = (
        P(None, "dir", "dof"),
        P(None, "dir", "dof"),
        P(None, None, "dof"),
        P(None, None, "dof"),
        P(None, None, "dof"),
        P("dof"),
        P("dof"),
        P(None, None, "dof"),
        P(None, None, "dof"),
    )
    out_specs = (P(None, "dir", "dof"), P(None, None, ("dof", "dir")), P())
    return jax.shard_map(
        functools.partial(on_device, mesh.shape["dof"], mesh.shape["dir"]),
        mesh=mesh,
        in_specs=in_specs,
        out_specs=out_specs,
        check_vma=False,
    )
```

```python
import functools

import jax
import jax.numpy as jnp
from jax import lax
from jax.experimental import pallas as pl
from jax.experimental.pallas import tpu as pltpu
from jax.sharding import PartitionSpec as P

STEP = 0.5
LANES = 128
SUB = 8
REACH = 32
CHIPS_X = 4
MESH = pl.DeviceIdType.MESH
HIGHEST = lax.Precision.HIGHEST


def iota(shape, axis):
    return lax.broadcasted_iota(jnp.int32, shape, axis)


def rolled(x, by, axis):
    by = by % x.shape[axis]
    return pltpu.roll(x, by, axis) if by else x


def lane_gather(x, index):
    return jnp.take_along_axis(x, index, axis=1, mode="promise_in_bounds")


def far_first(offsets, sizes):
    def distance(offset):
        return sum(min(o, n - o) for o, n in zip(offset, sizes))

    return [o for o in sorted(offsets, key=distance, reverse=True) if distance(o)]


def newmark_kernel(
    ndof,
    nx,
    ndir,
    disp_in,
    vel_in,
    elem_in,
    link_in,
    inv_in,
    offset_in,
    damper_at_in,
    damper_k_in,
    damper_c_in,
    vel_out,
    x_all,
    gram,
    disp_a,
    disp_b,
    vel,
    coef,
    link_raw,
    inv_raw,
    offset_raw,
    pm,
    qm,
    vm,
    to_send,
    arrived,
    gram_part,
    slots,
    z_part,
    z_slots,
    z_sum,
    damper_at,
    damper_k,
    damper_c,
    load_sem,
    halo_send,
    halo_recv,
    a2a_send,
    a2a_recv,
    rs_send,
    rs_recv,
    z_send,
    z_recv,
    ag_send,
    ag_recv,
):
    me_p = lax.axis_index("dof")
    me_t = lax.axis_index("dir")
    dirs = disp_in.shape[1]
    nodes = disp_in.shape[2]
    tiles = nodes // LANES
    around = tiles + 1
    nz = ndof // nx
    me_z, me_x = me_p // nx, lax.rem(me_p, nx)
    me = me_t * nx + me_x
    share = gram.shape[1] // (nx * ndir)
    plane = far_first([(x, t) for x in range(nx) for t in range(ndir)], (nx, ndir))
    line = [by for by, in far_first([(z,) for z in range(nz)], (nz,))]

    at_x = [lax.rem(me_x + by, nx) for by in range(nx)]
    at_t = [lax.rem(me_t + by, ndir) for by in range(ndir)]
    barrier = pltpu.get_barrier_semaphore()

    def greet(p, t):
        pl.semaphore_signal(barrier, inc=1, device_id=(p, t), device_id_type=MESH)

    for by in (1, ndof - 1):
        greet(lax.rem(me_p + by, ndof), me_t)
    loads = [
        (disp_in, disp_a.at[:, :, 0:nodes]),
        (vel_in, vel.at[:, :, 0:nodes]),
        (elem_in, coef.at[0:8, :, 0:nodes]),
        (link_in, link_raw),
        (inv_in, inv_raw),
        (offset_in, offset_raw),
        (damper_at_in, damper_at),
        (damper_k_in, damper_k),
        (damper_c_in, damper_c),
    ]
    loads = [pltpu.make_async_copy(s, d, load_sem.at[i]) for i, (s, d) in enumerate(loads)]
    for copy in loads:
        copy.start()

    for by, in far_first([(t,) for t in range(ndir)], (ndir,)):
        greet(me_p, lax.rem(me_t + by, ndir))
    for by in line:
        greet(lax.rem(me_z + by, nz) * nx + me_x, me_t)
    for by in range(1, nx):
        greet(me_z * nx + lax.rem(me_x + by, nx), me_t)

    lane = iota((SUB, LANES), 1)
    sub = iota((SUB, LANES), 0)

    def at_tile(t):
        return pl.ds(pl.multiple_of(t * LANES, LANES), LANES)

    for copy in loads[2:]:
        copy.wait()
    columns = []
    for q in range(2):
        column = jnp.zeros((SUB, LANES), jnp.float32)
        for kind, table in enumerate((damper_k, damper_c)):
            for i in range(2):
                for j in range(2):
                    column = jnp.where(sub == 4 * kind + 2 * i + j, table[i, j, q], column)
        columns.append(column)
    for t in range(tiles):
        where = slice(t * LANES, (t + 1) * LANES)
        dense = jnp.zeros((SUB, LANES), jnp.float32)
        for q in range(2):
            place = damper_at[q] - me_p * nodes - t * LANES
            dense = dense + jnp.where(lane == place, columns[q], 0.0)
        coef[12, :, where] = dense
        row = offset_raw[t : t + 1, :].astype(jnp.float32)
        coef[13, :, where] = jnp.broadcast_to(row, (SUB, LANES))
    for half in range(2):
        coef[8 + half, 0:4, 0:nodes] = link_raw[2 * half]
        coef[8 + half, 4:8, 0:nodes] = link_raw[2 * half + 1]
        coef[10 + half, 0:4, 0:nodes] = inv_raw[2 * half]
        coef[10 + half, 4:8, 0:nodes] = inv_raw[2 * half + 1]
    for copy in loads[:2]:
        copy.wait()

    groups = dirs // SUB
    packs = []
    for ref in (disp_a, vel):
        for g in range(groups):
            packs.append([(ref, c, slice(g * SUB, (g + 1) * SUB)) for c in range(4)])
    for g in range(0, 14, 4):
        packs.append([(coef, k, slice(0, SUB)) for k in range(g, min(g + 4, 14))])
    for side, start, first in ((0, nodes - LANES, LANES - REACH), (1, 0, 0)):
        for n, pack in enumerate(packs):
            held = None
            for s, (ref, c, rows) in enumerate(pack):
                piece = rolled(ref[c, rows, start : start + LANES], REACH * s - first, 1)
                held = piece if held is None else jnp.where(lane >= REACH * s, piece, held)
            to_send[side, n] = held

    pl.semaphore_wait(barrier, 2 + ndir - 1 + nz - 1 + nx - 1)
    halo = []
    for side, by in ((0, 1), (1, ndof - 1)):
        halo.append(
            pltpu.make_async_remote_copy(
                src_ref=to_send.at[side],
                dst_ref=arrived.at[side],
                send_sem=halo_send.at[side],
                recv_sem=halo_recv.at[side],
                device_id=(lax.rem(me_p + by, ndof), me_t),
                device_id_type=MESH,
            )
        )
        halo[-1].start()

    def prepare(t):
        now = at_tile(t)
        before = at_tile(lax.rem(t + around - 1, around))
        p_rows, q_rows = [], []
        for i in range(4):
            shifted = jnp.where(
                lane == 0,
                rolled(coef[4 + i, :, before], 1, 1),
                rolled(coef[4 + i, :, now], 1, 1),
            )
            link = coef[8 + i // 2, :, now]
            if i % 2 == 0:
                link = rolled(link, 4, 0)
            q_rows.append(jnp.where(sub < 4, shifted, link))
            p_rows.append(coef[i, :, now] + jnp.where(sub < 4, rolled(shifted, 4, 0), 0.0))
        film = coef[12, :, now]
        for k in range(2):
            p_rows[k] = p_rows[k] + jnp.where(sub < 2, rolled(film, -2 * k, 0), 0.0)
        v_rows = [rolled(film, -4 - 2 * k, 0) for k in range(2)]
        for i in range(4):
            inv = [
                -coef[10 + i // 2, 4 * (i % 2) + k : 4 * (i % 2) + k + 1, now] for k in range(4)
            ]
            for out, rows in ((pm, p_rows), (qm, q_rows), (vm, v_rows)):
                total = inv[0] * rows[0]
                for k in range(1, len(rows)):
                    total = total + inv[k] * rows[k]
                out[i, :, now] = total

    chunk = min(16, dirs)

    def evaluate(disp, t, finish):
        now = at_tile(t)
        before = at_tile(lax.rem(t + around - 1, around))
        after = at_tile(lax.rem(t + 1, around))
        wide_lane = iota((chunk, LANES), 1)
        target = coef[13, 0:1, now].astype(jnp.int32) + lane[0:1, :]
        inside = jnp.broadcast_to((target >= 0) & (target < LANES), (chunk, LANES))
        index = jnp.broadcast_to(target & (LANES - 1), (chunk, LANES))
        for r in range(0, dirs, chunk):
            rows = slice(r, r + chunk)
            speed = [vel[j, rows, now] for j in range(2)]
            acc = [None] * 4
            for j in range(4):
                here = disp[j, rows, now]
                left = disp[j, rows, before]
                right = disp[j, rows, after]
                previous = jnp.where(wide_lane == 0, rolled(left, 1, 1), rolled(here, 1, 1))
                following = jnp.where(
                    wide_lane == LANES - 1, rolled(right, -1, 1), rolled(here, -1, 1)
                )
                other = jnp.where(wide_lane < LANES // 2, right, left)
                linked = jnp.where(inside, lane_gather(here, index), lane_gather(other, index))
                for i in range(4):
                    total = pm[i, j : j + 1, now] * here
                    total = total + pm[i, 4 + j : 5 + j, now] * following
                    total = total + qm[i, j : j + 1, now] * previous
                    total = total + qm[i, 4 + j : 5 + j, now] * linked
                    if j < 2:
                        total = total + vm[i, j : j + 1, now] * speed[j]
                    acc[i] = total if acc[i] is None else acc[i] + total
            finish(rows, now, acc)

    def finish_first(rows, now, acc):
        for i in range(4):
            v = vel[i, rows, now]
            disp_b[i, rows, now] = (
                disp_a[i, rows, now] + STEP * v + (0.5 * STEP * STEP) * acc[i]
            )
            vel[i, rows, now] = v + (0.5 * STEP) * acc[i]

    def finish_second(rows, now, acc):
        for i in range(4):
            v = vel[i, rows, now] + (0.5 * STEP) * acc[i]
            disp_a[i, rows, now] = (
                disp_b[i, rows, now] + STEP * v + (0.5 * STEP * STEP) * acc[i]
            )
            vel[i, rows, now] = v + (0.5 * STEP) * acc[i]

    def finish_last(rows, now, acc):
        for i in range(4):
            vel_out[i, rows, now] = vel[i, rows, now] + (0.5 * STEP) * acc[i]

    def prepare_tile(t, carry):
        prepare(t)
        return carry

    def first_tile(t, carry):
        evaluate(disp_a, t, finish_first)
        return carry

    own_rows = pl.ds(pl.multiple_of(me_t * dirs, dirs), dirs)

    def tile_copy(peer, half):
        part = pl.ds(2 * half, 2)
        return pltpu.make_async_remote_copy(
            src_ref=disp_a.at[part, :, at_tile(peer)],
            dst_ref=x_all.at[part, own_rows, :],
            send_sem=a2a_send,
            recv_sem=a2a_recv.at[half],
            device_id=(me_p, peer),
            device_id_type=MESH,
        )

    def send_tile(t, halves):
        @pl.when(t != me_t)
        def _():
            for half in halves:
                tile_copy(t, half).start()

    def second_tile(t, carry):
        evaluate(disp_b, t, finish_second)
        return carry

    def second_and_send(t, carry):
        evaluate(disp_b, t, finish_second)
        send_tile(t, (0, 1))
        return carry

    lax.fori_loop(1, tiles, prepare_tile, 0)
    lax.fori_loop(1, tiles - 1, first_tile, 0)
    lax.fori_loop(0, 2, lambda k, c: second_and_send(2 + (tiles - 5) * k, c), 0)

    for copy in halo:
        copy.wait_recv()
    right_end = jnp.where(me_p < ndof - 1, REACH, 0)
    left_start = jnp.where(me_p > 0, LANES - REACH, LANES)
    for n, pack in enumerate(packs):
        from_left, from_right = arrived[0, n], arrived[1, n]
        for s, (ref, c, rows) in enumerate(pack):
            piece = jnp.where(lane < right_end, rolled(from_right, -REACH * s, 1), 0.0)
            ref[c, rows, nodes : nodes + LANES] = jnp.where(
                lane >= left_start, rolled(from_left, LANES - REACH - REACH * s, 1), piece
            )

    def wrapped(k):
        return lax.rem(k, around)

    lax.fori_loop(tiles, tiles + 2, lambda k, c: prepare_tile(wrapped(k), c), 0)

    def inner_end(k, carry):
        evaluate(disp_a, lax.rem(tiles - 1 + k, tiles), finish_first)
        second_and_send(lax.rem(tiles - 2 + 3 * k, tiles), carry)
        return second_and_send(3 + k, carry)

    def outer_end(k, carry):
        t = lax.rem(tiles - 1 + k, tiles)
        evaluate(disp_b, t, finish_second)
        send_tile(t, (0,))
        return carry

    def send_rest(k, carry):
        send_tile(lax.rem(tiles - 1 + k, tiles), (1,))
        return carry

    lax.fori_loop(0, 2, inner_end, 0)
    lax.fori_loop(tiles, tiles + 1, first_tile, 0)
    lax.fori_loop(0, 2, outer_end, 0)
    lax.fori_loop(0, 2, send_rest, 0)
    x_all[:, own_rows, :] = disp_a[:, :, at_tile(me_t)]
    evaluate(disp_b, tiles, finish_second)

    def last_tile(t, carry):
        evaluate(disp_a, t, finish_last)
        return carry

    lax.fori_loop(0, tiles, last_tile, 0)

    total = None
    for half in range(2):
        arrivals = x_all.at[pl.ds(2 * half, 2), pl.ds(0, (ndir - 1) * dirs), :]
        pltpu.make_async_copy(arrivals, arrivals, a2a_recv.at[half]).wait()
        pair = jnp.concatenate([x_all[2 * half], x_all[2 * half + 1]], axis=1)
        product = lax.dot_general(
            pair,
            pair,
            (((1,), (1,)), ((), ())),
            precision=HIGHEST,
            preferred_element_type=jnp.float32,
        )
        total = product if total is None else total + product
    half_n = gram.shape[1]
    gram_part[0] = total[0:half_n, 0:half_n]
    gram_part[1] = total[0:half_n, half_n:]
    gram_part[2] = total[half_n:, half_n:]

    def part_copy(by):
        to = at_x[by[0]], at_t[by[1]]
        member = to[1] * nx + to[0]
        return pltpu.make_async_remote_copy(
            src_ref=gram_part.at[:, pl.ds(member * share, share), :],
            dst_ref=slots.at[:, pl.ds(me * share, share), :],
            send_sem=rs_send,
            recv_sem=rs_recv,
            device_id=(me_z * nx + to[0], to[1]),
            device_id_type=MESH,
        )

    for by in plane:
        part_copy(by).start()
    mine = pl.ds(me * share, share)
    own = pltpu.make_async_copy(gram_part.at[:, mine, :], slots.at[:, mine, :], rs_recv)
    own.start()
    pltpu.make_async_copy(slots, slots, rs_recv).wait()
    total = slots[:, 0:SUB, :]
    for k in range(SUB, slots.shape[1], SUB):
        total = total + slots[:, k : k + SUB, :]
    for b in range(3):
        piece = total[b]
        for k in range(share, SUB, share):
            piece = piece + rolled(total[b], -k, 0)
        z_part[b] = piece

    def z_copy(by):
        return pltpu.make_async_remote_copy(
            src_ref=z_part.at[:, 0:share, :],
            dst_ref=z_slots.at[me_z, :, 0:share, :],
            send_sem=z_send,
            recv_sem=z_recv,
            device_id=(lax.rem(me_z + by, nz) * nx + me_x, me_t),
            device_id_type=MESH,
        )

    for by in line:
        z_copy(by).start()
    own = pltpu.make_async_copy(
        z_part.at[:, 0:share, :], z_slots.at[me_z, :, 0:share, :], z_recv
    )
    own.start()
    arrivals = z_slots.at[:, :, 0:share, :]
    pltpu.make_async_copy(arrivals, arrivals, z_recv).wait()
    total = z_slots[0, :, 0:share, :]
    for k in range(1, nz):
        total = total + z_slots[k, :, 0:share, :]
    z_sum[:, 0:share, :] = total

    def sum_copy(by):
        to = at_x[by[0]], at_t[by[1]]
        return pltpu.make_async_remote_copy(
            src_ref=z_sum.at[:, 0:share, :],
            dst_ref=gram.at[:, mine, :],
            send_sem=ag_send,
            recv_sem=ag_recv,
            device_id=(me_z * nx + to[0], to[1]),
            device_id_type=MESH,
        )

    for by in plane:
        sum_copy(by).start()
    own = pltpu.make_async_copy(z_sum.at[:, 0:share, :], gram.at[:, mine, :], ag_recv)
    own.start()
    pltpu.make_async_copy(gram, gram, ag_recv).wait()

    for copy in halo:
        copy.wait_send()
    for sent, sem in (
        (x_all.at[:, 0 : (ndir - 1) * dirs, :], a2a_send),
        (gram_part.at[:, 0 : len(plane) * share, :], rs_send),
        (z_slots.at[0 : len(line), :, 0:share, :], z_send),
        (gram_part.at[:, 0 : len(plane) * share, :], ag_send),
    ):
        pltpu.make_async_copy(sent, sent, sem).wait()


def newmark(ndof, nx, ndir, *args):
    dirs, nodes = args[0].shape[1:]
    around = nodes + LANES
    n = dirs * ndir
    packs = 2 * (dirs // SUB) + 4
    f32 = jnp.float32
    hbm = pl.BlockSpec(memory_space=pltpu.HBM)
    vmem = pl.BlockSpec(memory_space=pltpu.VMEM)
    dma = pltpu.SemaphoreType.DMA
    return pl.pallas_call(
        functools.partial(newmark_kernel, ndof, nx, ndir),
        out_shape=(
            pltpu.VMEM((4, dirs, nodes), f32),
            pltpu.VMEM((4, n, LANES), f32),
            pltpu.VMEM((3, n // 2, n // 2), f32),
        ),
        in_specs=[hbm] * 9,
        out_specs=[vmem] * 3,
        scratch_shapes=[
            pltpu.VMEM((4, dirs, around), f32),
            pltpu.VMEM((4, dirs, around), f32),
            pltpu.VMEM((4, dirs, around), f32),
            pltpu.VMEM((14, SUB, around), f32),
            pltpu.VMEM((4, 4, nodes), f32),
            pltpu.VMEM((4, 4, nodes), f32),
            pltpu.VMEM((nodes // LANES, LANES), jnp.int32),
            pltpu.VMEM((4, SUB, around), f32),
            pltpu.VMEM((4, SUB, around), f32),
            pltpu.VMEM((4, SUB, around), f32),
            pltpu.VMEM((2, packs, SUB, LANES), f32),
            pltpu.VMEM((2, packs, SUB, LANES), f32),
            pltpu.VMEM((3, n // 2, n // 2), f32),
            pltpu.VMEM((3, n // 2, n // 2), f32),
            pltpu.VMEM((3, SUB, n // 2), f32),
            pltpu.VMEM((ndof // nx, 3, SUB, n // 2), f32),
            pltpu.VMEM((3, SUB, n // 2), f32),
            pltpu.SMEM(args[6].shape, jnp.int32),
            pltpu.SMEM(args[7].shape, f32),
            pltpu.SMEM(args[8].shape, f32),
            dma((9,)),
            dma((2,)),
            dma((2,)),
            dma(()),
            dma((2,)),
            dma(()),
            dma(()),
            dma(()),
            dma(()),
            dma(()),
            dma(()),
        ],
        compiler_params=pltpu.CompilerParams(
            collective_id=0, has_side_effects=True, vmem_limit_bytes=32 * 2**20
        ),
        name="newmark_and_gram",
    )(*[pltpu.with_memory_space_constraint(x, pltpu.HBM) for x in args])


def spread(x, lane):
    return jnp.broadcast_to(x[:, lane : lane + 1], (x.shape[0], LANES))


def tiled(x, width):
    return x if width == LANES else jnp.concatenate([x] * (width // LANES), axis=1)


def eliminate(block, micro, near):
    size, width = block.shape
    sub = iota((SUB, LANES), 0)
    groups = micro // SUB
    rows = [block[i : i + SUB] for i in range(0, size, SUB)]
    done = []
    for s in range(0, size, micro):
        top = rows[:groups]
        rest = rows[groups:]
        column = [
            [spread(top[g], s + j) if g >= j // SUB else None for g in range(groups)]
            for j in range(micro)
        ]

        def entry(j, m):
            return column[j][m // SUB][m % SUB : m % SUB + 1]

        inverse = []
        pivots = [None] * groups
        for j in range(micro):
            group, at = j // SUB, j % SUB
            pivot = entry(j, j)
            inverse.append(1.0 / pivot)
            held = jnp.broadcast_to(pivot, (SUB, LANES))
            pivots[group] = held if at == 0 else jnp.where(sub == at, held, pivots[group])
            source = top[group][at : at + 1]
            for g in range(group, groups):
                if g == group and at == SUB - 1:
                    continue
                factor = column[j][g] * inverse[j]
                if g == group:
                    factor = jnp.where(sub > at, factor, 0.0)
                for m in range(j + 1, min(micro, (g + 1) * SUB)):
                    column[m][g] = column[m][g] - factor * entry(j, m)
                top[g] = top[g] - tiled(factor, width) * source
        rows = []
        for part in rest[:near]:
            own = [spread(part, s + j) for j in range(micro)]
            for j in range(micro):
                factor = own[j] * inverse[j]
                for m in range(j + 1, micro):
                    own[m] = own[m] - factor * entry(j, m)
                part = part - tiled(factor, width) * top[j // SUB][j % SUB : j % SUB + 1]
            rows.append(part)
        top = jnp.concatenate(
            [t * tiled(lax.rsqrt(p), width) for t, p in zip(top, pivots)], axis=0
        )
        if len(rest) > near:
            update = lax.dot_general(
                top[:, 0:size],
                top,
                (((0,), (0,)), ((), ())),
                precision=HIGHEST,
                preferred_element_type=jnp.float32,
            )
            for i in range(near, len(rest)):
                start = s + micro + SUB * i
                rows.append(rest[i] - update[start : start + SUB])
        done.append(top)
    return jnp.concatenate(done, axis=0)


def factor_kernel(
    scale, micro, near, gram, x, vel, q_out, r_out, vel_out, q, r, work, sems
):
    size = gram.shape[1]
    n = 2 * size
    vel_store = pltpu.make_async_copy(vel, vel_out, sems.at[0])
    vel_store.start()
    stores = []

    def store(source, target):
        copy = pltpu.make_async_copy(source, target, sems.at[1 + len(stores)])
        copy.start()
        stores.append(copy)

    def product(left, right, dims=(((1,), (0,)), ((), ()))):
        return lax.dot_general(
            left, right, dims, precision=HIGHEST, preferred_element_type=jnp.float32
        )

    transposed = (((0,), (0,)), ((), ()))
    row, col = iota((size, size), 0), iota((size, size), 1)
    identity = (row == col).astype(jnp.float32)
    upper, lower = pl.ds(0, size), pl.ds(size, size)
    r[size:, 0:size] = jnp.zeros((size, size), jnp.float32)

    block = eliminate(jnp.concatenate([gram[0] * scale, identity], axis=1), micro, near)
    inverse = block[:, size:]
    side = product(inverse, gram[1] * scale)
    corner = gram[2] * scale - product(side, side, transposed)
    r[0:size, 0:size] = jnp.where(row <= col, block[:, 0:size], 0.0)
    r[0:size, size:n] = side
    for c in range(4):
        first = product(inverse, x[c, 0:size, :])
        q[c, 0:size, :] = first
        work[c] = x[c, size:n, :] - product(side, first, transposed)

    block = eliminate(jnp.concatenate([corner, identity], axis=1), micro, near)
    inverse = block[:, size:]
    store(r.at[upper, :], r_out.at[upper, :])
    for c in range(4):
        store(q.at[c, upper, :], q_out.at[c, upper, :])
    r[size:n, size:n] = jnp.where(row <= col, block[:, 0:size], 0.0)
    store(r.at[lower, :], r_out.at[lower, :])
    for c in range(4):
        q[c, size:n, :] = product(inverse, work[c])
        store(q.at[c, lower, :], q_out.at[c, lower, :])
    for copy in stores:
        copy.wait()
    vel_store.wait()


def factor(gram, x, vel, scale):
    n = x.shape[1]
    vmem = pl.BlockSpec(memory_space=pltpu.VMEM)
    hbm = pl.BlockSpec(memory_space=pltpu.HBM)
    return pl.pallas_call(
        functools.partial(factor_kernel, scale, 2 * SUB, 2),
        out_shape=(
            pltpu.HBM(x.shape, jnp.float32),
            pltpu.HBM((n, n), jnp.float32),
            pltpu.HBM(vel.shape, jnp.float32),
        ),
        in_specs=[vmem, vmem, vmem],
        out_specs=[hbm, hbm, hbm],
        scratch_shapes=[
            pltpu.VMEM(x.shape, jnp.float32),
            pltpu.VMEM((n, n), jnp.float32),
            pltpu.VMEM((4, n // 2, LANES), jnp.float32),
            pltpu.SemaphoreType.DMA((11,)),
        ],
        compiler_params=pltpu.CompilerParams(vmem_limit_bytes=32 * 2**20),
        name="factor_and_solve",
    )(*[pltpu.with_memory_space_constraint(y, pltpu.VMEM) for y in (gram, x, vel)])


def on_device(ndof, ndir, disp, veloc, elem, link, inv, offset, damper_at, damper_k, damper_c):
    nodes = disp.shape[2]
    offset = offset.reshape(nodes // LANES, LANES)
    nx = CHIPS_X if ndof % CHIPS_X == 0 else 1
    veloc, x, gram = newmark(
        ndof, nx, ndir, disp, veloc, elem, link, inv, offset, damper_at, damper_k, damper_c
    )
    q_block, r_factor, veloc = factor(gram, x, veloc, 1.0 / (4.0 * nodes * ndof))
    return veloc, q_block, r_factor


def solution(mesh):
    in_specs = (
        P(None, "dir", "dof"),
        P(None, "dir", "dof"),
        P(None, None, "dof"),
        P(None, None, "dof"),
        P(None, None, "dof"),
        P("dof"),
        P("dof"),
        P(None, None, "dof"),
        P(None, None, "dof"),
    )
    out_specs = (P(None, "dir", "dof"), P(None, None, ("dof", "dir")), P())
    return jax.shard_map(
        functools.partial(on_device, mesh.shape["dof"], mesh.shape["dir"]),
        mesh=mesh,
        in_specs=in_specs,
        out_specs=out_specs,
        check_vma=False,
    )
```

```python
import functools

import jax
import jax.numpy as jnp
from jax import lax
from jax.experimental import pallas as pl
from jax.experimental.pallas import tpu as pltpu
from jax.sharding import PartitionSpec as P

STEP = 0.5
LANES = 128
SUB = 8
REACH = 32
CHIPS_X = 4
MESH = pl.DeviceIdType.MESH
HIGHEST = lax.Precision.HIGHEST


def iota(shape, axis):
    return lax.broadcasted_iota(jnp.int32, shape, axis)


def rolled(x, by, axis):
    by = by % x.shape[axis]
    return pltpu.roll(x, by, axis) if by else x


def lane_gather(x, index):
    return jnp.take_along_axis(x, index, axis=1, mode="promise_in_bounds")


def far_first(offsets, sizes):
    def distance(offset):
        return sum(min(o, n - o) for o, n in zip(offset, sizes))

    return [o for o in sorted(offsets, key=distance, reverse=True) if distance(o)]


def newmark_kernel(
    ndof,
    nx,
    ndir,
    disp_in,
    vel_in,
    elem_in,
    link_in,
    inv_in,
    offset_in,
    damper_at_in,
    damper_k_in,
    damper_c_in,
    vel_out,
    x_all,
    gram,
    disp_a,
    disp_b,
    vel,
    coef,
    link_raw,
    inv_raw,
    offset_raw,
    pm,
    qm,
    vm,
    to_send,
    arrived,
    gram_part,
    slots,
    z_part,
    z_slots,
    z_sum,
    damper_at,
    damper_k,
    damper_c,
    load_sem,
    halo_send,
    halo_recv,
    a2a_send,
    a2a_recv,
    rs_send,
    rs_recv,
    z_send,
    z_recv,
    ag_send,
    ag_recv,
):
    me_p = lax.axis_index("dof")
    me_t = lax.axis_index("dir")
    dirs = disp_in.shape[1]
    nodes = disp_in.shape[2]
    tiles = nodes // LANES
    around = tiles + 1
    nz = ndof // nx
    me_z, me_x = me_p // nx, lax.rem(me_p, nx)
    me = me_t * nx + me_x
    share = gram.shape[1] // (nx * ndir)
    plane = far_first([(x, t) for x in range(nx) for t in range(ndir)], (nx, ndir))
    line = [by for by, in far_first([(z,) for z in range(nz)], (nz,))]

    at_x = [lax.rem(me_x + by, nx) for by in range(nx)]
    at_t = [lax.rem(me_t + by, ndir) for by in range(ndir)]
    barrier = pltpu.get_barrier_semaphore()

    def greet(p, t):
        pl.semaphore_signal(barrier, inc=1, device_id=(p, t), device_id_type=MESH)

    for by in (1, ndof - 1):
        greet(lax.rem(me_p + by, ndof), me_t)
    loads = [
        (disp_in, disp_a.at[:, :, 0:nodes]),
        (vel_in, vel.at[:, :, 0:nodes]),
        (elem_in, coef.at[0:8, :, 0:nodes]),
        (link_in, link_raw),
        (inv_in, inv_raw),
        (offset_in, offset_raw),
        (damper_at_in, damper_at),
        (damper_k_in, damper_k),
        (damper_c_in, damper_c),
    ]
    loads = [pltpu.make_async_copy(s, d, load_sem.at[i]) for i, (s, d) in enumerate(loads)]
    for copy in loads:
        copy.start()

    for by, in far_first([(t,) for t in range(ndir)], (ndir,)):
        greet(me_p, lax.rem(me_t + by, ndir))
    for by in line:
        greet(lax.rem(me_z + by, nz) * nx + me_x, me_t)
    for by in range(1, nx):
        greet(me_z * nx + lax.rem(me_x + by, nx), me_t)

    lane = iota((SUB, LANES), 1)
    sub = iota((SUB, LANES), 0)

    def at_tile(t):
        return pl.ds(pl.multiple_of(t * LANES, LANES), LANES)

    for copy in loads[2:]:
        copy.wait()
    columns = []
    for q in range(2):
        column = jnp.zeros((SUB, LANES), jnp.float32)
        for kind, table in enumerate((damper_k, damper_c)):
            for i in range(2):
                for j in range(2):
                    column = jnp.where(sub == 4 * kind + 2 * i + j, table[i, j, q], column)
        columns.append(column)
    for t in range(tiles):
        where = slice(t * LANES, (t + 1) * LANES)
        dense = jnp.zeros((SUB, LANES), jnp.float32)
        for q in range(2):
            place = damper_at[q] - me_p * nodes - t * LANES
            dense = dense + jnp.where(lane == place, columns[q], 0.0)
        coef[12, :, where] = dense
        row = offset_raw[t : t + 1, :].astype(jnp.float32)
        coef[13, :, where] = jnp.broadcast_to(row, (SUB, LANES))
    for half in range(2):
        coef[8 + half, 0:4, 0:nodes] = link_raw[2 * half]
        coef[8 + half, 4:8, 0:nodes] = link_raw[2 * half + 1]
        coef[10 + half, 0:4, 0:nodes] = inv_raw[2 * half]
        coef[10 + half, 4:8, 0:nodes] = inv_raw[2 * half + 1]
    for copy in loads[:2]:
        copy.wait()

    groups = dirs // SUB
    packs = []
    for ref in (disp_a, vel):
        for g in range(groups):
            packs.append([(ref, c, slice(g * SUB, (g + 1) * SUB)) for c in range(4)])
    for g in range(0, 14, 4):
        packs.append([(coef, k, slice(0, SUB)) for k in range(g, min(g + 4, 14))])
    for side, start, first in ((0, nodes - LANES, LANES - REACH), (1, 0, 0)):
        for n, pack in enumerate(packs):
            held = None
            for s, (ref, c, rows) in enumerate(pack):
                piece = rolled(ref[c, rows, start : start + LANES], REACH * s - first, 1)
                held = piece if held is None else jnp.where(lane >= REACH * s, piece, held)
            to_send[side, n] = held

    pl.semaphore_wait(barrier, 2 + ndir - 1 + nz - 1 + nx - 1)
    halo = []
    for side, by in ((0, 1), (1, ndof - 1)):
        halo.append(
            pltpu.make_async_remote_copy(
                src_ref=to_send.at[side],
                dst_ref=arrived.at[side],
                send_sem=halo_send.at[side],
                recv_sem=halo_recv.at[side],
                device_id=(lax.rem(me_p + by, ndof), me_t),
                device_id_type=MESH,
            )
        )
        halo[-1].start()

    def prepare(t):
        now = at_tile(t)
        before = at_tile(lax.rem(t + around - 1, around))
        p_rows, q_rows = [], []
        for i in range(4):
            shifted = jnp.where(
                lane == 0,
                rolled(coef[4 + i, :, before], 1, 1),
                rolled(coef[4 + i, :, now], 1, 1),
            )
            link = coef[8 + i // 2, :, now]
            if i % 2 == 0:
                link = rolled(link, 4, 0)
            q_rows.append(jnp.where(sub < 4, shifted, link))
            p_rows.append(coef[i, :, now] + jnp.where(sub < 4, rolled(shifted, 4, 0), 0.0))
        film = coef[12, :, now]
        for k in range(2):
            p_rows[k] = p_rows[k] + jnp.where(sub < 2, rolled(film, -2 * k, 0), 0.0)
        v_rows = [rolled(film, -4 - 2 * k, 0) for k in range(2)]
        for i in range(4):
            inv = [
                -coef[10 + i // 2, 4 * (i % 2) + k : 4 * (i % 2) + k + 1, now] for k in range(4)
            ]
            for out, rows in ((pm, p_rows), (qm, q_rows), (vm, v_rows)):
                total = inv[0] * rows[0]
                for k in range(1, len(rows)):
                    total = total + inv[k] * rows[k]
                out[i, :, now] = total

    chunk = min(16, dirs)

    def evaluate(disp, t, finish):
        now = at_tile(t)
        before = at_tile(lax.rem(t + around - 1, around))
        after = at_tile(lax.rem(t + 1, around))
        wide_lane = iota((chunk, LANES), 1)
        target = coef[13, 0:1, now].astype(jnp.int32) + lane[0:1, :]
        inside = jnp.broadcast_to((target >= 0) & (target < LANES), (chunk, LANES))
        index = jnp.broadcast_to(target & (LANES - 1), (chunk, LANES))
        for r in range(0, dirs, chunk):
            rows = slice(r, r + chunk)
            speed = [vel[j, rows, now] for j in range(2)]
            acc = [None] * 4
            for j in range(4):
                here = disp[j, rows, now]
                left = disp[j, rows, before]
                right = disp[j, rows, after]
                previous = jnp.where(wide_lane == 0, rolled(left, 1, 1), rolled(here, 1, 1))
                following = jnp.where(
                    wide_lane == LANES - 1, rolled(right, -1, 1), rolled(here, -1, 1)
                )
                other = jnp.where(wide_lane < LANES // 2, right, left)
                linked = jnp.where(inside, lane_gather(here, index), lane_gather(other, index))
                for i in range(4):
                    total = pm[i, j : j + 1, now] * here
                    total = total + pm[i, 4 + j : 5 + j, now] * following
                    total = total + qm[i, j : j + 1, now] * previous
                    total = total + qm[i, 4 + j : 5 + j, now] * linked
                    if j < 2:
                        total = total + vm[i, j : j + 1, now] * speed[j]
                    acc[i] = total if acc[i] is None else acc[i] + total
            finish(rows, now, acc)

    def finish_first(rows, now, acc):
        for i in range(4):
            v = vel[i, rows, now]
            disp_b[i, rows, now] = (
                disp_a[i, rows, now] + STEP * v + (0.5 * STEP * STEP) * acc[i]
            )
            vel[i, rows, now] = v + (0.5 * STEP) * acc[i]

    def finish_second(rows, now, acc):
        for i in range(4):
            v = vel[i, rows, now] + (0.5 * STEP) * acc[i]
            disp_a[i, rows, now] = (
                disp_b[i, rows, now] + STEP * v + (0.5 * STEP * STEP) * acc[i]
            )
            vel[i, rows, now] = v + (0.5 * STEP) * acc[i]

    def finish_last(rows, now, acc):
        for i in range(4):
            vel_out[i, rows, now] = vel[i, rows, now] + (0.5 * STEP) * acc[i]

    def prepare_tile(t, carry):
        prepare(t)
        return carry

    def first_tile(t, carry):
        evaluate(disp_a, t, finish_first)
        return carry

    own_rows = pl.ds(pl.multiple_of(me_t * dirs, dirs), dirs)

    def tile_copy(peer, half):
        part = pl.ds(2 * half, 2)
        return pltpu.make_async_remote_copy(
            src_ref=disp_a.at[part, :, at_tile(peer)],
            dst_ref=x_all.at[part, own_rows, :],
            send_sem=a2a_send,
            recv_sem=a2a_recv.at[half],
            device_id=(me_p, peer),
            device_id_type=MESH,
        )

    def send_tile(t, halves):
        @pl.when(t != me_t)
        def _():
            for half in halves:
                tile_copy(t, half).start()

    def second_tile(t, carry):
        evaluate(disp_b, t, finish_second)
        return carry

    def second_and_send(t, carry):
        evaluate(disp_b, t, finish_second)
        send_tile(t, (0, 1))
        return carry

    def prepare_and_first(t, carry):
        prepare(t)
        return first_tile(t, carry)

    def advance(t, carry):
        prepare_and_first(t + 1, carry)
        return second_and_send(t, carry)

    lax.fori_loop(1, 3, prepare_and_first, 0)
    lax.fori_loop(2, tiles - 2, advance, 0)
    prepare(tiles - 1)

    for copy in halo:
        copy.wait_recv()
    right_end = jnp.where(me_p < ndof - 1, REACH, 0)
    left_start = jnp.where(me_p > 0, LANES - REACH, LANES)
    for n, pack in enumerate(packs):
        from_left, from_right = arrived[0, n], arrived[1, n]
        for s, (ref, c, rows) in enumerate(pack):
            piece = jnp.where(lane < right_end, rolled(from_right, -REACH * s, 1), 0.0)
            ref[c, rows, nodes : nodes + LANES] = jnp.where(
                lane >= left_start, rolled(from_left, LANES - REACH - REACH * s, 1), piece
            )

    def wrapped(k):
        return lax.rem(k, around)

    lax.fori_loop(tiles, tiles + 2, lambda k, c: prepare_tile(wrapped(k), c), 0)

    def inner_end(k, carry):
        evaluate(disp_a, lax.rem(tiles - 1 + k, tiles), finish_first)
        return second_and_send(lax.rem(tiles - 2 + 3 * k, tiles), carry)

    def outer_end(k, carry):
        t = lax.rem(tiles - 1 + k, tiles)
        evaluate(disp_b, t, finish_second)
        send_tile(t, (0,))
        return carry

    def send_rest(k, carry):
        send_tile(lax.rem(tiles - 1 + k, tiles), (1,))
        return carry

    lax.fori_loop(0, 2, inner_end, 0)
    lax.fori_loop(tiles, tiles + 1, first_tile, 0)
    lax.fori_loop(0, 2, outer_end, 0)
    lax.fori_loop(0, 2, send_rest, 0)
    x_all[:, own_rows, :] = disp_a[:, :, at_tile(me_t)]
    evaluate(disp_b, tiles, finish_second)

    def last_tile(t, carry):
        evaluate(disp_a, t, finish_last)
        return carry

    lax.fori_loop(0, tiles, last_tile, 0)

    total = None
    for half in range(2):
        arrivals = x_all.at[pl.ds(2 * half, 2), pl.ds(0, (ndir - 1) * dirs), :]
        pltpu.make_async_copy(arrivals, arrivals, a2a_recv.at[half]).wait()
        pair = jnp.concatenate([x_all[2 * half], x_all[2 * half + 1]], axis=1)
        product = lax.dot_general(
            pair,
            pair,
            (((1,), (1,)), ((), ())),
            precision=HIGHEST,
            preferred_element_type=jnp.float32,
        )
        total = product if total is None else total + product
    half_n = gram.shape[1]
    gram_part[0] = total[0:half_n, 0:half_n]
    gram_part[1] = total[0:half_n, half_n:]
    gram_part[2] = total[half_n:, half_n:]

    def part_copy(by):
        to = at_x[by[0]], at_t[by[1]]
        member = to[1] * nx + to[0]
        return pltpu.make_async_remote_copy(
            src_ref=gram_part.at[:, pl.ds(member * share, share), :],
            dst_ref=slots.at[:, pl.ds(me * share, share), :],
            send_sem=rs_send,
            recv_sem=rs_recv,
            device_id=(me_z * nx + to[0], to[1]),
            device_id_type=MESH,
        )

    for by in plane:
        part_copy(by).start()
    mine = pl.ds(me * share, share)
    own = pltpu.make_async_copy(gram_part.at[:, mine, :], slots.at[:, mine, :], rs_recv)
    own.start()
    pltpu.make_async_copy(slots, slots, rs_recv).wait()
    total = slots[:, 0:SUB, :]
    for k in range(SUB, slots.shape[1], SUB):
        total = total + slots[:, k : k + SUB, :]
    for b in range(3):
        piece = total[b]
        for k in range(share, SUB, share):
            piece = piece + rolled(total[b], -k, 0)
        z_part[b] = piece

    def z_copy(by):
        return pltpu.make_async_remote_copy(
            src_ref=z_part.at[:, 0:share, :],
            dst_ref=z_slots.at[me_z, :, 0:share, :],
            send_sem=z_send,
            recv_sem=z_recv,
            device_id=(lax.rem(me_z + by, nz) * nx + me_x, me_t),
            device_id_type=MESH,
        )

    for by in line:
        z_copy(by).start()
    own = pltpu.make_async_copy(
        z_part.at[:, 0:share, :], z_slots.at[me_z, :, 0:share, :], z_recv
    )
    own.start()
    arrivals = z_slots.at[:, :, 0:share, :]
    pltpu.make_async_copy(arrivals, arrivals, z_recv).wait()
    total = z_slots[0, :, 0:share, :]
    for k in range(1, nz):
        total = total + z_slots[k, :, 0:share, :]
    z_sum[:, 0:share, :] = total

    def sum_copy(by):
        to = at_x[by[0]], at_t[by[1]]
        return pltpu.make_async_remote_copy(
            src_ref=z_sum.at[:, 0:share, :],
            dst_ref=gram.at[:, mine, :],
            send_sem=ag_send,
            recv_sem=ag_recv,
            device_id=(me_z * nx + to[0], to[1]),
            device_id_type=MESH,
        )

    for by in plane:
        sum_copy(by).start()
    own = pltpu.make_async_copy(z_sum.at[:, 0:share, :], gram.at[:, mine, :], ag_recv)
    own.start()
    pltpu.make_async_copy(gram, gram, ag_recv).wait()

    for copy in halo:
        copy.wait_send()
    for sent, sem in (
        (x_all.at[:, 0 : (ndir - 1) * dirs, :], a2a_send),
        (gram_part.at[:, 0 : len(plane) * share, :], rs_send),
        (z_slots.at[0 : len(line), :, 0:share, :], z_send),
        (gram_part.at[:, 0 : len(plane) * share, :], ag_send),
    ):
        pltpu.make_async_copy(sent, sent, sem).wait()


def newmark(ndof, nx, ndir, *args):
    dirs, nodes = args[0].shape[1:]
    around = nodes + LANES
    n = dirs * ndir
    packs = 2 * (dirs // SUB) + 4
    f32 = jnp.float32
    hbm = pl.BlockSpec(memory_space=pltpu.HBM)
    vmem = pl.BlockSpec(memory_space=pltpu.VMEM)
    dma = pltpu.SemaphoreType.DMA
    return pl.pallas_call(
        functools.partial(newmark_kernel, ndof, nx, ndir),
        out_shape=(
            pltpu.VMEM((4, dirs, nodes), f32),
            pltpu.VMEM((4, n, LANES), f32),
            pltpu.VMEM((3, n // 2, n // 2), f32),
        ),
        in_specs=[hbm] * 9,
        out_specs=[vmem] * 3,
        scratch_shapes=[
            pltpu.VMEM((4, dirs, around), f32),
            pltpu.VMEM((4, dirs, around), f32),
            pltpu.VMEM((4, dirs, around), f32),
            pltpu.VMEM((14, SUB, around), f32),
            pltpu.VMEM((4, 4, nodes), f32),
            pltpu.VMEM((4, 4, nodes), f32),
            pltpu.VMEM((nodes // LANES, LANES), jnp.int32),
            pltpu.VMEM((4, SUB, around), f32),
            pltpu.VMEM((4, SUB, around), f32),
            pltpu.VMEM((4, SUB, around), f32),
            pltpu.VMEM((2, packs, SUB, LANES), f32),
            pltpu.VMEM((2, packs, SUB, LANES), f32),
            pltpu.VMEM((3, n // 2, n // 2), f32),
            pltpu.VMEM((3, n // 2, n // 2), f32),
            pltpu.VMEM((3, SUB, n // 2), f32),
            pltpu.VMEM((ndof // nx, 3, SUB, n // 2), f32),
            pltpu.VMEM((3, SUB, n // 2), f32),
            pltpu.SMEM(args[6].shape, jnp.int32),
            pltpu.SMEM(args[7].shape, f32),
            pltpu.SMEM(args[8].shape, f32),
            dma((9,)),
            dma((2,)),
            dma((2,)),
            dma(()),
            dma((2,)),
            dma(()),
            dma(()),
            dma(()),
            dma(()),
            dma(()),
            dma(()),
        ],
        compiler_params=pltpu.CompilerParams(
            collective_id=0, has_side_effects=True, vmem_limit_bytes=32 * 2**20
        ),
        name="newmark_and_gram",
    )(*[pltpu.with_memory_space_constraint(x, pltpu.HBM) for x in args])


def spread(x, lane):
    return jnp.broadcast_to(x[:, lane : lane + 1], (x.shape[0], LANES))


def tiled(x, width):
    return x if width == LANES else jnp.concatenate([x] * (width // LANES), axis=1)


def eliminate(block, micro, near):
    size, width = block.shape
    sub = iota((SUB, LANES), 0)
    groups = micro // SUB
    rows = [block[i : i + SUB] for i in range(0, size, SUB)]
    done = []
    for s in range(0, size, micro):
        top = rows[:groups]
        rest = rows[groups:]
        column = [
            [spread(top[g], s + j) if g >= j // SUB else None for g in range(groups)]
            for j in range(micro)
        ]

        def entry(j, m):
            return column[j][m // SUB][m % SUB : m % SUB + 1]

        inverse = []
        pivots = [None] * groups
        for j in range(micro):
            group, at = j // SUB, j % SUB
            pivot = entry(j, j)
            inverse.append(1.0 / pivot)
            held = jnp.broadcast_to(pivot, (SUB, LANES))
            pivots[group] = held if at == 0 else jnp.where(sub == at, held, pivots[group])
            source = top[group][at : at + 1]
            for g in range(group, groups):
                if g == group and at == SUB - 1:
                    continue
                factor = column[j][g] * inverse[j]
                if g == group:
                    factor = jnp.where(sub > at, factor, 0.0)
                for m in range(j + 1, min(micro, (g + 1) * SUB)):
                    column[m][g] = column[m][g] - factor * entry(j, m)
                top[g] = top[g] - tiled(factor, width) * source
        rows = []
        for part in rest[:near]:
            own = [spread(part, s + j) for j in range(micro)]
            for j in range(micro):
                factor = own[j] * inverse[j]
                for m in range(j + 1, micro):
                    own[m] = own[m] - factor * entry(j, m)
                part = part - tiled(factor, width) * top[j // SUB][j % SUB : j % SUB + 1]
            rows.append(part)
        top = jnp.concatenate(
            [t * tiled(lax.rsqrt(p), width) for t, p in zip(top, pivots)], axis=0
        )
        if len(rest) > near:
            update = lax.dot_general(
                top[:, 0:size],
                top,
                (((0,), (0,)), ((), ())),
                precision=HIGHEST,
                preferred_element_type=jnp.float32,
            )
            for i in range(near, len(rest)):
                start = s + micro + SUB * i
                rows.append(rest[i] - update[start : start + SUB])
        done.append(top)
    return jnp.concatenate(done, axis=0)


def factor_kernel(
    scale, micro, near, gram, x, vel, q_out, r_out, vel_out, q, r, work, sems
):
    size = gram.shape[1]
    n = 2 * size
    vel_store = pltpu.make_async_copy(vel, vel_out, sems.at[0])
    vel_store.start()
    stores = []

    def store(source, target):
        copy = pltpu.make_async_copy(source, target, sems.at[1 + len(stores)])
        copy.start()
        stores.append(copy)

    def product(left, right, dims=(((1,), (0,)), ((), ()))):
        return lax.dot_general(
            left, right, dims, precision=HIGHEST, preferred_element_type=jnp.float32
        )

    transposed = (((0,), (0,)), ((), ()))
    row, col = iota((size, size), 0), iota((size, size), 1)
    identity = (row == col).astype(jnp.float32)
    upper, lower = pl.ds(0, size), pl.ds(size, size)
    r[size:, 0:size] = jnp.zeros((size, size), jnp.float32)

    block = eliminate(jnp.concatenate([gram[0] * scale, identity], axis=1), micro, near)
    inverse = block[:, size:]
    side = product(inverse, gram[1] * scale)
    corner = gram[2] * scale - product(side, side, transposed)
    r[0:size, 0:size] = jnp.where(row <= col, block[:, 0:size], 0.0)
    r[0:size, size:n] = side
    for c in range(4):
        first = product(inverse, x[c, 0:size, :])
        q[c, 0:size, :] = first
        work[c] = x[c, size:n, :] - product(side, first, transposed)

    block = eliminate(jnp.concatenate([corner, identity], axis=1), micro, near)
    inverse = block[:, size:]
    store(r.at[upper, :], r_out.at[upper, :])
    for c in range(4):
        store(q.at[c, upper, :], q_out.at[c, upper, :])
    r[size:n, size:n] = jnp.where(row <= col, block[:, 0:size], 0.0)
    store(r.at[lower, :], r_out.at[lower, :])
    for c in range(4):
        q[c, size:n, :] = product(inverse, work[c])
        store(q.at[c, lower, :], q_out.at[c, lower, :])
    for copy in stores:
        copy.wait()
    vel_store.wait()


def factor(gram, x, vel, scale):
    n = x.shape[1]
    vmem = pl.BlockSpec(memory_space=pltpu.VMEM)
    hbm = pl.BlockSpec(memory_space=pltpu.HBM)
    return pl.pallas_call(
        functools.partial(factor_kernel, scale, 2 * SUB, 2),
        out_shape=(
            pltpu.HBM(x.shape, jnp.float32),
            pltpu.HBM((n, n), jnp.float32),
            pltpu.HBM(vel.shape, jnp.float32),
        ),
        in_specs=[vmem, vmem, vmem],
        out_specs=[hbm, hbm, hbm],
        scratch_shapes=[
            pltpu.VMEM(x.shape, jnp.float32),
            pltpu.VMEM((n, n), jnp.float32),
            pltpu.VMEM((4, n // 2, LANES), jnp.float32),
            pltpu.SemaphoreType.DMA((11,)),
        ],
        compiler_params=pltpu.CompilerParams(vmem_limit_bytes=32 * 2**20),
        name="factor_and_solve",
    )(*[pltpu.with_memory_space_constraint(y, pltpu.VMEM) for y in (gram, x, vel)])


def on_device(ndof, ndir, disp, veloc, elem, link, inv, offset, damper_at, damper_k, damper_c):
    nodes = disp.shape[2]
    offset = offset.reshape(nodes // LANES, LANES)
    nx = CHIPS_X if ndof % CHIPS_X == 0 else 1
    veloc, x, gram = newmark(
        ndof, nx, ndir, disp, veloc, elem, link, inv, offset, damper_at, damper_k, damper_c
    )
    q_block, r_factor, veloc = factor(gram, x, veloc, 1.0 / (4.0 * nodes * ndof))
    return veloc, q_block, r_factor


def solution(mesh):
    in_specs = (
        P(None, "dir", "dof"),
        P(None, "dir", "dof"),
        P(None, None, "dof"),
        P(None, None, "dof"),
        P(None, None, "dof"),
        P("dof"),
        P("dof"),
        P(None, None, "dof"),
        P(None, None, "dof"),
    )
    out_specs = (P(None, "dir", "dof"), P(None, None, ("dof", "dir")), P())
    return jax.shard_map(
        functools.partial(on_device, mesh.shape["dof"], mesh.shape["dir"]),
        mesh=mesh,
        in_specs=in_specs,
        out_specs=out_specs,
        check_vma=False,
    )
```

```python
import functools

import jax
import jax.numpy as jnp
from jax import lax
from jax.experimental import pallas as pl
from jax.experimental.pallas import tpu as pltpu
from jax.sharding import PartitionSpec as P

STEP = 0.5
LANES = 128
SUB = 8
REACH = 32
CHIPS_X = 4
MESH = pl.DeviceIdType.MESH
HIGHEST = lax.Precision.HIGHEST


def iota(shape, axis):
    return lax.broadcasted_iota(jnp.int32, shape, axis)


def rolled(x, by, axis):
    by = by % x.shape[axis]
    return pltpu.roll(x, by, axis) if by else x


def lane_gather(x, index):
    return jnp.take_along_axis(x, index, axis=1, mode="promise_in_bounds")


def far_first(offsets, sizes):
    def distance(offset):
        return sum(min(o, n - o) for o, n in zip(offset, sizes))

    return [o for o in sorted(offsets, key=distance, reverse=True) if distance(o)]


def newmark_kernel(
    ndof,
    nx,
    ndir,
    disp_in,
    vel_in,
    elem_in,
    link_in,
    inv_in,
    offset_in,
    damper_at_in,
    damper_k_in,
    damper_c_in,
    vel_out,
    x_all,
    gram,
    disp_a,
    disp_b,
    vel,
    coef,
    link_raw,
    inv_raw,
    offset_raw,
    pm,
    qm,
    vm,
    to_send,
    arrived,
    gram_part,
    slots,
    z_part,
    z_slots,
    z_sum,
    damper_at,
    damper_k,
    damper_c,
    load_sem,
    halo_send,
    halo_recv,
    a2a_send,
    a2a_recv,
    rs_send,
    rs_recv,
    z_send,
    z_recv,
    ag_send,
    ag_recv,
):
    me_p = lax.axis_index("dof")
    me_t = lax.axis_index("dir")
    dirs = disp_in.shape[1]
    nodes = disp_in.shape[2]
    tiles = nodes // LANES
    around = tiles + 1
    nz = ndof // nx
    me_z, me_x = me_p // nx, lax.rem(me_p, nx)
    me = me_t * nx + me_x
    share = gram.shape[1] // (nx * ndir)
    plane = far_first([(x, t) for x in range(nx) for t in range(ndir)], (nx, ndir))
    line = [by for by, in far_first([(z,) for z in range(nz)], (nz,))]

    at_x = [lax.rem(me_x + by, nx) for by in range(nx)]
    at_t = [lax.rem(me_t + by, ndir) for by in range(ndir)]
    barrier = pltpu.get_barrier_semaphore()

    def greet(p, t):
        pl.semaphore_signal(barrier, inc=1, device_id=(p, t), device_id_type=MESH)

    for by in (1, ndof - 1):
        greet(lax.rem(me_p + by, ndof), me_t)
    loads = [
        (disp_in, disp_a.at[:, :, 0:nodes]),
        (vel_in, vel.at[:, :, 0:nodes]),
        (elem_in, coef.at[0:8, :, 0:nodes]),
        (link_in, link_raw),
        (inv_in, inv_raw),
        (offset_in, offset_raw),
        (damper_at_in, damper_at),
        (damper_k_in, damper_k),
        (damper_c_in, damper_c),
    ]
    loads = [pltpu.make_async_copy(s, d, load_sem.at[i]) for i, (s, d) in enumerate(loads)]
    for copy in loads:
        copy.start()

    for by, in far_first([(t,) for t in range(ndir)], (ndir,)):
        greet(me_p, lax.rem(me_t + by, ndir))
    for by in line:
        greet(lax.rem(me_z + by, nz) * nx + me_x, me_t)
    for by in range(1, nx):
        greet(me_z * nx + lax.rem(me_x + by, nx), me_t)

    lane = iota((SUB, LANES), 1)
    sub = iota((SUB, LANES), 0)

    def at_tile(t):
        return pl.ds(pl.multiple_of(t * LANES, LANES), LANES)

    for copy in loads[2:]:
        copy.wait()
    columns = []
    for q in range(2):
        column = jnp.zeros((SUB, LANES), jnp.float32)
        for kind, table in enumerate((damper_k, damper_c)):
            for i in range(2):
                for j in range(2):
                    column = jnp.where(sub == 4 * kind + 2 * i + j, table[i, j, q], column)
        columns.append(column)
    for t in range(tiles):
        where = slice(t * LANES, (t + 1) * LANES)
        dense = jnp.zeros((SUB, LANES), jnp.float32)
        for q in range(2):
            place = damper_at[q] - me_p * nodes - t * LANES
            dense = dense + jnp.where(lane == place, columns[q], 0.0)
        coef[12, :, where] = dense
        row = offset_raw[t : t + 1, :].astype(jnp.float32)
        coef[13, :, where] = jnp.broadcast_to(row, (SUB, LANES))
    for half in range(2):
        coef[8 + half, 0:4, 0:nodes] = link_raw[2 * half]
        coef[8 + half, 4:8, 0:nodes] = link_raw[2 * half + 1]
        coef[10 + half, 0:4, 0:nodes] = inv_raw[2 * half]
        coef[10 + half, 4:8, 0:nodes] = inv_raw[2 * half + 1]
    for copy in loads[:2]:
        copy.wait()

    groups = dirs // SUB
    packs = []
    for ref in (disp_a, vel):
        for g in range(groups):
            packs.append([(ref, c, slice(g * SUB, (g + 1) * SUB)) for c in range(4)])
    for g in range(0, 14, 4):
        packs.append([(coef, k, slice(0, SUB)) for k in range(g, min(g + 4, 14))])
    for side, start, first in ((0, nodes - LANES, LANES - REACH), (1, 0, 0)):
        for n, pack in enumerate(packs):
            held = None
            for s, (ref, c, rows) in enumerate(pack):
                piece = rolled(ref[c, rows, start : start + LANES], REACH * s - first, 1)
                held = piece if held is None else jnp.where(lane >= REACH * s, piece, held)
            to_send[side, n] = held

    pl.semaphore_wait(barrier, 2 + ndir - 1 + nz - 1 + nx - 1)
    halo = []
    for side, by in ((0, 1), (1, ndof - 1)):
        halo.append(
            pltpu.make_async_remote_copy(
                src_ref=to_send.at[side],
                dst_ref=arrived.at[side],
                send_sem=halo_send.at[side],
                recv_sem=halo_recv.at[side],
                device_id=(lax.rem(me_p + by, ndof), me_t),
                device_id_type=MESH,
            )
        )
        halo[-1].start()

    def prepare(t):
        now = at_tile(t)
        before = at_tile(lax.rem(t + around - 1, around))
        p_rows, q_rows = [], []
        for i in range(4):
            shifted = jnp.where(
                lane == 0,
                rolled(coef[4 + i, :, before], 1, 1),
                rolled(coef[4 + i, :, now], 1, 1),
            )
            link = coef[8 + i // 2, :, now]
            if i % 2 == 0:
                link = rolled(link, 4, 0)
            q_rows.append(jnp.where(sub < 4, shifted, link))
            p_rows.append(coef[i, :, now] + jnp.where(sub < 4, rolled(shifted, 4, 0), 0.0))
        film = coef[12, :, now]
        for k in range(2):
            p_rows[k] = p_rows[k] + jnp.where(sub < 2, rolled(film, -2 * k, 0), 0.0)
        v_rows = [rolled(film, -4 - 2 * k, 0) for k in range(2)]
        for i in range(4):
            inv = [
                -coef[10 + i // 2, 4 * (i % 2) + k : 4 * (i % 2) + k + 1, now] for k in range(4)
            ]
            for out, rows in ((pm, p_rows), (qm, q_rows), (vm, v_rows)):
                total = inv[0] * rows[0]
                for k in range(1, len(rows)):
                    total = total + inv[k] * rows[k]
                out[i, :, now] = total

    chunk = min(16, dirs)

    def evaluate(disp, t, finish):
        now = at_tile(t)
        before = at_tile(lax.rem(t + around - 1, around))
        after = at_tile(lax.rem(t + 1, around))
        wide_lane = iota((chunk, LANES), 1)
        target = coef[13, 0:1, now].astype(jnp.int32) + lane[0:1, :]
        inside = jnp.broadcast_to((target >= 0) & (target < LANES), (chunk, LANES))
        index = jnp.broadcast_to(target & (LANES - 1), (chunk, LANES))
        for r in range(0, dirs, chunk):
            rows = slice(r, r + chunk)
            speed = [vel[j, rows, now] for j in range(2)]
            acc = [None] * 4
            for j in range(4):
                here = disp[j, rows, now]
                left = disp[j, rows, before]
                right = disp[j, rows, after]
                previous = jnp.where(wide_lane == 0, rolled(left, 1, 1), rolled(here, 1, 1))
                following = jnp.where(
                    wide_lane == LANES - 1, rolled(right, -1, 1), rolled(here, -1, 1)
                )
                other = jnp.where(wide_lane < LANES // 2, right, left)
                linked = jnp.where(inside, lane_gather(here, index), lane_gather(other, index))
                for i in range(4):
                    total = pm[i, j : j + 1, now] * here
                    total = total + pm[i, 4 + j : 5 + j, now] * following
                    total = total + qm[i, j : j + 1, now] * previous
                    total = total + qm[i, 4 + j : 5 + j, now] * linked
                    if j < 2:
                        total = total + vm[i, j : j + 1, now] * speed[j]
                    acc[i] = total if acc[i] is None else acc[i] + total
            finish(rows, now, acc)

    def finish_first(rows, now, acc):
        for i in range(4):
            v = vel[i, rows, now]
            disp_b[i, rows, now] = (
                disp_a[i, rows, now] + STEP * v + (0.5 * STEP * STEP) * acc[i]
            )
            vel[i, rows, now] = v + (0.5 * STEP) * acc[i]

    def finish_second(rows, now, acc):
        for i in range(4):
            v = vel[i, rows, now] + (0.5 * STEP) * acc[i]
            disp_a[i, rows, now] = (
                disp_b[i, rows, now] + STEP * v + (0.5 * STEP * STEP) * acc[i]
            )
            vel[i, rows, now] = v + (0.5 * STEP) * acc[i]

    def finish_last(rows, now, acc):
        for i in range(4):
            vel_out[i, rows, now] = vel[i, rows, now] + (0.5 * STEP) * acc[i]

    def prepare_tile(t, carry):
        prepare(t)
        return carry

    def first_tile(t, carry):
        evaluate(disp_a, t, finish_first)
        return carry

    own_rows = pl.ds(pl.multiple_of(me_t * dirs, dirs), dirs)

    def tile_copy(peer, half):
        part = pl.ds(2 * half, 2)
        return pltpu.make_async_remote_copy(
            src_ref=disp_a.at[part, :, at_tile(peer)],
            dst_ref=x_all.at[part, own_rows, :],
            send_sem=a2a_send,
            recv_sem=a2a_recv.at[half],
            device_id=(me_p, peer),
            device_id_type=MESH,
        )

    def send_tile(t, halves):
        @pl.when(t != me_t)
        def _():
            for half in halves:
                tile_copy(t, half).start()

    def second_tile(t, carry):
        evaluate(disp_b, t, finish_second)
        return carry

    def second_and_send(t, carry):
        evaluate(disp_b, t, finish_second)
        send_tile(t, (0, 1))
        return carry

    lax.fori_loop(1, tiles, prepare_tile, 0)
    lax.fori_loop(1, tiles - 1, first_tile, 0)
    lax.fori_loop(2, tiles - 2, second_and_send, 0)

    for copy in halo:
        copy.wait_recv()
    right_end = jnp.where(me_p < ndof - 1, REACH, 0)
    left_start = jnp.where(me_p > 0, LANES - REACH, LANES)
    for n, pack in enumerate(packs):
        from_left, from_right = arrived[0, n], arrived[1, n]
        for s, (ref, c, rows) in enumerate(pack):
            piece = jnp.where(lane < right_end, rolled(from_right, -REACH * s, 1), 0.0)
            ref[c, rows, nodes : nodes + LANES] = jnp.where(
                lane >= left_start, rolled(from_left, LANES - REACH - REACH * s, 1), piece
            )

    def wrapped(k):
        return lax.rem(k, around)

    lax.fori_loop(tiles, tiles + 2, lambda k, c: prepare_tile(wrapped(k), c), 0)

    def inner_end(k, carry):
        evaluate(disp_a, lax.rem(tiles - 1 + k, tiles), finish_first)
        return second_and_send(lax.rem(tiles - 2 + 3 * k, tiles), carry)

    def outer_end(k, carry):
        t = lax.rem(tiles - 1 + k, tiles)
        evaluate(disp_b, t, finish_second)
        send_tile(t, (0,))
        return carry

    def send_rest(k, carry):
        send_tile(lax.rem(tiles - 1 + k, tiles), (1,))
        return carry

    lax.fori_loop(0, 2, inner_end, 0)
    lax.fori_loop(tiles, tiles + 1, first_tile, 0)
    lax.fori_loop(0, 2, outer_end, 0)
    lax.fori_loop(0, 2, send_rest, 0)
    x_all[:, own_rows, :] = disp_a[:, :, at_tile(me_t)]

    def last_tile(t, carry):
        evaluate(disp_a, t, finish_last)
        return carry

    total = None
    for half in range(2):
        arrivals = x_all.at[pl.ds(2 * half, 2), pl.ds(0, (ndir - 1) * dirs), :]
        pltpu.make_async_copy(arrivals, arrivals, a2a_recv.at[half]).wait()
        pair = jnp.concatenate([x_all[2 * half], x_all[2 * half + 1]], axis=1)
        product = lax.dot_general(
            pair,
            pair,
            (((1,), (1,)), ((), ())),
            precision=HIGHEST,
            preferred_element_type=jnp.float32,
        )
        total = product if total is None else total + product
    half_n = gram.shape[1]
    gram_part[0] = total[0:half_n, 0:half_n]
    gram_part[1] = total[0:half_n, half_n:]
    gram_part[2] = total[half_n:, half_n:]

    def part_copy(by):
        to = at_x[by[0]], at_t[by[1]]
        member = to[1] * nx + to[0]
        return pltpu.make_async_remote_copy(
            src_ref=gram_part.at[:, pl.ds(member * share, share), :],
            dst_ref=slots.at[:, pl.ds(me * share, share), :],
            send_sem=rs_send,
            recv_sem=rs_recv,
            device_id=(me_z * nx + to[0], to[1]),
            device_id_type=MESH,
        )

    for by in plane:
        part_copy(by).start()
    mine = pl.ds(me * share, share)
    own = pltpu.make_async_copy(gram_part.at[:, mine, :], slots.at[:, mine, :], rs_recv)
    own.start()
    evaluate(disp_b, tiles, finish_second)
    lax.fori_loop(0, tiles, last_tile, 0)
    pltpu.make_async_copy(slots, slots, rs_recv).wait()
    total = slots[:, 0:SUB, :]
    for k in range(SUB, slots.shape[1], SUB):
        total = total + slots[:, k : k + SUB, :]
    for b in range(3):
        piece = total[b]
        for k in range(share, SUB, share):
            piece = piece + rolled(total[b], -k, 0)
        z_part[b] = piece

    def z_copy(by):
        return pltpu.make_async_remote_copy(
            src_ref=z_part.at[:, 0:share, :],
            dst_ref=z_slots.at[me_z, :, 0:share, :],
            send_sem=z_send,
            recv_sem=z_recv,
            device_id=(lax.rem(me_z + by, nz) * nx + me_x, me_t),
            device_id_type=MESH,
        )

    for by in line:
        z_copy(by).start()
    own = pltpu.make_async_copy(
        z_part.at[:, 0:share, :], z_slots.at[me_z, :, 0:share, :], z_recv
    )
    own.start()
    arrivals = z_slots.at[:, :, 0:share, :]
    pltpu.make_async_copy(arrivals, arrivals, z_recv).wait()
    total = z_slots[0, :, 0:share, :]
    for k in range(1, nz):
        total = total + z_slots[k, :, 0:share, :]
    z_sum[:, 0:share, :] = total

    def sum_copy(by):
        to = at_x[by[0]], at_t[by[1]]
        return pltpu.make_async_remote_copy(
            src_ref=z_sum.at[:, 0:share, :],
            dst_ref=gram.at[:, mine, :],
            send_sem=ag_send,
            recv_sem=ag_recv,
            device_id=(me_z * nx + to[0], to[1]),
            device_id_type=MESH,
        )

    for by in plane:
        sum_copy(by).start()
    own = pltpu.make_async_copy(z_sum.at[:, 0:share, :], gram.at[:, mine, :], ag_recv)
    own.start()
    pltpu.make_async_copy(gram, gram, ag_recv).wait()

    for copy in halo:
        copy.wait_send()
    for sent, sem in (
        (x_all.at[:, 0 : (ndir - 1) * dirs, :], a2a_send),
        (gram_part.at[:, 0 : len(plane) * share, :], rs_send),
        (z_slots.at[0 : len(line), :, 0:share, :], z_send),
        (gram_part.at[:, 0 : len(plane) * share, :], ag_send),
    ):
        pltpu.make_async_copy(sent, sent, sem).wait()


def newmark(ndof, nx, ndir, *args):
    dirs, nodes = args[0].shape[1:]
    around = nodes + LANES
    n = dirs * ndir
    packs = 2 * (dirs // SUB) + 4
    f32 = jnp.float32
    hbm = pl.BlockSpec(memory_space=pltpu.HBM)
    vmem = pl.BlockSpec(memory_space=pltpu.VMEM)
    dma = pltpu.SemaphoreType.DMA
    return pl.pallas_call(
        functools.partial(newmark_kernel, ndof, nx, ndir),
        out_shape=(
            pltpu.VMEM((4, dirs, nodes), f32),
            pltpu.VMEM((4, n, LANES), f32),
            pltpu.VMEM((3, n // 2, n // 2), f32),
        ),
        in_specs=[hbm] * 9,
        out_specs=[vmem] * 3,
        scratch_shapes=[
            pltpu.VMEM((4, dirs, around), f32),
            pltpu.VMEM((4, dirs, around), f32),
            pltpu.VMEM((4, dirs, around), f32),
            pltpu.VMEM((14, SUB, around), f32),
            pltpu.VMEM((4, 4, nodes), f32),
            pltpu.VMEM((4, 4, nodes), f32),
            pltpu.VMEM((nodes // LANES, LANES), jnp.int32),
            pltpu.VMEM((4, SUB, around), f32),
            pltpu.VMEM((4, SUB, around), f32),
            pltpu.VMEM((4, SUB, around), f32),
            pltpu.VMEM((2, packs, SUB, LANES), f32),
            pltpu.VMEM((2, packs, SUB, LANES), f32),
            pltpu.VMEM((3, n // 2, n // 2), f32),
            pltpu.VMEM((3, n // 2, n // 2), f32),
            pltpu.VMEM((3, SUB, n // 2), f32),
            pltpu.VMEM((ndof // nx, 3, SUB, n // 2), f32),
            pltpu.VMEM((3, SUB, n // 2), f32),
            pltpu.SMEM(args[6].shape, jnp.int32),
            pltpu.SMEM(args[7].shape, f32),
            pltpu.SMEM(args[8].shape, f32),
            dma((9,)),
            dma((2,)),
            dma((2,)),
            dma(()),
            dma((2,)),
            dma(()),
            dma(()),
            dma(()),
            dma(()),
            dma(()),
            dma(()),
        ],
        compiler_params=pltpu.CompilerParams(
            collective_id=0, has_side_effects=True, vmem_limit_bytes=32 * 2**20
        ),
        name="newmark_and_gram",
    )(*[pltpu.with_memory_space_constraint(x, pltpu.HBM) for x in args])


def spread(x, lane):
    return jnp.broadcast_to(x[:, lane : lane + 1], (x.shape[0], LANES))


def tiled(x, width):
    return x if width == LANES else jnp.concatenate([x] * (width // LANES), axis=1)


def eliminate(block, micro, near):
    size, width = block.shape
    sub = iota((SUB, LANES), 0)
    groups = micro // SUB
    rows = [block[i : i + SUB] for i in range(0, size, SUB)]
    done = []
    for s in range(0, size, micro):
        top = rows[:groups]
        rest = rows[groups:]
        column = [
            [spread(top[g], s + j) if g >= j // SUB else None for g in range(groups)]
            for j in range(micro)
        ]

        def entry(j, m):
            return column[j][m // SUB][m % SUB : m % SUB + 1]

        inverse = []
        pivots = [None] * groups
        for j in range(micro):
            group, at = j // SUB, j % SUB
            pivot = entry(j, j)
            inverse.append(1.0 / pivot)
            held = jnp.broadcast_to(pivot, (SUB, LANES))
            pivots[group] = held if at == 0 else jnp.where(sub == at, held, pivots[group])
            source = top[group][at : at + 1]
            for g in range(group, groups):
                if g == group and at == SUB - 1:
                    continue
                factor = column[j][g] * inverse[j]
                if g == group:
                    factor = jnp.where(sub > at, factor, 0.0)
                for m in range(j + 1, min(micro, (g + 1) * SUB)):
                    column[m][g] = column[m][g] - factor * entry(j, m)
                top[g] = top[g] - tiled(factor, width) * source
        rows = []
        for part in rest[:near]:
            own = [spread(part, s + j) for j in range(micro)]
            for j in range(micro):
                factor = own[j] * inverse[j]
                for m in range(j + 1, micro):
                    own[m] = own[m] - factor * entry(j, m)
                part = part - tiled(factor, width) * top[j // SUB][j % SUB : j % SUB + 1]
            rows.append(part)
        top = jnp.concatenate(
            [t * tiled(lax.rsqrt(p), width) for t, p in zip(top, pivots)], axis=0
        )
        if len(rest) > near:
            update = lax.dot_general(
                top[:, 0:size],
                top,
                (((0,), (0,)), ((), ())),
                precision=HIGHEST,
                preferred_element_type=jnp.float32,
            )
            for i in range(near, len(rest)):
                start = s + micro + SUB * i
                rows.append(rest[i] - update[start : start + SUB])
        done.append(top)
    return jnp.concatenate(done, axis=0)


def factor_kernel(
    scale, micro, near, gram, x, vel, q_out, r_out, vel_out, q, r, work, sems
):
    size = gram.shape[1]
    n = 2 * size
    vel_store = pltpu.make_async_copy(vel, vel_out, sems.at[0])
    vel_store.start()
    stores = []

    def store(source, target):
        copy = pltpu.make_async_copy(source, target, sems.at[1 + len(stores)])
        copy.start()
        stores.append(copy)

    def product(left, right, dims=(((1,), (0,)), ((), ()))):
        return lax.dot_general(
            left, right, dims, precision=HIGHEST, preferred_element_type=jnp.float32
        )

    transposed = (((0,), (0,)), ((), ()))
    row, col = iota((size, size), 0), iota((size, size), 1)
    identity = (row == col).astype(jnp.float32)
    upper, lower = pl.ds(0, size), pl.ds(size, size)
    r[size:, 0:size] = jnp.zeros((size, size), jnp.float32)

    block = eliminate(jnp.concatenate([gram[0] * scale, identity], axis=1), micro, near)
    inverse = block[:, size:]
    side = product(inverse, gram[1] * scale)
    corner = gram[2] * scale - product(side, side, transposed)
    r[0:size, 0:size] = jnp.where(row <= col, block[:, 0:size], 0.0)
    r[0:size, size:n] = side
    for c in range(4):
        first = product(inverse, x[c, 0:size, :])
        q[c, 0:size, :] = first
        work[c] = x[c, size:n, :] - product(side, first, transposed)

    block = eliminate(jnp.concatenate([corner, identity], axis=1), micro, near)
    inverse = block[:, size:]
    store(r.at[upper, :], r_out.at[upper, :])
    for c in range(4):
        store(q.at[c, upper, :], q_out.at[c, upper, :])
    r[size:n, size:n] = jnp.where(row <= col, block[:, 0:size], 0.0)
    store(r.at[lower, :], r_out.at[lower, :])
    for c in range(4):
        q[c, size:n, :] = product(inverse, work[c])
        store(q.at[c, lower, :], q_out.at[c, lower, :])
    for copy in stores:
        copy.wait()
    vel_store.wait()


def factor(gram, x, vel, scale):
    n = x.shape[1]
    vmem = pl.BlockSpec(memory_space=pltpu.VMEM)
    hbm = pl.BlockSpec(memory_space=pltpu.HBM)
    return pl.pallas_call(
        functools.partial(factor_kernel, scale, 2 * SUB, 2),
        out_shape=(
            pltpu.HBM(x.shape, jnp.float32),
            pltpu.HBM((n, n), jnp.float32),
            pltpu.HBM(vel.shape, jnp.float32),
        ),
        in_specs=[vmem, vmem, vmem],
        out_specs=[hbm, hbm, hbm],
        scratch_shapes=[
            pltpu.VMEM(x.shape, jnp.float32),
            pltpu.VMEM((n, n), jnp.float32),
            pltpu.VMEM((4, n // 2, LANES), jnp.float32),
            pltpu.SemaphoreType.DMA((11,)),
        ],
        compiler_params=pltpu.CompilerParams(vmem_limit_bytes=32 * 2**20),
        name="factor_and_solve",
    )(*[pltpu.with_memory_space_constraint(y, pltpu.VMEM) for y in (gram, x, vel)])


def on_device(ndof, ndir, disp, veloc, elem, link, inv, offset, damper_at, damper_k, damper_c):
    nodes = disp.shape[2]
    offset = offset.reshape(nodes // LANES, LANES)
    nx = CHIPS_X if ndof % CHIPS_X == 0 else 1
    veloc, x, gram = newmark(
        ndof, nx, ndir, disp, veloc, elem, link, inv, offset, damper_at, damper_k, damper_c
    )
    q_block, r_factor, veloc = factor(gram, x, veloc, 1.0 / (4.0 * nodes * ndof))
    return veloc, q_block, r_factor


def solution(mesh):
    in_specs = (
        P(None, "dir", "dof"),
        P(None, "dir", "dof"),
        P(None, None, "dof"),
        P(None, None, "dof"),
        P(None, None, "dof"),
        P("dof"),
        P("dof"),
        P(None, None, "dof"),
        P(None, None, "dof"),
    )
    out_specs = (P(None, "dir", "dof"), P(None, None, ("dof", "dir")), P())
    return jax.shard_map(
        functools.partial(on_device, mesh.shape["dof"], mesh.shape["dir"]),
        mesh=mesh,
        in_specs=in_specs,
        out_specs=out_specs,
        check_vma=False,
    )
```

```python
import functools

import jax
import jax.numpy as jnp
from jax import lax
from jax.experimental import pallas as pl
from jax.experimental.pallas import tpu as pltpu
from jax.sharding import PartitionSpec as P

STEP = 0.5
LANES = 128
SUB = 8
REACH = 32
CHIPS_X = 4
MESH = pl.DeviceIdType.MESH
HIGHEST = lax.Precision.HIGHEST


def iota(shape, axis):
    return lax.broadcasted_iota(jnp.int32, shape, axis)


def rolled(x, by, axis):
    by = by % x.shape[axis]
    return pltpu.roll(x, by, axis) if by else x


def lane_gather(x, index):
    return jnp.take_along_axis(x, index, axis=1, mode="promise_in_bounds")


def far_first(offsets, sizes):
    def distance(offset):
        return sum(min(o, n - o) for o, n in zip(offset, sizes))

    return [o for o in sorted(offsets, key=distance, reverse=True) if distance(o)]


def newmark_kernel(
    ndof,
    nx,
    ndir,
    disp_in,
    vel_in,
    elem_in,
    link_in,
    inv_in,
    offset_in,
    damper_at_in,
    damper_k_in,
    damper_c_in,
    vel_out,
    x_all,
    gram,
    disp_a,
    disp_b,
    vel,
    coef,
    link_raw,
    inv_raw,
    offset_raw,
    pm,
    qm,
    vm,
    to_send,
    arrived,
    gram_part,
    slots,
    z_part,
    z_slots,
    z_sum,
    damper_at,
    damper_k,
    damper_c,
    load_sem,
    halo_send,
    halo_recv,
    a2a_send,
    a2a_recv,
    rs_send,
    rs_recv,
    z_send,
    z_recv,
    ag_send,
    ag_recv,
):
    me_p = lax.axis_index("dof")
    me_t = lax.axis_index("dir")
    dirs = disp_in.shape[1]
    nodes = disp_in.shape[2]
    tiles = nodes // LANES
    around = tiles + 1
    nz = ndof // nx
    me_z, me_x = me_p // nx, lax.rem(me_p, nx)
    me = me_t * nx + me_x
    share = gram.shape[1] // (nx * ndir)
    plane = far_first([(x, t) for x in range(nx) for t in range(ndir)], (nx, ndir))
    line = [by for by, in far_first([(z,) for z in range(nz)], (nz,))]

    at_x = [lax.rem(me_x + by, nx) for by in range(nx)]
    at_t = [lax.rem(me_t + by, ndir) for by in range(ndir)]
    barrier = pltpu.get_barrier_semaphore()

    def greet(p, t):
        pl.semaphore_signal(barrier, inc=1, device_id=(p, t), device_id_type=MESH)

    for by in (1, ndof - 1):
        greet(lax.rem(me_p + by, ndof), me_t)
    loads = [
        (disp_in, disp_a.at[:, :, 0:nodes]),
        (vel_in, vel.at[:, :, 0:nodes]),
        (elem_in, coef.at[0:8, :, 0:nodes]),
        (link_in, link_raw),
        (inv_in, inv_raw),
        (offset_in, offset_raw),
        (damper_at_in, damper_at),
        (damper_k_in, damper_k),
        (damper_c_in, damper_c),
    ]
    loads = [pltpu.make_async_copy(s, d, load_sem.at[i]) for i, (s, d) in enumerate(loads)]
    for copy in loads:
        copy.start()

    for by, in far_first([(t,) for t in range(ndir)], (ndir,)):
        greet(me_p, lax.rem(me_t + by, ndir))
    for by in line:
        greet(lax.rem(me_z + by, nz) * nx + me_x, me_t)
    for by in range(1, nx):
        greet(me_z * nx + lax.rem(me_x + by, nx), me_t)

    lane = iota((SUB, LANES), 1)
    sub = iota((SUB, LANES), 0)

    def at_tile(t):
        return pl.ds(pl.multiple_of(t * LANES, LANES), LANES)

    for copy in loads[2:]:
        copy.wait()
    columns = []
    for q in range(2):
        column = jnp.zeros((SUB, LANES), jnp.float32)
        for kind, table in enumerate((damper_k, damper_c)):
            for i in range(2):
                for j in range(2):
                    column = jnp.where(sub == 4 * kind + 2 * i + j, table[i, j, q], column)
        columns.append(column)
    for t in range(tiles):
        where = slice(t * LANES, (t + 1) * LANES)
        dense = jnp.zeros((SUB, LANES), jnp.float32)
        for q in range(2):
            place = damper_at[q] - me_p * nodes - t * LANES
            dense = dense + jnp.where(lane == place, columns[q], 0.0)
        coef[12, :, where] = dense
        row = offset_raw[t : t + 1, :].astype(jnp.float32)
        coef[13, :, where] = jnp.broadcast_to(row, (SUB, LANES))
    for half in range(2):
        coef[8 + half, 0:4, 0:nodes] = link_raw[2 * half]
        coef[8 + half, 4:8, 0:nodes] = link_raw[2 * half + 1]
        coef[10 + half, 0:4, 0:nodes] = inv_raw[2 * half]
        coef[10 + half, 4:8, 0:nodes] = inv_raw[2 * half + 1]
    for copy in loads[:2]:
        copy.wait()

    groups = dirs // SUB
    packs = []
    for ref in (disp_a, vel):
        for g in range(groups):
            packs.append([(ref, c, slice(g * SUB, (g + 1) * SUB)) for c in range(4)])
    for g in range(0, 14, 4):
        packs.append([(coef, k, slice(0, SUB)) for k in range(g, min(g + 4, 14))])
    for side, start, first in ((0, nodes - LANES, LANES - REACH), (1, 0, 0)):
        for n, pack in enumerate(packs):
            held = None
            for s, (ref, c, rows) in enumerate(pack):
                piece = rolled(ref[c, rows, start : start + LANES], REACH * s - first, 1)
                held = piece if held is None else jnp.where(lane >= REACH * s, piece, held)
            to_send[side, n] = held

    pl.semaphore_wait(barrier, 2 + ndir - 1 + nz - 1 + nx - 1)
    halo = []
    for side, by in ((0, 1), (1, ndof - 1)):
        halo.append(
            pltpu.make_async_remote_copy(
                src_ref=to_send.at[side],
                dst_ref=arrived.at[side],
                send_sem=halo_send.at[side],
                recv_sem=halo_recv.at[side],
                device_id=(lax.rem(me_p + by, ndof), me_t),
                device_id_type=MESH,
            )
        )
        halo[-1].start()

    def prepare(t):
        now = at_tile(t)
        before = at_tile(lax.rem(t + around - 1, around))
        p_rows, q_rows = [], []
        for i in range(4):
            shifted = jnp.where(
                lane == 0,
                rolled(coef[4 + i, :, before], 1, 1),
                rolled(coef[4 + i, :, now], 1, 1),
            )
            link = coef[8 + i // 2, :, now]
            if i % 2 == 0:
                link = rolled(link, 4, 0)
            q_rows.append(jnp.where(sub < 4, shifted, link))
            p_rows.append(coef[i, :, now] + jnp.where(sub < 4, rolled(shifted, 4, 0), 0.0))
        film = coef[12, :, now]
        for k in range(2):
            p_rows[k] = p_rows[k] + jnp.where(sub < 2, rolled(film, -2 * k, 0), 0.0)
        v_rows = [rolled(film, -4 - 2 * k, 0) for k in range(2)]
        for i in range(4):
            inv = [
                -coef[10 + i // 2, 4 * (i % 2) + k : 4 * (i % 2) + k + 1, now] for k in range(4)
            ]
            for out, rows in ((pm, p_rows), (qm, q_rows), (vm, v_rows)):
                total = inv[0] * rows[0]
                for k in range(1, len(rows)):
                    total = total + inv[k] * rows[k]
                out[i, :, now] = total

    chunk = min(16, dirs)

    def evaluate(disp, t, finish):
        now = at_tile(t)
        before = at_tile(lax.rem(t + around - 1, around))
        after = at_tile(lax.rem(t + 1, around))
        wide_lane = iota((chunk, LANES), 1)
        target = coef[13, 0:1, now].astype(jnp.int32) + lane[0:1, :]
        inside = jnp.broadcast_to((target >= 0) & (target < LANES), (chunk, LANES))
        index = jnp.broadcast_to(target & (LANES - 1), (chunk, LANES))
        for r in range(0, dirs, chunk):
            rows = slice(r, r + chunk)
            speed = [vel[j, rows, now] for j in range(2)]
            acc = [None] * 4
            for j in range(4):
                here = disp[j, rows, now]
                left = disp[j, rows, before]
                right = disp[j, rows, after]
                previous = jnp.where(wide_lane == 0, rolled(left, 1, 1), rolled(here, 1, 1))
                following = jnp.where(
                    wide_lane == LANES - 1, rolled(right, -1, 1), rolled(here, -1, 1)
                )
                other = jnp.where(wide_lane < LANES // 2, right, left)
                linked = jnp.where(inside, lane_gather(here, index), lane_gather(other, index))
                for i in range(4):
                    total = pm[i, j : j + 1, now] * here
                    total = total + pm[i, 4 + j : 5 + j, now] * following
                    total = total + qm[i, j : j + 1, now] * previous
                    total = total + qm[i, 4 + j : 5 + j, now] * linked
                    if j < 2:
                        total = total + vm[i, j : j + 1, now] * speed[j]
                    acc[i] = total if acc[i] is None else acc[i] + total
            finish(rows, now, acc)

    def finish_first(rows, now, acc):
        for i in range(4):
            v = vel[i, rows, now]
            disp_b[i, rows, now] = (
                disp_a[i, rows, now] + STEP * v + (0.5 * STEP * STEP) * acc[i]
            )
            vel[i, rows, now] = v + (0.5 * STEP) * acc[i]

    def finish_second(rows, now, acc):
        for i in range(4):
            v = vel[i, rows, now] + (0.5 * STEP) * acc[i]
            disp_a[i, rows, now] = (
                disp_b[i, rows, now] + STEP * v + (0.5 * STEP * STEP) * acc[i]
            )
            vel[i, rows, now] = v + (0.5 * STEP) * acc[i]

    def finish_last(rows, now, acc):
        for i in range(4):
            vel_out[i, rows, now] = vel[i, rows, now] + (0.5 * STEP) * acc[i]

    def prepare_tile(t, carry):
        prepare(t)
        return carry

    def first_tile(t, carry):
        evaluate(disp_a, t, finish_first)
        return carry

    own_rows = pl.ds(pl.multiple_of(me_t * dirs, dirs), dirs)

    def tile_copy(peer, half):
        part = pl.ds(2 * half, 2)
        return pltpu.make_async_remote_copy(
            src_ref=disp_a.at[part, :, at_tile(peer)],
            dst_ref=x_all.at[part, own_rows, :],
            send_sem=a2a_send,
            recv_sem=a2a_recv.at[half],
            device_id=(me_p, peer),
            device_id_type=MESH,
        )

    def send_tile(t, halves):
        @pl.when(t != me_t)
        def _():
            for half in halves:
                tile_copy(t, half).start()

    def second_tile(t, carry):
        evaluate(disp_b, t, finish_second)
        return carry

    def second_and_send(t, carry):
        evaluate(disp_b, t, finish_second)
        send_tile(t, (0, 1))
        return carry

    lax.fori_loop(1, tiles, prepare_tile, 0)
    lax.fori_loop(1, tiles - 1, first_tile, 0)
    lax.fori_loop(2, tiles - 2, second_and_send, 0)

    for copy in halo:
        copy.wait_recv()
    right_end = jnp.where(me_p < ndof - 1, REACH, 0)
    left_start = jnp.where(me_p > 0, LANES - REACH, LANES)
    for n, pack in enumerate(packs):
        from_left, from_right = arrived[0, n], arrived[1, n]
        for s, (ref, c, rows) in enumerate(pack):
            piece = jnp.where(lane < right_end, rolled(from_right, -REACH * s, 1), 0.0)
            ref[c, rows, nodes : nodes + LANES] = jnp.where(
                lane >= left_start, rolled(from_left, LANES - REACH - REACH * s, 1), piece
            )

    def wrapped(k):
        return lax.rem(k, around)

    lax.fori_loop(tiles, tiles + 2, lambda k, c: prepare_tile(wrapped(k), c), 0)

    def inner_end(k, carry):
        evaluate(disp_a, lax.rem(tiles - 1 + k, tiles), finish_first)
        return second_and_send(lax.rem(tiles - 2 + 3 * k, tiles), carry)

    def outer_end(k, carry):
        t = lax.rem(tiles - 1 + k, tiles)
        evaluate(disp_b, t, finish_second)
        send_tile(t, (0, 1))
        return carry

    lax.fori_loop(0, 2, inner_end, 0)
    lax.fori_loop(tiles, tiles + 1, first_tile, 0)
    lax.fori_loop(0, 2, outer_end, 0)
    x_all[:, own_rows, :] = disp_a[:, :, at_tile(me_t)]
    evaluate(disp_b, tiles, finish_second)

    def last_tile(t, carry):
        evaluate(disp_a, t, finish_last)
        return carry

    lax.fori_loop(0, tiles, last_tile, 0)

    total = None
    for half in range(2):
        arrivals = x_all.at[pl.ds(2 * half, 2), pl.ds(0, (ndir - 1) * dirs), :]
        pltpu.make_async_copy(arrivals, arrivals, a2a_recv.at[half]).wait()
        pair = jnp.concatenate([x_all[2 * half], x_all[2 * half + 1]], axis=1)
        product = lax.dot_general(
            pair,
            pair,
            (((1,), (1,)), ((), ())),
            precision=HIGHEST,
            preferred_element_type=jnp.float32,
        )
        total = product if total is None else total + product
    half_n = gram.shape[1]
    gram_part[0] = total[0:half_n, 0:half_n]
    gram_part[1] = total[0:half_n, half_n:]
    gram_part[2] = total[half_n:, half_n:]

    def part_copy(by):
        to = at_x[by[0]], at_t[by[1]]
        member = to[1] * nx + to[0]
        return pltpu.make_async_remote_copy(
            src_ref=gram_part.at[:, pl.ds(member * share, share), :],
            dst_ref=slots.at[:, pl.ds(me * share, share), :],
            send_sem=rs_send,
            recv_sem=rs_recv,
            device_id=(me_z * nx + to[0], to[1]),
            device_id_type=MESH,
        )

    for by in plane:
        part_copy(by).start()
    mine = pl.ds(me * share, share)
    own = pltpu.make_async_copy(gram_part.at[:, mine, :], slots.at[:, mine, :], rs_recv)
    own.start()
    pltpu.make_async_copy(slots, slots, rs_recv).wait()
    total = slots[:, 0:SUB, :]
    for k in range(SUB, slots.shape[1], SUB):
        total = total + slots[:, k : k + SUB, :]
    for b in range(3):
        piece = total[b]
        for k in range(share, SUB, share):
            piece = piece + rolled(total[b], -k, 0)
        z_part[b] = piece

    def z_copy(by):
        return pltpu.make_async_remote_copy(
            src_ref=z_part.at[:, 0:share, :],
            dst_ref=z_slots.at[me_z, :, 0:share, :],
            send_sem=z_send,
            recv_sem=z_recv,
            device_id=(lax.rem(me_z + by, nz) * nx + me_x, me_t),
            device_id_type=MESH,
        )

    for by in line:
        z_copy(by).start()
    own = pltpu.make_async_copy(
        z_part.at[:, 0:share, :], z_slots.at[me_z, :, 0:share, :], z_recv
    )
    own.start()
    arrivals = z_slots.at[:, :, 0:share, :]
    pltpu.make_async_copy(arrivals, arrivals, z_recv).wait()
    total = z_slots[0, :, 0:share, :]
    for k in range(1, nz):
        total = total + z_slots[k, :, 0:share, :]
    z_sum[:, 0:share, :] = total

    def sum_copy(by):
        to = at_x[by[0]], at_t[by[1]]
        return pltpu.make_async_remote_copy(
            src_ref=z_sum.at[:, 0:share, :],
            dst_ref=gram.at[:, mine, :],
            send_sem=ag_send,
            recv_sem=ag_recv,
            device_id=(me_z * nx + to[0], to[1]),
            device_id_type=MESH,
        )

    for by in plane:
        sum_copy(by).start()
    own = pltpu.make_async_copy(z_sum.at[:, 0:share, :], gram.at[:, mine, :], ag_recv)
    own.start()
    pltpu.make_async_copy(gram, gram, ag_recv).wait()

    for copy in halo:
        copy.wait_send()
    for sent, sem in (
        (x_all.at[:, 0 : (ndir - 1) * dirs, :], a2a_send),
        (gram_part.at[:, 0 : len(plane) * share, :], rs_send),
        (z_slots.at[0 : len(line), :, 0:share, :], z_send),
        (gram_part.at[:, 0 : len(plane) * share, :], ag_send),
    ):
        pltpu.make_async_copy(sent, sent, sem).wait()


def newmark(ndof, nx, ndir, *args):
    dirs, nodes = args[0].shape[1:]
    around = nodes + LANES
    n = dirs * ndir
    packs = 2 * (dirs // SUB) + 4
    f32 = jnp.float32
    hbm = pl.BlockSpec(memory_space=pltpu.HBM)
    vmem = pl.BlockSpec(memory_space=pltpu.VMEM)
    dma = pltpu.SemaphoreType.DMA
    return pl.pallas_call(
        functools.partial(newmark_kernel, ndof, nx, ndir),
        out_shape=(
            pltpu.VMEM((4, dirs, nodes), f32),
            pltpu.VMEM((4, n, LANES), f32),
            pltpu.VMEM((3, n // 2, n // 2), f32),
        ),
        in_specs=[hbm] * 9,
        out_specs=[vmem] * 3,
        scratch_shapes=[
            pltpu.VMEM((4, dirs, around), f32),
            pltpu.VMEM((4, dirs, around), f32),
            pltpu.VMEM((4, dirs, around), f32),
            pltpu.VMEM((14, SUB, around), f32),
            pltpu.VMEM((4, 4, nodes), f32),
            pltpu.VMEM((4, 4, nodes), f32),
            pltpu.VMEM((nodes // LANES, LANES), jnp.int32),
            pltpu.VMEM((4, SUB, around), f32),
            pltpu.VMEM((4, SUB, around), f32),
            pltpu.VMEM((4, SUB, around), f32),
            pltpu.VMEM((2, packs, SUB, LANES), f32),
            pltpu.VMEM((2, packs, SUB, LANES), f32),
            pltpu.VMEM((3, n // 2, n // 2), f32),
            pltpu.VMEM((3, n // 2, n // 2), f32),
            pltpu.VMEM((3, SUB, n // 2), f32),
            pltpu.VMEM((ndof // nx, 3, SUB, n // 2), f32),
            pltpu.VMEM((3, SUB, n // 2), f32),
            pltpu.SMEM(args[6].shape, jnp.int32),
            pltpu.SMEM(args[7].shape, f32),
            pltpu.SMEM(args[8].shape, f32),
            dma((9,)),
            dma((2,)),
            dma((2,)),
            dma(()),
            dma((2,)),
            dma(()),
            dma(()),
            dma(()),
            dma(()),
            dma(()),
            dma(()),
        ],
        compiler_params=pltpu.CompilerParams(
            collective_id=0, has_side_effects=True, vmem_limit_bytes=32 * 2**20
        ),
        name="newmark_and_gram",
    )(*[pltpu.with_memory_space_constraint(x, pltpu.HBM) for x in args])


def spread(x, lane):
    return jnp.broadcast_to(x[:, lane : lane + 1], (x.shape[0], LANES))


def tiled(x, width):
    return x if width == LANES else jnp.concatenate([x] * (width // LANES), axis=1)


def eliminate(block, micro, near):
    size, width = block.shape
    sub = iota((SUB, LANES), 0)
    groups = micro // SUB
    rows = [block[i : i + SUB] for i in range(0, size, SUB)]
    done = []
    for s in range(0, size, micro):
        top = rows[:groups]
        rest = rows[groups:]
        column = [
            [spread(top[g], s + j) if g >= j // SUB else None for g in range(groups)]
            for j in range(micro)
        ]

        def entry(j, m):
            return column[j][m // SUB][m % SUB : m % SUB + 1]

        inverse = []
        pivots = [None] * groups
        for j in range(micro):
            group, at = j // SUB, j % SUB
            pivot = entry(j, j)
            inverse.append(1.0 / pivot)
            held = jnp.broadcast_to(pivot, (SUB, LANES))
            pivots[group] = held if at == 0 else jnp.where(sub == at, held, pivots[group])
            source = top[group][at : at + 1]
            for g in range(group, groups):
                if g == group and at == SUB - 1:
                    continue
                factor = column[j][g] * inverse[j]
                if g == group:
                    factor = jnp.where(sub > at, factor, 0.0)
                for m in range(j + 1, min(micro, (g + 1) * SUB)):
                    column[m][g] = column[m][g] - factor * entry(j, m)
                top[g] = top[g] - tiled(factor, width) * source
        rows = []
        for part in rest[:near]:
            own = [spread(part, s + j) for j in range(micro)]
            for j in range(micro):
                factor = own[j] * inverse[j]
                for m in range(j + 1, micro):
                    own[m] = own[m] - factor * entry(j, m)
                part = part - tiled(factor, width) * top[j // SUB][j % SUB : j % SUB + 1]
            rows.append(part)
        top = jnp.concatenate(
            [t * tiled(lax.rsqrt(p), width) for t, p in zip(top, pivots)], axis=0
        )
        if len(rest) > near:
            update = lax.dot_general(
                top[:, 0:size],
                top,
                (((0,), (0,)), ((), ())),
                precision=HIGHEST,
                preferred_element_type=jnp.float32,
            )
            for i in range(near, len(rest)):
                start = s + micro + SUB * i
                rows.append(rest[i] - update[start : start + SUB])
        done.append(top)
    return jnp.concatenate(done, axis=0)


def factor_kernel(
    scale, micro, near, gram, x, vel, q_out, r_out, vel_out, q, r, work, sems
):
    size = gram.shape[1]
    n = 2 * size
    vel_store = pltpu.make_async_copy(vel, vel_out, sems.at[0])
    vel_store.start()
    stores = []

    def store(source, target):
        copy = pltpu.make_async_copy(source, target, sems.at[1 + len(stores)])
        copy.start()
        stores.append(copy)

    def product(left, right, dims=(((1,), (0,)), ((), ()))):
        return lax.dot_general(
            left, right, dims, precision=HIGHEST, preferred_element_type=jnp.float32
        )

    transposed = (((0,), (0,)), ((), ()))
    row, col = iota((size, size), 0), iota((size, size), 1)
    identity = (row == col).astype(jnp.float32)
    upper, lower = pl.ds(0, size), pl.ds(size, size)
    r[size:, 0:size] = jnp.zeros((size, size), jnp.float32)

    block = eliminate(jnp.concatenate([gram[0] * scale, identity], axis=1), micro, near)
    inverse = block[:, size:]
    side = product(inverse, gram[1] * scale)
    corner = gram[2] * scale - product(side, side, transposed)
    r[0:size, 0:size] = jnp.where(row <= col, block[:, 0:size], 0.0)
    r[0:size, size:n] = side
    for c in range(4):
        first = product(inverse, x[c, 0:size, :])
        q[c, 0:size, :] = first
        work[c] = x[c, size:n, :] - product(side, first, transposed)

    block = eliminate(jnp.concatenate([corner, identity], axis=1), micro, near)
    inverse = block[:, size:]
    store(r.at[upper, :], r_out.at[upper, :])
    for c in range(4):
        store(q.at[c, upper, :], q_out.at[c, upper, :])
    r[size:n, size:n] = jnp.where(row <= col, block[:, 0:size], 0.0)
    store(r.at[lower, :], r_out.at[lower, :])
    for c in range(4):
        q[c, size:n, :] = product(inverse, work[c])
        store(q.at[c, lower, :], q_out.at[c, lower, :])
    for copy in stores:
        copy.wait()
    vel_store.wait()


def factor(gram, x, vel, scale):
    n = x.shape[1]
    vmem = pl.BlockSpec(memory_space=pltpu.VMEM)
    hbm = pl.BlockSpec(memory_space=pltpu.HBM)
    return pl.pallas_call(
        functools.partial(factor_kernel, scale, 2 * SUB, 2),
        out_shape=(
            pltpu.HBM(x.shape, jnp.float32),
            pltpu.HBM((n, n), jnp.float32),
            pltpu.HBM(vel.shape, jnp.float32),
        ),
        in_specs=[vmem, vmem, vmem],
        out_specs=[hbm, hbm, hbm],
        scratch_shapes=[
            pltpu.VMEM(x.shape, jnp.float32),
            pltpu.VMEM((n, n), jnp.float32),
            pltpu.VMEM((4, n // 2, LANES), jnp.float32),
            pltpu.SemaphoreType.DMA((11,)),
        ],
        compiler_params=pltpu.CompilerParams(vmem_limit_bytes=32 * 2**20),
        name="factor_and_solve",
    )(*[pltpu.with_memory_space_constraint(y, pltpu.VMEM) for y in (gram, x, vel)])


def on_device(ndof, ndir, disp, veloc, elem, link, inv, offset, damper_at, damper_k, damper_c):
    nodes = disp.shape[2]
    offset = offset.reshape(nodes // LANES, LANES)
    nx = CHIPS_X if ndof % CHIPS_X == 0 else 1
    veloc, x, gram = newmark(
        ndof, nx, ndir, disp, veloc, elem, link, inv, offset, damper_at, damper_k, damper_c
    )
    q_block, r_factor, veloc = factor(gram, x, veloc, 1.0 / (4.0 * nodes * ndof))
    return veloc, q_block, r_factor


def solution(mesh):
    in_specs = (
        P(None, "dir", "dof"),
        P(None, "dir", "dof"),
        P(None, None, "dof"),
        P(None, None, "dof"),
        P(None, None, "dof"),
        P("dof"),
        P("dof"),
        P(None, None, "dof"),
        P(None, None, "dof"),
    )
    out_specs = (P(None, "dir", "dof"), P(None, None, ("dof", "dir")), P())
    return jax.shard_map(
        functools.partial(on_device, mesh.shape["dof"], mesh.shape["dir"]),
        mesh=mesh,
        in_specs=in_specs,
        out_specs=out_specs,
        check_vma=False,
    )
```
